32 devices in a mesh: cell: 16 (over z, y, core), seq: 2 (over x).
Axes of the slice: x: 2, y: 2, z: 4, core: 2. Of those that a mesh axis runs over, the one named last changes fastest.
Arguments:
- tokens: bfloat16 [16, 1024, 1280], P('cell', 'seq'), may hold values from -6 to 6
- out_grad: bfloat16 [16, 1024, 1280], P('cell', 'seq'), may hold values from -6 to 6
- query_counts: int32 [16], P('cell'), may hold values from 50 to 2000
- first_gain: bfloat16 [1280], P('seq'), may hold values from 0.25 to 1.75
- first_bias: bfloat16 [1280], P('seq'), may hold values from -1 to 1
- query_weight: bfloat16 [1280, 1280], P('seq'), may hold values from -0.15625 to 0.15625
- query_bias: bfloat16 [1280], P('seq'), may hold values from -1 to 1
- key_weight: bfloat16 [1280, 1280], P('seq'), may hold values from -0.15625 to 0.15625
- value_weight: bfloat16 [1280, 1280], P('seq'), may hold values from -0.15625 to 0.15625
- value_bias: bfloat16 [1280], P('seq'), may hold values from -1 to 1
- output_weight: bfloat16 [1280, 1280], P('seq'), may hold values from -2.5 to 2.5
- output_bias: bfloat16 [1280], P('seq'), may hold values from -1 to 1
- second_gain: bfloat16 [1280], P('seq'), may hold values from 0.25 to 1.75
- second_bias: bfloat16 [1280], P('seq'), may hold values from -1 to 1
- up_weight: bfloat16 [1280, 5120], P('seq'), may hold values from -0.15625 to 0.15625
- up_bias: bfloat16 [5120], P('seq'), may hold values from -1 to 1
- down_weight: bfloat16 [5120, 1280], P('seq'), may hold values from -0.078125 to 0.078125
- down_bias: bfloat16 [1280], P('seq'), may hold values from -1 to 1
Outputs:
- result: bfloat16 [16, 1024, 1280], P('cell', 'seq')
- input_grad: bfloat16 [16, 1024, 1280], P('cell', 'seq')
- grad_first_gain: float32 [1280], P('seq')
- grad_first_bias: float32 [1280], P('seq')
- grad_query_weight: float32 [1280, 1280], P('seq')
- grad_query_bias: float32 [1280], P('seq')
- grad_key_weight: float32 [1280, 1280], P('seq')
- grad_value_weight: float32 [1280, 1280], P('seq')
- grad_value_bias: float32 [1280], P('seq')
- grad_output_weight: float32 [1280, 1280], P('seq')
- grad_output_bias: float32 [1280], P('seq')
- grad_second_gain: float32 [1280], P('seq')
- grad_second_bias: float32 [1280], P('seq')
- grad_up_weight: float32 [1280, 5120], P('seq')
- grad_up_bias: float32 [5120], P('seq')
- grad_down_weight: float32 [5120, 1280], P('seq')
- grad_down_bias: float32 [1280], P('seq')
The draws below stay inside these ranges and needn't reach their ends.
All inputs are finite; a program needn't handle non-finite values.
Results may differ from the reference program's by a relative error of at most 0.019.
Values may be sent and summed in bfloat16 or wider, within the bound.
A program may use at most 320 MiB of HBM per device.

```python
import jax
import jax.numpy as jnp
from jax import lax

HEADS = 20
HDIM = 64
D = 1280
FF = 5120
CELLS_GRP = 1
CELL_LEN = 1024
CELLS = 16
N_CELL = 16


def set_ends(values, own_key, least, top_value):
    index_at = [jax.random.randint(jax.random.fold_in(own_key, axis), (), 0, length) for axis, length in enumerate(values.shape)]
    main_axis = values.shape.index(max(values.shape))
    beside = index_at[:main_axis] + [(index_at[main_axis] + 1) % values.shape[main_axis]] + index_at[main_axis + 1:]
    return values.at[tuple(index_at)].set(least).at[tuple(beside)].set(top_value)


def shard_levels(stream_key, dims, pieces, least, high):
    factor_of, own = 1.0, jax.random.fold_in(stream_key, 6)
    for dim, blocks in pieces:
        draws = jnp.exp(jax.random.uniform(jax.random.fold_in(own, dim), (blocks,), jnp.float32, least / len(pieces), high / len(pieces)))
        factor_of = factor_of * jnp.repeat(draws, dims[dim] // blocks).reshape([-1 if axis == dim else 1 for axis in range(len(dims))])
    return factor_of


def bell_draw(rng, extent, spread, limit, shards=(), dtype=jnp.bfloat16):
    array = spread * jax.random.normal(rng, extent, jnp.float32)
    if shards:
        array = array * shard_levels(rng, extent, shards, -0.22, 0.18)
    return jnp.clip(array, -limit, limit).astype(dtype)


def setup_inputs(seed: int = 0) -> dict:
    keys = jax.random.split(jax.random.key(seed), 19)
    return {
        "tokens": bell_draw(keys[0], (CELLS, CELL_LEN, D), 1.0, 6.0, ((0, 16), (1, 2))),
        "out_grad": bell_draw(keys[1], (CELLS, CELL_LEN, D), 1.0, 6.0, ((0, 16), (1, 2))),
        "query_counts": set_ends(jax.random.randint(keys[2], (CELLS,), 50, 2001), jax.random.fold_in(keys[2], 1), 50, 2000).astype(jnp.int32),
        "first_gain": jnp.clip(1.0 + 0.15 * jax.random.normal(keys[3], (D,), jnp.float32), 0.25, 1.75).astype(jnp.bfloat16),
        "first_bias": bell_draw(keys[4], (D,), 0.2, 1.0, ((0, 2),)),
        "query_weight": bell_draw(keys[5], (D, D), D ** -0.5, 0.15625, ((0, 2),)),
        "query_bias": bell_draw(keys[6], (D,), 0.2, 1.0, ((0, 2),)),
        "key_weight": bell_draw(keys[7], (D, D), D ** -0.5, 0.15625, ((0, 2),)),
        "value_weight": bell_draw(keys[8], (D, D), D ** -0.5, 0.15625, ((0, 2),)),
        "value_bias": bell_draw(keys[9], (D,), 0.2, 1.0, ((0, 2),)),
        "output_weight": bell_draw(keys[10], (D, D), (max(1, 4 * D // CELL_LEN)) ** -0.5, 2.5, ((0, 2),)),
        "output_bias": bell_draw(keys[11], (D,), 0.2, 1.0, ((0, 2),)),
        "second_gain": jnp.clip(1.0 + 0.15 * jax.random.normal(keys[12], (D,), jnp.float32), 0.25, 1.75).astype(jnp.bfloat16),
        "second_bias": bell_draw(keys[13], (D,), 0.2, 1.0, ((0, 2),)),
        "up_weight": bell_draw(keys[14], (D, FF), D ** -0.5, 0.15625, ((0, 2),)),
        "up_bias": bell_draw(keys[15], (FF,), 0.2, 1.0, ((0, 2),)),
        "down_weight": bell_draw(keys[16], (FF, D), FF ** -0.5, 0.078125, ((0, 2),)),
        "down_bias": bell_draw(keys[17], (D,), 0.2, 1.0, ((0, 2),)),
    }


@jax.custom_vjp
def low(v):
    return lax.optimization_barrier(v.astype(jnp.bfloat16)).astype(jnp.float32)

@jax.custom_vjp
def low_back(v):
    return v

def low_keep(v):
    return (low(v), None)

def low_pass(kept, grad):
    return (grad,)

def back_keep(v):
    return (v, None)

def back_low(kept, grad):
    return (low(grad),)
low.defvjp(low_keep, low_pass)
low_back.defvjp(back_keep, back_low)

def project(left, right):
    return jnp.dot(left, right, precision=lax.Precision.HIGHEST)

def layer_norm(values, norm_gain, norm_bias):
    average = lax.optimization_barrier(jnp.mean(values, axis=-1, keepdims=True))
    centred = values - average
    variance = lax.optimization_barrier(jnp.mean(centred * centred, axis=-1, keepdims=True))
    return centred * lax.rsqrt(variance + 1e-05) * norm_gain + norm_bias

def gelu_exact(values):
    return 0.5 * values * (1.0 + lax.erf(values * 0.7071067811865476))

def attend_cell(triple):
    queries, key_rows, value_rows = triple
    scores = low_back(0.125 * jnp.einsum('qhd,khd->hqk', queries, key_rows, precision=lax.Precision.HIGHEST))
    largest = lax.optimization_barrier(jnp.max(scores, axis=-1, keepdims=True))
    exp_scores = jnp.exp(scores - largest)
    weights = low(exp_scores / lax.optimization_barrier(jnp.sum(exp_scores, axis=-1, keepdims=True)))
    return jnp.einsum('hqk,khd->qhd', weights, value_rows, precision=lax.Precision.HIGHEST)

def forward(block, params):
    first_gain, first_bias, query_weight, query_bias, key_weight, value_weight, value_bias, output_weight, output_bias, second_gain, second_bias, up_weight, up_bias, down_weight, down_bias = params
    cell_count, cell_len, model_width = block.shape
    flat_input = block.reshape(cell_count * cell_len, model_width)
    normed_one = low(layer_norm(flat_input, first_gain, first_bias))
    queries = low(low_back(project(normed_one, query_weight) + query_bias))
    key_rows = low(low_back(project(normed_one, key_weight)))
    value_rows = low(low_back(project(normed_one, value_weight) + value_bias))
    head_shape = (cell_count, cell_len, HEADS, HDIM)
    attended = lax.map(jax.checkpoint(attend_cell), (queries.reshape(head_shape), key_rows.reshape(head_shape), value_rows.reshape(head_shape)))
    mixed = low(low_back(attended.reshape(cell_count * cell_len, model_width)))
    middle = flat_input + low_back(project(mixed, output_weight) + output_bias)
    normed_two = low(layer_norm(middle, second_gain, second_bias))
    up_proj = low_back(project(normed_two, up_weight) + up_bias)
    hidden = low(gelu_exact(up_proj))
    result = middle + low_back(project(hidden, down_weight) + down_bias)
    return result.reshape(cell_count, cell_len, model_width)

def reference(tokens, out_grad, query_counts, first_gain, first_bias, query_weight, query_bias, key_weight, value_weight, value_bias, output_weight, output_bias, second_gain, second_bias, up_weight, up_bias, down_weight, down_bias):
    params = (first_gain.astype(jnp.float32), first_bias.astype(jnp.float32), query_weight.astype(jnp.float32), query_bias.astype(jnp.float32), key_weight.astype(jnp.float32), value_weight.astype(jnp.float32), value_bias.astype(jnp.float32), output_weight.astype(jnp.float32), output_bias.astype(jnp.float32), second_gain.astype(jnp.float32), second_bias.astype(jnp.float32), up_weight.astype(jnp.float32), up_bias.astype(jnp.float32), down_weight.astype(jnp.float32), down_bias.astype(jnp.float32))
    weight_cell = jnp.sqrt(query_counts.astype(jnp.float32) / 1000.0)
    group_input = tokens.astype(jnp.float32).reshape(N_CELL, CELLS_GRP, CELL_LEN, D)
    group_cotan = out_grad.astype(jnp.float32).reshape(N_CELL, CELLS_GRP, CELL_LEN, D)
    group_cotan = group_cotan * weight_cell.reshape(N_CELL, CELLS_GRP, 1, 1)

    def one_group(carry, inputs):
        block_input, block_cotan = inputs
        result, pullback = jax.vjp(forward, block_input, params)
        grad_input, grad_params = pullback(block_cotan)
        carry = jax.tree.map(jnp.add, carry, grad_params)
        return (carry, (result.astype(jnp.bfloat16), grad_input.astype(jnp.bfloat16)))
    zero_grads = jax.tree.map(jnp.zeros_like, params)
    sums, outputs = lax.scan(one_group, zero_grads, (group_input, group_cotan))
    result = outputs[0].reshape(CELLS, CELL_LEN, D)
    input_grad = outputs[1].reshape(CELLS, CELL_LEN, D)
    return (result, input_grad, sums[0], sums[1], sums[2], sums[3], sums[4], sums[5], sums[6], sums[7], sums[8], sums[9], sums[10], sums[11], sums[12], sums[13], sums[14])
```

```python
import jax
import jax.numpy as jnp
from jax import lax
from jax.experimental import pallas as pl
from jax.experimental.pallas import tpu as pltpu
from jax.sharding import PartitionSpec as P

HEADS = 20
HDIM = 64


def from_behind(value, axis, steps):
    count = lax.axis_size(axis)
    pairs = [(source, (source + steps) % count) for source in range(count)]
    return lax.ppermute(value, axis, pairs)


def for_sending(x):
    return jax.tree.map(lambda a: a.astype(jnp.bfloat16) if a.dtype == jnp.float32 else a, x)


def matmul(left, right):
    return jnp.dot(left, right, preferred_element_type=jnp.float32)


def matmul_right_t(left, right):
    return jnp.einsum("to,io->ti", left, right, preferred_element_type=jnp.float32)


def weight_grad(left, right):
    return jnp.einsum("ti,to->io", left, right, preferred_element_type=jnp.float32)


def standardize(values):
    average = jnp.mean(values, axis=-1, keepdims=True)
    centred = values - average
    inverse = lax.rsqrt(jnp.mean(centred * centred, axis=-1, keepdims=True) + 1e-05)
    return (centred * inverse, inverse)


def standardize_back(grad_normed, standard, inverse, gain_vec):
    scaled = grad_normed * gain_vec
    return inverse * (
        scaled
        - jnp.mean(scaled, axis=-1, keepdims=True)
        - standard * jnp.mean(scaled * standard, axis=-1, keepdims=True)
    )


def gelu_value(up_proj):
    return 0.5 * up_proj * (1.0 + lax.erf(up_proj * 0.7071067811865476))


def gelu_slope(up_proj):
    return (
        0.5 * (1.0 + lax.erf(up_proj * 0.7071067811865476))
        + up_proj * jnp.exp(-0.5 * up_proj * up_proj) * 0.3989422804014327
    )


def score_block(queries, key_rows):
    return (
        jnp.einsum("cqhd,ckhd->chqk", queries, key_rows, preferred_element_type=jnp.float32) * 0.125
    )


def column_sum(values):
    return jnp.sum(values.astype(jnp.float32), axis=0)


def general(
    tokens,
    out_grad,
    query_counts,
    first_gain,
    first_bias,
    query_weight,
    query_bias,
    key_weight,
    value_weight,
    value_bias,
    output_weight,
    output_bias,
    second_gain,
    second_bias,
    up_weight,
    up_bias,
    down_weight,
    down_bias,
):
    (
        first_gain,
        first_bias,
        query_weight,
        query_bias,
        key_weight,
        value_weight,
        value_bias,
        output_weight,
        output_bias,
        second_gain,
        second_bias,
        up_weight,
        up_bias,
        down_weight,
        down_bias,
    ) = (
        lax.all_gather(first_gain, "seq", axis=0, tiled=True),
        lax.all_gather(first_bias, "seq", axis=0, tiled=True),
        lax.all_gather(query_weight, "seq", axis=0, tiled=True),
        lax.all_gather(query_bias, "seq", axis=0, tiled=True),
        lax.all_gather(key_weight, "seq", axis=0, tiled=True),
        lax.all_gather(value_weight, "seq", axis=0, tiled=True),
        lax.all_gather(value_bias, "seq", axis=0, tiled=True),
        lax.all_gather(output_weight, "seq", axis=0, tiled=True),
        lax.all_gather(output_bias, "seq", axis=0, tiled=True),
        lax.all_gather(second_gain, "seq", axis=0, tiled=True),
        lax.all_gather(second_bias, "seq", axis=0, tiled=True),
        lax.all_gather(up_weight, "seq", axis=0, tiled=True),
        lax.all_gather(up_bias, "seq", axis=0, tiled=True),
        lax.all_gather(down_weight, "seq", axis=0, tiled=True),
        lax.all_gather(down_bias, "seq", axis=0, tiled=True),
    )
    f32 = jnp.float32
    bf16 = jnp.bfloat16
    gain_first = first_gain.astype(f32)
    gain_second = second_gain.astype(f32)
    cell_count, seg_len, model_width = tokens.shape
    row_count = cell_count * seg_len
    head_shape = (cell_count, seg_len, HEADS, HDIM)
    cycle_size = lax.axis_size("seq")
    flat_input = tokens.reshape(row_count, model_width).astype(f32)
    standard_one, inverse_one = standardize(flat_input)
    normed_one = (standard_one * gain_first + first_bias.astype(f32)).astype(bf16)
    query_heads = (
        (matmul(normed_one, query_weight) + query_bias.astype(f32)).astype(bf16).reshape(head_shape)
    )
    key_heads = matmul(normed_one, key_weight).astype(bf16).reshape(head_shape)
    value_heads = (
        (matmul(normed_one, value_weight) + value_bias.astype(f32)).astype(bf16).reshape(head_shape)
    )
    running_max = jnp.full((cell_count, HEADS, seg_len), -1e30, f32)
    running_sum = jnp.zeros((cell_count, HEADS, seg_len), f32)
    weighted = jnp.zeros((cell_count, HEADS, seg_len, HDIM), f32)
    travel = (key_heads, value_heads)
    for step in range(cycle_size):
        if step > 0:
            travel = from_behind((travel[0], travel[1]), "seq", 1)
        scores = score_block(query_heads, travel[0])
        new_max = jnp.maximum(running_max, jnp.max(scores, axis=-1))
        rescale = jnp.exp(running_max - new_max)
        exp_scores = jnp.exp(scores - new_max[..., None])
        running_sum = running_sum * rescale + jnp.sum(exp_scores, axis=-1)
        weighted = weighted * rescale[..., None] + jnp.einsum(
            "chqk,ckhd->chqd", exp_scores.astype(bf16), travel[1], preferred_element_type=f32
        )
        running_max = new_max
    attended = weighted / running_sum[..., None]
    log_total = running_max + jnp.log(running_sum)
    mixed = attended.transpose(0, 2, 1, 3).reshape(row_count, model_width).astype(bf16)
    middle = flat_input + matmul(mixed, output_weight) + output_bias.astype(f32)
    standard_two, inverse_two = standardize(middle)
    normed_two = (standard_two * gain_second + second_bias.astype(f32)).astype(bf16)
    up_proj = matmul(normed_two, up_weight) + up_bias.astype(f32)
    hidden = gelu_value(up_proj).astype(bf16)
    result = middle + matmul(hidden, down_weight) + down_bias.astype(f32)
    result_out = result.astype(bf16).reshape(cell_count, seg_len, model_width)
    weight_cell = jnp.sqrt(query_counts.astype(f32) / 1000.0)
    grad_result = (out_grad.astype(f32) * weight_cell[:, None, None]).reshape(
        row_count, model_width
    )
    grad_ffn_out = grad_result.astype(bf16)
    grad_down_weight = weight_grad(hidden, grad_ffn_out)
    grad_down_bias = column_sum(grad_ffn_out)
    grad_up = (matmul_right_t(grad_ffn_out, down_weight) * gelu_slope(up_proj)).astype(bf16)
    grad_up_weight = weight_grad(normed_two, grad_up)
    grad_up_bias = column_sum(grad_up)
    grad_normed_two = matmul_right_t(grad_up, up_weight)
    grad_second_gain = jnp.sum(grad_normed_two * standard_two, axis=0)
    grad_second_bias = jnp.sum(grad_normed_two, axis=0)
    grad_middle = grad_result + standardize_back(
        grad_normed_two, standard_two, inverse_two, gain_second
    )
    grad_attn_out = grad_middle.astype(bf16)
    grad_output_weight = weight_grad(mixed, grad_attn_out)
    grad_output_bias = column_sum(grad_attn_out)
    grad_mixed = matmul_right_t(grad_attn_out, output_weight).astype(bf16).reshape(head_shape)
    row_delta = jnp.sum(grad_mixed.astype(f32).transpose(0, 2, 1, 3) * attended, axis=-1)
    grad_query_acc = jnp.zeros(head_shape, f32)
    moving = (jnp.zeros(head_shape, f32), jnp.zeros(head_shape, f32))
    travel = (key_heads, value_heads)
    for step in range(cycle_size):
        if step > 0:
            travel = from_behind((travel[0], travel[1]), "seq", 1)
        block_keys, block_values = travel
        scores = score_block(query_heads, block_keys)
        prob_block = jnp.exp(scores - log_total[..., None])
        part_values = jnp.einsum(
            "chqk,cqhd->ckhd", prob_block.astype(bf16), grad_mixed, preferred_element_type=f32
        )
        grad_probs = jnp.einsum(
            "cqhd,ckhd->chqk", grad_mixed, block_values, preferred_element_type=f32
        )
        grad_scores = (prob_block * (grad_probs - row_delta[..., None])).astype(bf16)
        grad_query_acc = (
            grad_query_acc
            + jnp.einsum("chqk,ckhd->cqhd", grad_scores, block_keys, preferred_element_type=f32)
            * 0.125
        )
        part_keys = (
            jnp.einsum("chqk,cqhd->ckhd", grad_scores, query_heads, preferred_element_type=f32)
            * 0.125
        )
        moving = from_behind(
            (for_sending(moving[0] + part_keys), for_sending(moving[1] + part_values)), "seq", 1
        )
    grad_queries = grad_query_acc.astype(bf16).reshape(row_count, model_width)
    grad_keys = moving[0].astype(bf16).reshape(row_count, model_width)
    grad_values = moving[1].astype(bf16).reshape(row_count, model_width)
    grad_query_weight = weight_grad(normed_one, grad_queries)
    grad_query_bias = column_sum(grad_queries)
    grad_key_weight = weight_grad(normed_one, grad_keys)
    grad_value_weight = weight_grad(normed_one, grad_values)
    grad_value_bias = column_sum(grad_values)
    grad_normed_one = (
        matmul_right_t(grad_queries, query_weight)
        + matmul_right_t(grad_keys, key_weight)
        + matmul_right_t(grad_values, value_weight)
    )
    grad_first_gain = jnp.sum(grad_normed_one * standard_one, axis=0)
    grad_first_bias = jnp.sum(grad_normed_one, axis=0)
    grad_input = grad_middle + standardize_back(
        grad_normed_one, standard_one, inverse_one, gain_first
    )
    input_grad = grad_input.astype(bf16).reshape(cell_count, seg_len, model_width)
    shared_all = (
        lax.psum_scatter(
            grad_first_gain.astype(jnp.bfloat16), "seq", scatter_dimension=0, tiled=True
        ).astype(jnp.float32),
        lax.psum_scatter(
            grad_first_bias.astype(jnp.bfloat16), "seq", scatter_dimension=0, tiled=True
        ).astype(jnp.float32),
        lax.psum_scatter(
            grad_query_weight.astype(jnp.bfloat16), "seq", scatter_dimension=0, tiled=True
        ).astype(jnp.float32),
        lax.psum_scatter(
            grad_query_bias.astype(jnp.bfloat16), "seq", scatter_dimension=0, tiled=True
        ).astype(jnp.float32),
        lax.psum_scatter(
            grad_key_weight.astype(jnp.bfloat16), "seq", scatter_dimension=0, tiled=True
        ).astype(jnp.float32),
        lax.psum_scatter(
            grad_value_weight.astype(jnp.bfloat16), "seq", scatter_dimension=0, tiled=True
        ).astype(jnp.float32),
        lax.psum_scatter(
            grad_value_bias.astype(jnp.bfloat16), "seq", scatter_dimension=0, tiled=True
        ).astype(jnp.float32),
        lax.psum_scatter(
            grad_output_weight.astype(jnp.bfloat16), "seq", scatter_dimension=0, tiled=True
        ).astype(jnp.float32),
        lax.psum_scatter(
            grad_output_bias.astype(jnp.bfloat16), "seq", scatter_dimension=0, tiled=True
        ).astype(jnp.float32),
        lax.psum_scatter(
            grad_second_gain.astype(jnp.bfloat16), "seq", scatter_dimension=0, tiled=True
        ).astype(jnp.float32),
        lax.psum_scatter(
            grad_second_bias.astype(jnp.bfloat16), "seq", scatter_dimension=0, tiled=True
        ).astype(jnp.float32),
        lax.psum_scatter(
            grad_up_weight.astype(jnp.bfloat16), "seq", scatter_dimension=0, tiled=True
        ).astype(jnp.float32),
        lax.psum_scatter(
            grad_up_bias.astype(jnp.bfloat16), "seq", scatter_dimension=0, tiled=True
        ).astype(jnp.float32),
        lax.psum_scatter(
            grad_down_weight.astype(jnp.bfloat16), "seq", scatter_dimension=0, tiled=True
        ).astype(jnp.float32),
        lax.psum_scatter(
            grad_down_bias.astype(jnp.bfloat16), "seq", scatter_dimension=0, tiled=True
        ).astype(jnp.float32),
    )
    (
        grad_first_gain,
        grad_first_bias,
        grad_query_weight,
        grad_query_bias,
        grad_key_weight,
        grad_value_weight,
        grad_value_bias,
        grad_output_weight,
        grad_output_bias,
        grad_second_gain,
        grad_second_bias,
        grad_up_weight,
        grad_up_bias,
        grad_down_weight,
        grad_down_bias,
    ) = shared_all
    (
        grad_first_gain,
        grad_first_bias,
        grad_query_weight,
        grad_query_bias,
        grad_key_weight,
        grad_value_weight,
        grad_value_bias,
        grad_output_weight,
        grad_output_bias,
        grad_second_gain,
        grad_second_bias,
        grad_up_weight,
        grad_up_bias,
        grad_down_weight,
        grad_down_bias,
    ) = (
        lax.psum(grad_first_gain.astype(jnp.bfloat16), "cell").astype(jnp.float32),
        lax.psum(grad_first_bias.astype(jnp.bfloat16), "cell").astype(jnp.float32),
        lax.psum(grad_query_weight.astype(jnp.bfloat16), "cell").astype(jnp.float32),
        lax.psum(grad_query_bias.astype(jnp.bfloat16), "cell").astype(jnp.float32),
        lax.psum(grad_key_weight.astype(jnp.bfloat16), "cell").astype(jnp.float32),
        lax.psum(grad_value_weight.astype(jnp.bfloat16), "cell").astype(jnp.float32),
        lax.psum(grad_value_bias.astype(jnp.bfloat16), "cell").astype(jnp.float32),
        lax.psum(grad_output_weight.astype(jnp.bfloat16), "cell").astype(jnp.float32),
        lax.psum(grad_output_bias.astype(jnp.bfloat16), "cell").astype(jnp.float32),
        lax.psum(grad_second_gain.astype(jnp.bfloat16), "cell").astype(jnp.float32),
        lax.psum(grad_second_bias.astype(jnp.bfloat16), "cell").astype(jnp.float32),
        lax.psum(grad_up_weight.astype(jnp.bfloat16), "cell").astype(jnp.float32),
        lax.psum(grad_up_bias.astype(jnp.bfloat16), "cell").astype(jnp.float32),
        lax.psum(grad_down_weight.astype(jnp.bfloat16), "cell").astype(jnp.float32),
        lax.psum(grad_down_bias.astype(jnp.bfloat16), "cell").astype(jnp.float32),
    )
    return (
        result_out,
        input_grad,
        grad_first_gain,
        grad_first_bias,
        grad_query_weight,
        grad_query_bias,
        grad_key_weight,
        grad_value_weight,
        grad_value_bias,
        grad_output_weight,
        grad_output_bias,
        grad_second_gain,
        grad_second_bias,
        grad_up_weight,
        grad_up_bias,
        grad_down_weight,
        grad_down_bias,
    )


BOTH = ("cell", "seq")
SEQ_BIT = 1
CORE_BIT = 2
Q_BLOCK = 512
VMEM = 48 * 1024 * 1024


def across(value, bit):
    count = lax.axis_size("cell") * lax.axis_size("seq")
    return lax.ppermute(value, BOTH, [(i, i ^ bit) for i in range(count)])


def across_diagonal(value):
    count = lax.axis_size("cell") * lax.axis_size("seq")
    pairs = [(i, i ^ 3) for i in range(count) if (i & 3) in (1, 2)]
    return lax.ppermute(value, BOTH, pairs)


def in_order(first, own, received, axis=0):
    low = jnp.where(first, own, received)
    high = jnp.where(first, received, own)
    return jnp.concatenate([low, high], axis=axis)


def half_of(value, index, axis=0):
    size = value.shape[axis] // 2
    return lax.dynamic_slice_in_dim(value, index * size, size, axis)


class Place:
    def __init__(self):
        self.x = lax.axis_index("seq")
        cell = lax.axis_index("cell")
        self.core = cell % 2
        self.bits = []
        bit = 2
        while bit < lax.axis_size("cell"):
            self.bits.append((2 * bit, (cell // bit) % 2))
            bit *= 2

    def share(self, value):
        for _, index in self.bits:
            value = half_of(value, index)
        return value

    def widen(self, block):
        for bit, index in reversed(self.bits):
            block = in_order(index == 0, block, across(block, bit))
        return block

    def fetch(self, piece):
        return self.widen(across(self.share(piece), SEQ_BIT))

    def add_up(self, keep, give):
        total = keep.astype(jnp.float32) + across(give, SEQ_BIT).astype(jnp.float32)
        for bit, index in self.bits:
            send = half_of(total, 1 - index).astype(jnp.bfloat16)
            total = half_of(total, index) + across(send, bit).astype(jnp.float32)
        return self.widen(total.astype(jnp.bfloat16))


def attend_kernel(q_ref, k_ref, v_ref, mixed_ref, total_ref):
    f32, bf16 = jnp.float32, jnp.bfloat16
    rows, lanes = q_ref.shape
    lane = lax.broadcasted_iota(jnp.int32, (1, lanes), 1)
    keys = k_ref[...]
    values_t = v_ref[...].T
    for block in range(rows // Q_BLOCK):
        part = pl.ds(block * Q_BLOCK, Q_BLOCK)
        queries = q_ref[part, :] * jnp.asarray(0.125, bf16)
        outs = []
        for head in range(2):
            own = (lane // HDIM) == head
            scores = lax.dot_general(
                keys,
                jnp.where(own, queries, jnp.zeros_like(queries)),
                (((1,), (1,)), ((), ())),
                preferred_element_type=f32,
            )
            largest = jnp.max(scores, axis=0, keepdims=True)
            weights = jnp.exp(scores - largest)
            total = jnp.sum(weights, axis=0, keepdims=True)
            mixed = jnp.dot(
                values_t[head * HDIM : (head + 1) * HDIM, :],
                weights.astype(bf16),
                preferred_element_type=f32,
            )
            outs.append(mixed / total)
            total_ref[head, :, part] = largest + jnp.log(total)
        mixed_ref[part, :] = jnp.concatenate(outs, axis=0).T.astype(bf16)


def attend_back_kernel(q_ref, k_ref, v_ref, total_ref, grad_ref, dq_ref, dk_ref, dv_ref, dk_acc, dv_acc):
    f32, bf16 = jnp.float32, jnp.bfloat16
    rows, lanes = q_ref.shape
    lane = lax.broadcasted_iota(jnp.int32, (1, lanes), 1)
    keys = k_ref[...]
    keys_t = keys.T
    values = v_ref[...]
    nt = (((1,), (1,)), ((), ()))
    for block in range(rows // Q_BLOCK):
        part = pl.ds(block * Q_BLOCK, Q_BLOCK)
        queries = q_ref[part, :] * jnp.asarray(0.125, bf16)
        grads = grad_ref[part, :]
        outs = []
        key_part = None
        value_part = None
        for head in range(2):
            own = (lane // HDIM) == head
            q_own = jnp.where(own, queries, jnp.zeros_like(queries))
            g_own = jnp.where(own, grads, jnp.zeros_like(grads))
            scores = lax.dot_general(keys, q_own, nt, preferred_element_type=f32)
            probs = jnp.exp(scores - total_ref[head, :, part])
            grad_probs = lax.dot_general(values, g_own, nt, preferred_element_type=f32)
            delta = jnp.sum(probs * grad_probs, axis=0, keepdims=True)
            grad_scores = (probs * (grad_probs - delta)).astype(bf16)
            one_value = jnp.dot(probs.astype(bf16), g_own, preferred_element_type=f32)
            one_key = jnp.dot(grad_scores, q_own, preferred_element_type=f32)
            value_part = one_value if head == 0 else value_part + one_value
            key_part = one_key if head == 0 else key_part + one_key
            outs.append(
                jnp.dot(
                    keys_t[head * HDIM : (head + 1) * HDIM, :],
                    grad_scores,
                    preferred_element_type=f32,
                )
            )
        dq_ref[part, :] = (jnp.concatenate(outs, axis=0) * 0.125).T.astype(bf16)
        if block == 0:
            dk_acc[...] = key_part
            dv_acc[...] = value_part
        else:
            dk_acc[...] += key_part
            dv_acc[...] += value_part
    dk_ref[...] = dk_acc[...].astype(bf16)
    dv_ref[...] = dv_acc[...].astype(bf16)


def attend(qkv):
    rows, width = qkv.shape[0], qkv.shape[1] // 3
    pairs = width // 128
    macs = 2 * rows * rows * width
    return pl.pallas_call(
        attend_kernel,
        grid=(pairs,),
        in_specs=[
            pl.BlockSpec((rows, 128), lambda p: (0, p)),
            pl.BlockSpec((rows, 128), lambda p: (0, pairs + p)),
            pl.BlockSpec((rows, 128), lambda p: (0, 2 * pairs + p)),
        ],
        out_specs=[
            pl.BlockSpec((rows, 128), lambda p: (0, p)),
            pl.BlockSpec((2, 1, rows), lambda p: (p, 0, 0)),
        ],
        out_shape=[
            jax.ShapeDtypeStruct((rows, width), jnp.bfloat16),
            jax.ShapeDtypeStruct((2 * pairs, 1, rows), jnp.float32),
        ],
        compiler_params=pltpu.CompilerParams(vmem_limit_bytes=VMEM),
        cost_estimate=pl.CostEstimate(
            flops=8 * macs, bytes_accessed=8 * rows * width, transcendentals=macs // 128
        ),
        name="attend",
    )(qkv, qkv, qkv)


def attend_back(qkv, total, grad_mixed):
    rows, width = grad_mixed.shape
    pairs = width // 128
    macs = 5 * rows * rows * width
    block = pl.BlockSpec((rows, 128), lambda p: (0, p))
    return pl.pallas_call(
        attend_back_kernel,
        grid=(pairs,),
        in_specs=[
            block,
            pl.BlockSpec((rows, 128), lambda p: (0, pairs + p)),
            pl.BlockSpec((rows, 128), lambda p: (0, 2 * pairs + p)),
            pl.BlockSpec((2, 1, rows), lambda p: (p, 0, 0)),
            block,
        ],
        out_specs=[block] * 3,
        out_shape=[jax.ShapeDtypeStruct((rows, width), jnp.bfloat16)] * 3,
        scratch_shapes=[pltpu.VMEM((rows, 128), jnp.float32)] * 2,
        compiler_params=pltpu.CompilerParams(vmem_limit_bytes=VMEM),
        cost_estimate=pl.CostEstimate(
            flops=8 * macs, bytes_accessed=14 * rows * width, transcendentals=macs // 320
        ),
        name="attend_back",
    )(qkv, qkv, qkv, total, grad_mixed)


def tuned(
    tokens,
    out_grad,
    query_counts,
    first_gain,
    first_bias,
    query_weight,
    query_bias,
    key_weight,
    value_weight,
    value_bias,
    output_weight,
    output_bias,
    second_gain,
    second_bias,
    up_weight,
    up_bias,
    down_weight,
    down_bias,
):
    f32, bf16 = jnp.float32, jnp.bfloat16
    at = Place()
    x, core = at.x, at.core
    swapped = x != core
    rows, width = tokens.shape[1:]
    hidden_width = up_weight.shape[1] // 2
    head_width = width // 2

    vectors = (first_gain, first_bias, query_bias, value_bias, output_bias, second_gain, second_bias, down_bias, up_bias)
    packed = jnp.concatenate(vectors)
    packed = in_order(x == 0, packed[None], across(packed, SEQ_BIT)[None])
    full = []
    start = 0
    for vector in vectors:
        full.append(packed[:, start : start + vector.shape[0]].reshape(-1).astype(f32))
        start += vector.shape[0]
    gain_one, bias_one, q_bias, v_bias, o_bias, gain_two, bias_two, d_bias, u_bias = full

    own = tokens[0]
    own = jnp.where(swapped, across_diagonal(own), own)
    own_grad = out_grad[0]
    own_grad = jnp.where(swapped, across_diagonal(own_grad), own_grad)
    weight_cell = jnp.broadcast_to(jnp.sqrt(query_counts.astype(f32) / 1000.0), (8, 128))
    weight_cell = jnp.where(swapped, across_diagonal(weight_cell), weight_cell)[:1, :1]

    def columns(weight):
        return half_of(weight, core, 1)

    def up_columns(weight):
        halves = weight.reshape(weight.shape[0], 2, 2, hidden_width // 2)
        halves = lax.dynamic_index_in_dim(halves, core, 2, keepdims=False)
        return halves.reshape(weight.shape[0], hidden_width)

    qkv_piece = jnp.concatenate([columns(query_weight), columns(key_weight), columns(value_weight)], axis=1)
    qkv_weight = in_order(x == 0, qkv_piece, at.fetch(qkv_piece))
    out_piece = at.fetch(half_of(output_weight, core))
    out_piece = in_order(core == 0, out_piece, across(out_piece, CORE_BIT))
    out_weight = in_order(x == 0, output_weight, out_piece)
    up_piece = up_columns(up_weight)
    up_all = in_order(x == 0, up_piece, at.fetch(up_piece))
    down_piece = half_of(down_weight, core)
    down_all = in_order(x == 0, down_piece, at.fetch(down_piece))

    own = own.astype(f32)
    standard_one, inverse_one = standardize(own)
    normed_own = (standard_one * gain_one + bias_one).astype(bf16)
    normed_one = jnp.concatenate([normed_own, across(normed_own, CORE_BIT)])
    qkv_bias = jnp.concatenate(
        [half_of(q_bias, core), jnp.zeros((head_width,), f32), half_of(v_bias, core)]
    )
    qkv = (matmul(normed_one, qkv_weight) + qkv_bias).astype(bf16)
    mixed_heads, log_total = attend(qkv)
    other_heads = across(mixed_heads, CORE_BIT)
    other_heads = jnp.concatenate([other_heads[rows:], other_heads[:rows]])
    mixed = in_order(core == 0, mixed_heads, other_heads, axis=1)
    middle = own + matmul(mixed[:rows], out_weight) + o_bias
    standard_two, inverse_two = standardize(middle)
    normed_own = (standard_two * gain_two + bias_two).astype(bf16)
    normed_two = jnp.concatenate([normed_own, across(normed_own, CORE_BIT)])
    up_bias_own = lax.dynamic_index_in_dim(u_bias.reshape(2, 2, -1), core, 1, keepdims=False).reshape(-1)
    up_proj = matmul(normed_two, up_all) + up_bias_own
    hidden = gelu_value(up_proj).astype(bf16)

    grad_result = own_grad.astype(f32) * weight_cell
    grad_own = grad_result.astype(bf16)
    grad_ffn = jnp.concatenate([grad_own, across(grad_own, CORE_BIT)])

    def weight_sum(left, right):
        give = weight_grad(half_of(left, 1 - x, 1), right).astype(bf16)
        keep = weight_grad(half_of(left, x, 1), right).astype(bf16)
        return at.add_up(keep, give)

    sum_down = weight_sum(hidden, grad_ffn)
    grad_up = (matmul_right_t(grad_ffn, down_all) * gelu_slope(up_proj)).astype(bf16)
    sum_up = weight_sum(normed_two, grad_up)
    partial = matmul_right_t(grad_up, up_all)
    grad_normed_two = partial[:rows] + across(partial[rows:].astype(bf16), CORE_BIT).astype(f32)
    grad_middle = grad_result + standardize_back(grad_normed_two, standard_two, inverse_two, gain_two)
    grad_attn_own = grad_middle.astype(bf16)
    grad_attn = jnp.concatenate([grad_attn_own, across(grad_attn_own, CORE_BIT)])
    sum_out = weight_sum(mixed, half_of(grad_attn, core, 1))

    partial = matmul(hidden, down_all)
    result = middle + partial[:rows] + across(partial[rows:].astype(bf16), CORE_BIT).astype(f32) + d_bias
    result = result.astype(bf16)
    result = jnp.where(swapped, across_diagonal(result), result)

    grad_mixed = matmul_right_t(grad_attn, half_of(out_weight, core)).astype(bf16)
    grad_qkv = jnp.concatenate(attend_back(qkv, log_total, grad_mixed), axis=1)
    sum_qkv = weight_sum(normed_one, grad_qkv)
    partial = matmul_right_t(grad_qkv, qkv_weight)
    grad_normed_one = partial[:rows] + across(partial[rows:].astype(bf16), CORE_BIT).astype(f32)
    input_grad = grad_middle + standardize_back(grad_normed_one, standard_one, inverse_one, gain_one)
    input_grad = input_grad.astype(bf16)
    input_grad = jnp.where(swapped, across_diagonal(input_grad), input_grad)

    def at_core(value):
        zero = jnp.zeros_like(value)
        return jnp.concatenate([jnp.where(core == 0, value, zero), jnp.where(core == 0, zero, value)], axis=-1)

    qkv_sum = column_sum(grad_qkv).reshape(3, head_width)
    up_sum = at_core(column_sum(grad_up).reshape(2, 1, -1)).reshape(-1)
    sums = [
        jnp.sum(grad_normed_one * standard_one, axis=0),
        jnp.sum(grad_normed_one, axis=0),
        at_core(qkv_sum[0]),
        at_core(qkv_sum[2]),
        column_sum(grad_attn_own),
        jnp.sum(grad_normed_two * standard_two, axis=0),
        jnp.sum(grad_normed_two, axis=0),
        column_sum(grad_own),
        up_sum,
    ]
    sums = [half_of(v, x) for v in jnp.split(lax.psum(jnp.concatenate(sums), BOTH), np_offsets(sums))]
    s_gain_one, s_bias_one, s_q_bias, s_v_bias, s_o_bias, s_gain_two, s_bias_two, s_d_bias, s_u_bias = sums

    def both_columns(value):
        return in_order(core == 0, value, across(value, CORE_BIT), axis=1).astype(f32)

    other = across(sum_qkv, CORE_BIT)
    each = [
        in_order(
            core == 0,
            sum_qkv[:, i * head_width : (i + 1) * head_width],
            other[:, i * head_width : (i + 1) * head_width],
            axis=1,
        ).astype(f32)
        for i in range(3)
    ]
    up_own = sum_up.reshape(-1, 2, hidden_width // 2)
    up_other = across(sum_up, CORE_BIT).reshape(-1, 2, hidden_width // 2)
    s_up = jnp.concatenate(
        [in_order(core == 0, up_own[:, h], up_other[:, h], axis=1) for h in range(2)], axis=1
    ).astype(f32)
    s_down = in_order(core == 0, sum_down, across(sum_down, CORE_BIT)).astype(f32)
    return (
        result[None],
        input_grad[None],
        s_gain_one,
        s_bias_one,
        each[0],
        s_q_bias,
        each[1],
        each[2],
        s_v_bias,
        both_columns(sum_out),
        s_o_bias,
        s_gain_two,
        s_bias_two,
        s_up,
        s_u_bias,
        s_down,
        s_d_bias,
    )


def np_offsets(values):
    offsets = []
    total = 0
    for value in values[:-1]:
        total += value.shape[0]
        offsets.append(total)
    return offsets


def chosen(mesh):
    cells, blocks = mesh.shape["cell"], mesh.shape["seq"]

    def per_device(tokens, *rest):
        power = cells & (cells - 1) == 0
        if blocks == 2 and power and cells >= 4 and tokens.shape[0] == 1:
            return tuned(tokens, *rest)
        return general(tokens, *rest)

    return per_device


def solution(mesh):
    placed = (
        P("cell", "seq", None),
        P("cell", "seq", None),
        P("cell"),
        P("seq"),
        P("seq"),
        P("seq", None),
        P("seq"),
        P("seq", None),
        P("seq", None),
        P("seq"),
        P("seq", None),
        P("seq"),
        P("seq"),
        P("seq"),
        P("seq", None),
        P("seq"),
        P("seq", None),
        P("seq"),
    )
    return jax.shard_map(
        chosen(mesh),
        mesh=mesh,
        in_specs=placed,
        out_specs=(
            P("cell", "seq", None),
            P("cell", "seq", None),
            P("seq"),
            P("seq"),
            P("seq", None),
            P("seq"),
            P("seq", None),
            P("seq", None),
            P("seq"),
            P("seq", None),
            P("seq"),
            P("seq"),
            P("seq"),
            P("seq", None),
            P("seq"),
            P("seq", None),
            P("seq"),
        ),
        check_vma=False,
    )
```

```python
import jax
import jax.numpy as jnp
from jax import lax
from jax.experimental import pallas as pl
from jax.experimental.pallas import tpu as pltpu
from jax.sharding import PartitionSpec as P

HEADS = 20
HDIM = 64


def from_behind(value, axis, steps):
    count = lax.axis_size(axis)
    pairs = [(source, (source + steps) % count) for source in range(count)]
    return lax.ppermute(value, axis, pairs)


def for_sending(x):
    return jax.tree.map(lambda a: a.astype(jnp.bfloat16) if a.dtype == jnp.float32 else a, x)


def matmul(left, right):
    return jnp.dot(left, right, preferred_element_type=jnp.float32)


def matmul_right_t(left, right):
    return jnp.einsum("to,io->ti", left, right, preferred_element_type=jnp.float32)


def weight_grad(left, right):
    return jnp.einsum("ti,to->io", left, right, preferred_element_type=jnp.float32)


def standardize(values):
    average = jnp.mean(values, axis=-1, keepdims=True)
    centred = values - average
    inverse = lax.rsqrt(jnp.mean(centred * centred, axis=-1, keepdims=True) + 1e-05)
    return (centred * inverse, inverse)


def standardize_back(grad_normed, standard, inverse, gain_vec):
    scaled = grad_normed * gain_vec
    return inverse * (
        scaled
        - jnp.mean(scaled, axis=-1, keepdims=True)
        - standard * jnp.mean(scaled * standard, axis=-1, keepdims=True)
    )


def gelu_value(up_proj):
    return 0.5 * up_proj * (1.0 + lax.erf(up_proj * 0.7071067811865476))


def gelu_slope(up_proj):
    return (
        0.5 * (1.0 + lax.erf(up_proj * 0.7071067811865476))
        + up_proj * jnp.exp(-0.5 * up_proj * up_proj) * 0.3989422804014327
    )


def score_block(queries, key_rows):
    return (
        jnp.einsum("cqhd,ckhd->chqk", queries, key_rows, preferred_element_type=jnp.float32) * 0.125
    )


def column_sum(values):
    return jnp.sum(values.astype(jnp.float32), axis=0)


def general(
    tokens,
    out_grad,
    query_counts,
    first_gain,
    first_bias,
    query_weight,
    query_bias,
    key_weight,
    value_weight,
    value_bias,
    output_weight,
    output_bias,
    second_gain,
    second_bias,
    up_weight,
    up_bias,
    down_weight,
    down_bias,
):
    (
        first_gain,
        first_bias,
        query_weight,
        query_bias,
        key_weight,
        value_weight,
        value_bias,
        output_weight,
        output_bias,
        second_gain,
        second_bias,
        up_weight,
        up_bias,
        down_weight,
        down_bias,
    ) = (
        lax.all_gather(first_gain, "seq", axis=0, tiled=True),
        lax.all_gather(first_bias, "seq", axis=0, tiled=True),
        lax.all_gather(query_weight, "seq", axis=0, tiled=True),
        lax.all_gather(query_bias, "seq", axis=0, tiled=True),
        lax.all_gather(key_weight, "seq", axis=0, tiled=True),
        lax.all_gather(value_weight, "seq", axis=0, tiled=True),
        lax.all_gather(value_bias, "seq", axis=0, tiled=True),
        lax.all_gather(output_weight, "seq", axis=0, tiled=True),
        lax.all_gather(output_bias, "seq", axis=0, tiled=True),
        lax.all_gather(second_gain, "seq", axis=0, tiled=True),
        lax.all_gather(second_bias, "seq", axis=0, tiled=True),
        lax.all_gather(up_weight, "seq", axis=0, tiled=True),
        lax.all_gather(up_bias, "seq", axis=0, tiled=True),
        lax.all_gather(down_weight, "seq", axis=0, tiled=True),
        lax.all_gather(down_bias, "seq", axis=0, tiled=True),
    )
    f32 = jnp.float32
    bf16 = jnp.bfloat16
    gain_first = first_gain.astype(f32)
    gain_second = second_gain.astype(f32)
    cell_count, seg_len, model_width = tokens.shape
    row_count = cell_count * seg_len
    head_shape = (cell_count, seg_len, HEADS, HDIM)
    cycle_size = lax.axis_size("seq")
    flat_input = tokens.reshape(row_count, model_width).astype(f32)
    standard_one, inverse_one = standardize(flat_input)
    normed_one = (standard_one * gain_first + first_bias.astype(f32)).astype(bf16)
    query_heads = (
        (matmul(normed_one, query_weight) + query_bias.astype(f32)).astype(bf16).reshape(head_shape)
    )
    key_heads = matmul(normed_one, key_weight).astype(bf16).reshape(head_shape)
    value_heads = (
        (matmul(normed_one, value_weight) + value_bias.astype(f32)).astype(bf16).reshape(head_shape)
    )
    running_max = jnp.full((cell_count, HEADS, seg_len), -1e30, f32)
    running_sum = jnp.zeros((cell_count, HEADS, seg_len), f32)
    weighted = jnp.zeros((cell_count, HEADS, seg_len, HDIM), f32)
    travel = (key_heads, value_heads)
    for step in range(cycle_size):
        if step > 0:
            travel = from_behind((travel[0], travel[1]), "seq", 1)
        scores = score_block(query_heads, travel[0])
        new_max = jnp.maximum(running_max, jnp.max(scores, axis=-1))
        rescale = jnp.exp(running_max - new_max)
        exp_scores = jnp.exp(scores - new_max[..., None])
        running_sum = running_sum * rescale + jnp.sum(exp_scores, axis=-1)
        weighted = weighted * rescale[..., None] + jnp.einsum(
            "chqk,ckhd->chqd", exp_scores.astype(bf16), travel[1], preferred_element_type=f32
        )
        running_max = new_max
    attended = weighted / running_sum[..., None]
    log_total = running_max + jnp.log(running_sum)
    mixed = attended.transpose(0, 2, 1, 3).reshape(row_count, model_width).astype(bf16)
    middle = flat_input + matmul(mixed, output_weight) + output_bias.astype(f32)
    standard_two, inverse_two = standardize(middle)
    normed_two = (standard_two * gain_second + second_bias.astype(f32)).astype(bf16)
    up_proj = matmul(normed_two, up_weight) + up_bias.astype(f32)
    hidden = gelu_value(up_proj).astype(bf16)
    result = middle + matmul(hidden, down_weight) + down_bias.astype(f32)
    result_out = result.astype(bf16).reshape(cell_count, seg_len, model_width)
    weight_cell = jnp.sqrt(query_counts.astype(f32) / 1000.0)
    grad_result = (out_grad.astype(f32) * weight_cell[:, None, None]).reshape(
        row_count, model_width
    )
    grad_ffn_out = grad_result.astype(bf16)
    grad_down_weight = weight_grad(hidden, grad_ffn_out)
    grad_down_bias = column_sum(grad_ffn_out)
    grad_up = (matmul_right_t(grad_ffn_out, down_weight) * gelu_slope(up_proj)).astype(bf16)
    grad_up_weight = weight_grad(normed_two, grad_up)
    grad_up_bias = column_sum(grad_up)
    grad_normed_two = matmul_right_t(grad_up, up_weight)
    grad_second_gain = jnp.sum(grad_normed_two * standard_two, axis=0)
    grad_second_bias = jnp.sum(grad_normed_two, axis=0)
    grad_middle = grad_result + standardize_back(
        grad_normed_two, standard_two, inverse_two, gain_second
    )
    grad_attn_out = grad_middle.astype(bf16)
    grad_output_weight = weight_grad(mixed, grad_attn_out)
    grad_output_bias = column_sum(grad_attn_out)
    grad_mixed = matmul_right_t(grad_attn_out, output_weight).astype(bf16).reshape(head_shape)
    row_delta = jnp.sum(grad_mixed.astype(f32).transpose(0, 2, 1, 3) * attended, axis=-1)
    grad_query_acc = jnp.zeros(head_shape, f32)
    moving = (jnp.zeros(head_shape, f32), jnp.zeros(head_shape, f32))
    travel = (key_heads, value_heads)
    for step in range(cycle_size):
        if step > 0:
            travel = from_behind((travel[0], travel[1]), "seq", 1)
        block_keys, block_values = travel
        scores = score_block(query_heads, block_keys)
        prob_block = jnp.exp(scores - log_total[..., None])
        part_values = jnp.einsum(
            "chqk,cqhd->ckhd", prob_block.astype(bf16), grad_mixed, preferred_element_type=f32
        )
        grad_probs = jnp.einsum(
            "cqhd,ckhd->chqk", grad_mixed, block_values, preferred_element_type=f32
        )
        grad_scores = (prob_block * (grad_probs - row_delta[..., None])).astype(bf16)
        grad_query_acc = (
            grad_query_acc
            + jnp.einsum("chqk,ckhd->cqhd", grad_scores, block_keys, preferred_element_type=f32)
            * 0.125
        )
        part_keys = (
            jnp.einsum("chqk,cqhd->ckhd", grad_scores, query_heads, preferred_element_type=f32)
            * 0.125
        )
        moving = from_behind(
            (for_sending(moving[0] + part_keys), for_sending(moving[1] + part_values)), "seq", 1
        )
    grad_queries = grad_query_acc.astype(bf16).reshape(row_count, model_width)
    grad_keys = moving[0].astype(bf16).reshape(row_count, model_width)
    grad_values = moving[1].astype(bf16).reshape(row_count, model_width)
    grad_query_weight = weight_grad(normed_one, grad_queries)
    grad_query_bias = column_sum(grad_queries)
    grad_key_weight = weight_grad(normed_one, grad_keys)
    grad_value_weight = weight_grad(normed_one, grad_values)
    grad_value_bias = column_sum(grad_values)
    grad_normed_one = (
        matmul_right_t(grad_queries, query_weight)
        + matmul_right_t(grad_keys, key_weight)
        + matmul_right_t(grad_values, value_weight)
    )
    grad_first_gain = jnp.sum(grad_normed_one * standard_one, axis=0)
    grad_first_bias = jnp.sum(grad_normed_one, axis=0)
    grad_input = grad_middle + standardize_back(
        grad_normed_one, standard_one, inverse_one, gain_first
    )
    input_grad = grad_input.astype(bf16).reshape(cell_count, seg_len, model_width)
    shared_all = (
        lax.psum_scatter(
            grad_first_gain.astype(jnp.bfloat16), "seq", scatter_dimension=0, tiled=True
        ).astype(jnp.float32),
        lax.psum_scatter(
            grad_first_bias.astype(jnp.bfloat16), "seq", scatter_dimension=0, tiled=True
        ).astype(jnp.float32),
        lax.psum_scatter(
            grad_query_weight.astype(jnp.bfloat16), "seq", scatter_dimension=0, tiled=True
        ).astype(jnp.float32),
        lax.psum_scatter(
            grad_query_bias.astype(jnp.bfloat16), "seq", scatter_dimension=0, tiled=True
        ).astype(jnp.float32),
        lax.psum_scatter(
            grad_key_weight.astype(jnp.bfloat16), "seq", scatter_dimension=0, tiled=True
        ).astype(jnp.float32),
        lax.psum_scatter(
            grad_value_weight.astype(jnp.bfloat16), "seq", scatter_dimension=0, tiled=True
        ).astype(jnp.float32),
        lax.psum_scatter(
            grad_value_bias.astype(jnp.bfloat16), "seq", scatter_dimension=0, tiled=True
        ).astype(jnp.float32),
        lax.psum_scatter(
            grad_output_weight.astype(jnp.bfloat16), "seq", scatter_dimension=0, tiled=True
        ).astype(jnp.float32),
        lax.psum_scatter(
            grad_output_bias.astype(jnp.bfloat16), "seq", scatter_dimension=0, tiled=True
        ).astype(jnp.float32),
        lax.psum_scatter(
            grad_second_gain.astype(jnp.bfloat16), "seq", scatter_dimension=0, tiled=True
        ).astype(jnp.float32),
        lax.psum_scatter(
            grad_second_bias.astype(jnp.bfloat16), "seq", scatter_dimension=0, tiled=True
        ).astype(jnp.float32),
        lax.psum_scatter(
            grad_up_weight.astype(jnp.bfloat16), "seq", scatter_dimension=0, tiled=True
        ).astype(jnp.float32),
        lax.psum_scatter(
            grad_up_bias.astype(jnp.bfloat16), "seq", scatter_dimension=0, tiled=True
        ).astype(jnp.float32),
        lax.psum_scatter(
            grad_down_weight.astype(jnp.bfloat16), "seq", scatter_dimension=0, tiled=True
        ).astype(jnp.float32),
        lax.psum_scatter(
            grad_down_bias.astype(jnp.bfloat16), "seq", scatter_dimension=0, tiled=True
        ).astype(jnp.float32),
    )
    (
        grad_first_gain,
        grad_first_bias,
        grad_query_weight,
        grad_query_bias,
        grad_key_weight,
        grad_value_weight,
        grad_value_bias,
        grad_output_weight,
        grad_output_bias,
        grad_second_gain,
        grad_second_bias,
        grad_up_weight,
        grad_up_bias,
        grad_down_weight,
        grad_down_bias,
    ) = shared_all
    (
        grad_first_gain,
        grad_first_bias,
        grad_query_weight,
        grad_query_bias,
        grad_key_weight,
        grad_value_weight,
        grad_value_bias,
        grad_output_weight,
        grad_output_bias,
        grad_second_gain,
        grad_second_bias,
        grad_up_weight,
        grad_up_bias,
        grad_down_weight,
        grad_down_bias,
    ) = (
        lax.psum(grad_first_gain.astype(jnp.bfloat16), "cell").astype(jnp.float32),
        lax.psum(grad_first_bias.astype(jnp.bfloat16), "cell").astype(jnp.float32),
        lax.psum(grad_query_weight.astype(jnp.bfloat16), "cell").astype(jnp.float32),
        lax.psum(grad_query_bias.astype(jnp.bfloat16), "cell").astype(jnp.float32),
        lax.psum(grad_key_weight.astype(jnp.bfloat16), "cell").astype(jnp.float32),
        lax.psum(grad_value_weight.astype(jnp.bfloat16), "cell").astype(jnp.float32),
        lax.psum(grad_value_bias.astype(jnp.bfloat16), "cell").astype(jnp.float32),
        lax.psum(grad_output_weight.astype(jnp.bfloat16), "cell").astype(jnp.float32),
        lax.psum(grad_output_bias.astype(jnp.bfloat16), "cell").astype(jnp.float32),
        lax.psum(grad_second_gain.astype(jnp.bfloat16), "cell").astype(jnp.float32),
        lax.psum(grad_second_bias.astype(jnp.bfloat16), "cell").astype(jnp.float32),
        lax.psum(grad_up_weight.astype(jnp.bfloat16), "cell").astype(jnp.float32),
        lax.psum(grad_up_bias.astype(jnp.bfloat16), "cell").astype(jnp.float32),
        lax.psum(grad_down_weight.astype(jnp.bfloat16), "cell").astype(jnp.float32),
        lax.psum(grad_down_bias.astype(jnp.bfloat16), "cell").astype(jnp.float32),
    )
    return (
        result_out,
        input_grad,
        grad_first_gain,
        grad_first_bias,
        grad_query_weight,
        grad_query_bias,
        grad_key_weight,
        grad_value_weight,
        grad_value_bias,
        grad_output_weight,
        grad_output_bias,
        grad_second_gain,
        grad_second_bias,
        grad_up_weight,
        grad_up_bias,
        grad_down_weight,
        grad_down_bias,
    )


BOTH = ("cell", "seq")
CORE_BIT = 2
Q_BLOCK = 512
VMEM = 48 * 1024 * 1024


def across(value, bit):
    count = lax.axis_size("cell") * lax.axis_size("seq")
    return lax.ppermute(value, BOTH, [(i, i ^ bit) for i in range(count)])


def across_diagonal(value):
    count = lax.axis_size("cell") * lax.axis_size("seq")
    pairs = [(i, i ^ 3) for i in range(count) if (i & 3) in (1, 2)]
    return lax.ppermute(value, BOTH, pairs)


def in_order(first, own, received, axis=0):
    low = jnp.where(first, own, received)
    high = jnp.where(first, received, own)
    return jnp.concatenate([low, high], axis=axis)


def half_of(value, index, axis=0):
    size = value.shape[axis] // 2
    return lax.dynamic_slice_in_dim(value, index * size, size, axis)


MESH = pl.DeviceIdType.MESH
ANY = pl.BlockSpec(memory_space=pl.ANY)
EDGE = 640


class Spot:
    def __init__(self):
        self.x = lax.axis_index("seq")
        self.cell = lax.axis_index("cell")
        self.core = lax.rem(self.cell, 2)
        self.y = lax.rem(self.cell // 2, 2)
        self.low = lax.rem(self.cell // 4, 2)
        self.high = lax.rem(self.cell // 8, 2)

    def flip(self, index, bit):
        return {"cell": self.cell + bit - 2 * bit * index}

    def over(self, name):
        if name == "x":
            return {"seq": 1 - self.x}
        if name == "core":
            return self.flip(self.core, 1)
        if name == "diagonal":
            return {"seq": 1 - self.x, **self.flip(self.core, 1)}
        return self.flip(*{"y": (self.y, 2), "low": (self.low, 4), "high": (self.high, 8)}[name])

    def meet(self, names):
        barrier = pltpu.get_barrier_semaphore()
        for name in names:
            pl.semaphore_signal(barrier, inc=1, device_id=self.over(name), device_id_type=MESH)
        pl.semaphore_wait(barrier, len(names))

    def send(self, name, source, target, send_sem, recv_sem):
        return pltpu.make_async_remote_copy(
            source, target, send_sem, recv_sem, device_id=self.over(name), device_id_type=MESH
        )


def rows_at(start, size):
    return pl.ds(pl.multiple_of(start, 16), size)


def lanes_at(start, size):
    return pl.ds(pl.multiple_of(start, 128), size)


def gather_kernel(
    tokens, out_grad, cell_weight, vectors, wq, wk, wv, wo, wup, wdown,
    own, own_grad, own_weight, all_vectors, qkv_w, out_w, up_w, down_w,
    send_sems, recv_sems, local_sems, side_send, side_recv, side_local,
):
    at = Spot()
    x, core = at.x, at.core
    at.meet(("x", "core", "diagonal", "y", "low", "high"))
    side = [(tokens, own), (cell_weight, own_weight), (out_grad, own_grad)]
    diagonal = [at.send("diagonal", s, t, side_send.at[i], side_recv.at[i]) for i, (s, t) in enumerate(side)]
    straight = [pltpu.make_async_copy(s, t, side_local.at[i]) for i, (s, t) in enumerate(side)]

    def swap_start(i):
        @pl.when(x != core)
        def _():
            diagonal[i].start()

        @pl.when(x == core)
        def _():
            straight[i].start()

    swap_start(0)
    swap_start(1)
    vector_copy = at.send("x", vectors, all_vectors.at[x], side_send.at[3], side_recv.at[3])
    vector_copy.start()
    vector_local = pltpu.make_async_copy(vectors, all_vectors.at[x], side_local.at[3])
    vector_local.start()

    chunks = []
    for i, ref in enumerate((wq, wk, wv)):
        chunks.append((ref.at[:, lanes_at(core * EDGE, EDGE)], qkv_w, EDGE, 0, i * EDGE))
    for i in range(4):
        start = (i // 2) * 4 * EDGE + core * 2 * EDGE + (i % 2) * EDGE
        chunks.append((wup.at[:, lanes_at(start, EDGE)], up_w, EDGE, 0, i * EDGE))
    for i in range(4):
        source = wdown.at[rows_at(core * 2 * EDGE + (i // 2) * EDGE, EDGE), pl.ds((i % 2) * EDGE, EDGE)]
        chunks.append((source, down_w, 2 * EDGE, (i // 2) * EDGE, (i % 2) * EDGE))
    eighth = EDGE // 8
    place = at.y * 4 + at.low * 2 + at.high

    def region(k, half, start, size):
        _, ref, stride, row, column = chunks[k]
        return ref.at[rows_at(half * stride + row + start * eighth, size * eighth), pl.ds(column, EDGE)]

    stages = {}
    for k, chunk in enumerate(chunks):
        stages["x", k] = at.send(
            "x", chunk[0].at[rows_at(place * eighth, eighth)], region(k, x, place, 1), send_sems.at[0, k], recv_sems.at[0, k]
        )
        for s, (name, start, size) in enumerate(
            (("high", place, 1), ("low", at.y * 4 + at.low * 2, 2), ("y", at.y * 4, 4))
        ):
            part = region(k, 1 - x, start, size)
            stages[name, k] = at.send(name, part, part, send_sems.at[s + 1, k], recv_sems.at[s + 1, k])
        stages["local", k] = pltpu.make_async_copy(chunk[0], region(k, x, 0, 8), local_sems.at[k])

    half = EDGE // 2
    out_x = at.send(
        "x", wo.at[rows_at(core * half, half)], out_w.at[rows_at(x * EDGE + core * half, half)], side_send.at[4], side_recv.at[4]
    )
    part = out_w.at[rows_at((1 - x) * EDGE + core * half, half)]
    out_core = at.send("core", part, part, side_send.at[5], side_recv.at[5])
    out_local = pltpu.make_async_copy(wo, out_w.at[rows_at(x * EDGE, EDGE)], side_local.at[4])

    count = len(chunks)
    for k in range(3):
        stages["x", k].start()
    out_x.start()
    for k in range(3, count):
        stages["x", k].start()
    swap_start(2)
    for k in range(count):
        stages["local", k].start()
    out_local.start()
    for tick in range(count + 3):
        for before, name, after in ((0, "x", "high"), (1, "high", "low"), (2, "low", "y"), (3, "y", None)):
            k = tick - before
            if 0 <= k < count:
                stages[name, k].wait_recv()
                if after:
                    stages[after, k].start()
        if tick == 3:
            out_x.wait_recv()
            out_core.start()
    out_core.wait_recv()
    vector_copy.wait()
    vector_local.wait()
    for i in range(3):

        @pl.when(x != core)
        def _():
            diagonal[i].wait()

        @pl.when(x == core)
        def _():
            straight[i].wait()

    for k in range(count):
        stages["local", k].wait()
        for name in ("x", "high", "low", "y"):
            stages[name, k].wait_send()
    out_local.wait()
    out_x.wait_send()
    out_core.wait_send()


def gather(*args):
    tokens = args[0]
    bf16 = jnp.bfloat16
    shape = jax.ShapeDtypeStruct
    width = tokens.shape[1]
    vectors = args[3]
    return pl.pallas_call(
        gather_kernel,
        in_specs=[ANY] * len(args),
        out_specs=[ANY] * 8,
        out_shape=[
            shape(tokens.shape, bf16),
            shape(tokens.shape, bf16),
            shape(args[2].shape, jnp.float32),
            shape((2,) + vectors.shape, bf16),
            shape((width, 3 * EDGE), bf16),
            shape((width, width), bf16),
            shape((width, 4 * EDGE), bf16),
            shape((4 * EDGE, width), bf16),
        ],
        scratch_shapes=[
            pltpu.SemaphoreType.DMA((4, 11)),
            pltpu.SemaphoreType.DMA((4, 11)),
            pltpu.SemaphoreType.DMA((11,)),
            pltpu.SemaphoreType.DMA((6,)),
            pltpu.SemaphoreType.DMA((6,)),
            pltpu.SemaphoreType.DMA((5,)),
        ],
        compiler_params=pltpu.CompilerParams(collective_id=0, has_side_effects=True),
        name="gather",
    )(*args)


def reduce_kernel(
    give_down, keep_down, give_up, keep_up, give_out, keep_out, give_qkv, keep_qkv, vec,
    down_ref, up_ref, out_ref, q_ref, k_ref, v_ref, vec_ref,
    acc, from_x, from_y, from_low, from_high, res, vec_acc, vec_in,
    send_sems, recv_sems, load_sems, store_sems, vec_send, vec_recv, vec_local,
):
    f32, bf16 = jnp.float32, jnp.bfloat16
    at = Spot()
    core = at.core
    at.meet(("x", "core", "y", "low", "high"))
    chunks = []
    for i in range(4):
        part = (pl.ds((i // 2) * EDGE, EDGE), pl.ds((i % 2) * EDGE, EDGE))
        target = down_ref.at[rows_at(core * 2 * EDGE + (i // 2) * EDGE, EDGE), pl.ds((i % 2) * EDGE, EDGE)]
        chunks.append((give_down.at[part], keep_down.at[part], target))
    for i in range(4):
        part = (slice(None), pl.ds(i * EDGE, EDGE))
        target = up_ref.at[:, lanes_at((i // 2) * 4 * EDGE + core * 2 * EDGE + (i % 2) * EDGE, EDGE)]
        chunks.append((give_up.at[part], keep_up.at[part], target))
    mine = lanes_at(core * EDGE, EDGE)
    chunks.append((give_out, keep_out, out_ref.at[:, mine]))
    for i, ref in enumerate((q_ref, k_ref, v_ref)):
        part = (slice(None), pl.ds(i * EDGE, EDGE))
        chunks.append((give_qkv.at[part], keep_qkv.at[part], ref.at[:, mine]))
    count = len(chunks)

    half, quarter, eighth = EDGE // 2, EDGE // 4, EDGE // 8
    y0 = at.y * half
    l0 = y0 + at.low * quarter
    h0 = l0 + at.high * eighth
    ops = {}
    for k, (give, keep, target) in enumerate(chunks):
        hops = (
            ("x", "x", give, from_x.at[k]),
            ("y", "y", acc.at[k, rows_at((1 - at.y) * half, half)], from_y.at[k]),
            ("low", "low", acc.at[k, rows_at(y0 + (1 - at.low) * quarter, quarter)], from_low.at[k]),
            ("high", "high", acc.at[k, rows_at(l0 + (1 - at.high) * eighth, eighth)], from_high.at[k]),
            ("all_high", "high", res.at[k, rows_at(h0, eighth)], res.at[k, rows_at(h0, eighth)]),
            ("all_low", "low", res.at[k, rows_at(l0, quarter)], res.at[k, rows_at(l0, quarter)]),
            ("all_y", "y", res.at[k, rows_at(y0, half)], res.at[k, rows_at(y0, half)]),
            ("core", "core", res.at[k], target),
        )
        for s, (stage, name, source, goal) in enumerate(hops):
            ops[stage, k] = at.send(name, source, goal, send_sems.at[s, k], recv_sems.at[s, k])
        ops["load", k] = pltpu.make_async_copy(keep, acc.at[k], load_sems.at[k])
        ops["store", k] = pltpu.make_async_copy(res.at[k], target, store_sems.at[k])

    def add(k, start, size, other, goal):
        @pl.loop(0, size // 80)
        def _(i):
            here = rows_at(start + i * 80, 80)
            there = rows_at(i * 80, 80)
            goal[k, here, :] = (acc[k, here, :].astype(f32) + other[k, there, :].astype(f32)).astype(bf16)

    for k in range(count):
        ops["x", k].start()
        ops["load", k].start()
    vec_load = pltpu.make_async_copy(vec, vec_acc.at[0], vec_local.at[0])
    vec_load.start()
    vec_load.wait()
    vec_names = ("x", "core", "y", "low", "high")
    vec_ops = [
        at.send(name, vec_acc.at[i], vec_in.at[i], vec_send.at[i], vec_recv.at[i]) for i, name in enumerate(vec_names)
    ]
    vec_ops[0].start()
    after = ("y", "low", "high", "all_high", "all_low", "all_y", "core", None)
    stages = ("x",) + after[:-1]
    for tick in range(count + 7):
        for before, (stage, following) in enumerate(zip(stages, after)):
            k = tick - before
            if not 0 <= k < count:
                continue
            ops[stage, k].wait_recv()
            if stage == "x":
                ops["load", k].wait()
                add(k, 0, EDGE, from_x, acc)
            elif stage == "y":
                add(k, y0, half, from_y, acc)
            elif stage == "low":
                add(k, l0, quarter, from_low, acc)
            elif stage == "high":
                add(k, h0, eighth, from_high, res)
            if following:
                ops[following, k].start()
            if stage == "all_y":
                ops["store", k].start()
        if tick < 5:
            vec_ops[tick].wait_recv()
            vec_acc[tick + 1] = vec_acc[tick] + vec_in[tick]
            if tick < 4:
                vec_ops[tick + 1].start()
    vec_store = pltpu.make_async_copy(vec_acc.at[5], vec_ref, vec_local.at[1])
    vec_store.start()
    vec_store.wait()
    for op in vec_ops:
        op.wait_send()
    for k in range(count):
        for stage in stages:
            ops[stage, k].wait_send()
        ops["store", k].wait()


def reduce(*args):
    bf16, f32 = jnp.bfloat16, jnp.float32
    shape = jax.ShapeDtypeStruct
    vec = args[-1]
    count = 12
    square = shape((EDGE, 2 * EDGE), bf16)
    return pl.pallas_call(
        reduce_kernel,
        in_specs=[ANY] * len(args),
        out_specs=[ANY] * 7,
        out_shape=[
            shape((4 * EDGE, 2 * EDGE), bf16),
            shape((EDGE, 8 * EDGE), bf16),
            square,
            square,
            square,
            square,
            shape(vec.shape, f32),
        ],
        scratch_shapes=[
            pltpu.VMEM((count, EDGE, EDGE), bf16),
            pltpu.VMEM((count, EDGE, EDGE), bf16),
            pltpu.VMEM((count, EDGE // 2, EDGE), bf16),
            pltpu.VMEM((count, EDGE // 4, EDGE), bf16),
            pltpu.VMEM((count, EDGE // 8, EDGE), bf16),
            pltpu.VMEM((count, EDGE, EDGE), bf16),
            pltpu.VMEM((6,) + vec.shape, f32),
            pltpu.VMEM((5,) + vec.shape, f32),
            pltpu.SemaphoreType.DMA((8, count)),
            pltpu.SemaphoreType.DMA((8, count)),
            pltpu.SemaphoreType.DMA((count,)),
            pltpu.SemaphoreType.DMA((count,)),
            pltpu.SemaphoreType.DMA((5,)),
            pltpu.SemaphoreType.DMA((5,)),
            pltpu.SemaphoreType.DMA((2,)),
        ],
        compiler_params=pltpu.CompilerParams(
            collective_id=1, has_side_effects=True, vmem_limit_bytes=56 * 1024 * 1024
        ),
        name="reduce",
    )(*args)


def attend_kernel(q_ref, k_ref, v_ref, mixed_ref, total_ref):
    f32, bf16 = jnp.float32, jnp.bfloat16
    rows, lanes = q_ref.shape
    lane = lax.broadcasted_iota(jnp.int32, (1, lanes), 1)
    keys = k_ref[...]
    values_t = v_ref[...].T
    for block in range(rows // Q_BLOCK):
        part = pl.ds(block * Q_BLOCK, Q_BLOCK)
        queries = q_ref[part, :] * jnp.asarray(0.125, bf16)
        outs = []
        for head in range(2):
            own = (lane // HDIM) == head
            scores = lax.dot_general(
                keys,
                jnp.where(own, queries, jnp.zeros_like(queries)),
                (((1,), (1,)), ((), ())),
                preferred_element_type=f32,
            )
            largest = jnp.max(scores, axis=0, keepdims=True)
            weights = jnp.exp(scores - largest)
            total = jnp.sum(weights, axis=0, keepdims=True)
            mixed = jnp.dot(
                values_t[head * HDIM : (head + 1) * HDIM, :],
                weights.astype(bf16),
                preferred_element_type=f32,
            )
            outs.append(mixed / total)
            total_ref[head, :, part] = largest + jnp.log(total)
        mixed_ref[part, :] = jnp.concatenate(outs, axis=0).T.astype(bf16)


def attend_back_kernel(q_ref, k_ref, v_ref, total_ref, grad_ref, dq_ref, dk_ref, dv_ref, dk_acc, dv_acc):
    f32, bf16 = jnp.float32, jnp.bfloat16
    rows, lanes = q_ref.shape
    lane = lax.broadcasted_iota(jnp.int32, (1, lanes), 1)
    keys = k_ref[...]
    keys_t = keys.T
    values = v_ref[...]
    nt = (((1,), (1,)), ((), ()))
    for block in range(rows // Q_BLOCK):
        part = pl.ds(block * Q_BLOCK, Q_BLOCK)
        queries = q_ref[part, :] * jnp.asarray(0.125, bf16)
        grads = grad_ref[part, :]
        outs = []
        key_part = None
        value_part = None
        for head in range(2):
            own = (lane // HDIM) == head
            q_own = jnp.where(own, queries, jnp.zeros_like(queries))
            g_own = jnp.where(own, grads, jnp.zeros_like(grads))
            scores = lax.dot_general(keys, q_own, nt, preferred_element_type=f32)
            probs = jnp.exp(scores - total_ref[head, :, part])
            grad_probs = lax.dot_general(values, g_own, nt, preferred_element_type=f32)
            delta = jnp.sum(probs * grad_probs, axis=0, keepdims=True)
            grad_scores = (probs * (grad_probs - delta)).astype(bf16)
            one_value = jnp.dot(probs.astype(bf16), g_own, preferred_element_type=f32)
            one_key = jnp.dot(grad_scores, q_own, preferred_element_type=f32)
            value_part = one_value if head == 0 else value_part + one_value
            key_part = one_key if head == 0 else key_part + one_key
            outs.append(
                jnp.dot(
                    keys_t[head * HDIM : (head + 1) * HDIM, :],
                    grad_scores,
                    preferred_element_type=f32,
                )
            )
        dq_ref[part, :] = (jnp.concatenate(outs, axis=0) * 0.125).T.astype(bf16)
        if block == 0:
            dk_acc[...] = key_part
            dv_acc[...] = value_part
        else:
            dk_acc[...] += key_part
            dv_acc[...] += value_part
    dk_ref[...] = dk_acc[...].astype(bf16)
    dv_ref[...] = dv_acc[...].astype(bf16)


def attend(qkv):
    rows, width = qkv.shape[0], qkv.shape[1] // 3
    pairs = width // 128
    macs = 2 * rows * rows * width
    return pl.pallas_call(
        attend_kernel,
        grid=(pairs,),
        in_specs=[
            pl.BlockSpec((rows, 128), lambda p: (0, p)),
            pl.BlockSpec((rows, 128), lambda p: (0, pairs + p)),
            pl.BlockSpec((rows, 128), lambda p: (0, 2 * pairs + p)),
        ],
        out_specs=[
            pl.BlockSpec((rows, 128), lambda p: (0, p)),
            pl.BlockSpec((2, 1, rows), lambda p: (p, 0, 0)),
        ],
        out_shape=[
            jax.ShapeDtypeStruct((rows, width), jnp.bfloat16),
            jax.ShapeDtypeStruct((2 * pairs, 1, rows), jnp.float32),
        ],
        compiler_params=pltpu.CompilerParams(vmem_limit_bytes=VMEM),
        cost_estimate=pl.CostEstimate(
            flops=8 * macs, bytes_accessed=8 * rows * width, transcendentals=macs // 128
        ),
        name="attend",
    )(qkv, qkv, qkv)


def attend_back(qkv, total, grad_mixed):
    rows, width = grad_mixed.shape
    pairs = width // 128
    macs = 5 * rows * rows * width
    block = pl.BlockSpec((rows, 128), lambda p: (0, p))
    return pl.pallas_call(
        attend_back_kernel,
        grid=(pairs,),
        in_specs=[
            block,
            pl.BlockSpec((rows, 128), lambda p: (0, pairs + p)),
            pl.BlockSpec((rows, 128), lambda p: (0, 2 * pairs + p)),
            pl.BlockSpec((2, 1, rows), lambda p: (p, 0, 0)),
            block,
        ],
        out_specs=[block] * 3,
        out_shape=[jax.ShapeDtypeStruct((rows, width), jnp.bfloat16)] * 3,
        scratch_shapes=[pltpu.VMEM((rows, 128), jnp.float32)] * 2,
        compiler_params=pltpu.CompilerParams(vmem_limit_bytes=VMEM),
        cost_estimate=pl.CostEstimate(
            flops=8 * macs, bytes_accessed=14 * rows * width, transcendentals=macs // 320
        ),
        name="attend_back",
    )(qkv, qkv, qkv, total, grad_mixed)


def tuned(
    tokens,
    out_grad,
    query_counts,
    first_gain,
    first_bias,
    query_weight,
    query_bias,
    key_weight,
    value_weight,
    value_bias,
    output_weight,
    output_bias,
    second_gain,
    second_bias,
    up_weight,
    up_bias,
    down_weight,
    down_bias,
):
    f32, bf16 = jnp.float32, jnp.bfloat16
    x = lax.axis_index("seq")
    core = lax.axis_index("cell") % 2
    swapped = x != core
    rows, width = tokens.shape[1:]
    hidden_width = up_weight.shape[1] // 2
    head_width = width // 2

    vectors = (first_gain, first_bias, query_bias, value_bias, output_bias, second_gain, second_bias, down_bias)
    vectors = jnp.stack(vectors)
    vectors = jnp.pad(vectors, ((0, 15 - vectors.shape[0]), (0, hidden_width - vectors.shape[1])))
    vectors = jnp.concatenate([vectors, up_bias[None]])
    cell_weight = jnp.broadcast_to(jnp.sqrt(query_counts.astype(f32) / 1000.0), (8, 128))
    own, own_grad, cell_weight, vectors, qkv_weight, out_weight, up_all, down_all = gather(
        tokens[0],
        out_grad[0],
        cell_weight,
        vectors,
        query_weight,
        key_weight,
        value_weight,
        output_weight,
        up_weight,
        down_weight,
    )
    weight_cell = cell_weight[:1, :1]
    vectors = vectors.astype(f32)
    short = [vectors[:, i, :head_width].reshape(-1) for i in range(8)]
    gain_one, bias_one, q_bias, v_bias, o_bias, gain_two, bias_two, d_bias = short
    u_bias = vectors[:, 15].reshape(-1)

    own = own.astype(f32)
    standard_one, inverse_one = standardize(own)
    normed_own = (standard_one * gain_one + bias_one).astype(bf16)
    normed_one = jnp.concatenate([normed_own, across(normed_own, CORE_BIT)])
    qkv_bias = jnp.concatenate(
        [half_of(q_bias, core), jnp.zeros((head_width,), f32), half_of(v_bias, core)]
    )
    qkv = (matmul(normed_one, qkv_weight) + qkv_bias).astype(bf16)
    mixed_heads, log_total = attend(qkv)
    other_heads = across(mixed_heads, CORE_BIT)
    other_heads = jnp.concatenate([other_heads[rows:], other_heads[:rows]])
    mixed = in_order(core == 0, mixed_heads, other_heads, axis=1)
    middle = own + matmul(mixed[:rows], out_weight) + o_bias
    standard_two, inverse_two = standardize(middle)
    normed_own = (standard_two * gain_two + bias_two).astype(bf16)
    normed_two = jnp.concatenate([normed_own, across(normed_own, CORE_BIT)])
    up_bias_own = lax.dynamic_index_in_dim(u_bias.reshape(2, 2, -1), core, 1, keepdims=False).reshape(-1)
    up_proj = matmul(normed_two, up_all) + up_bias_own
    hidden = gelu_value(up_proj).astype(bf16)

    grad_result = own_grad.astype(f32) * weight_cell
    grad_own = grad_result.astype(bf16)
    grad_ffn = jnp.concatenate([grad_own, across(grad_own, CORE_BIT)])

    def weight_sum(left, right):
        give = weight_grad(half_of(left, 1 - x, 1), right).astype(bf16)
        keep = weight_grad(half_of(left, x, 1), right).astype(bf16)
        return give, keep

    sum_down = weight_sum(hidden, grad_ffn)
    grad_up = (matmul_right_t(grad_ffn, down_all) * gelu_slope(up_proj)).astype(bf16)
    sum_up = weight_sum(normed_two, grad_up)
    partial = matmul_right_t(grad_up, up_all)
    grad_normed_two = partial[:rows] + across(partial[rows:].astype(bf16), CORE_BIT).astype(f32)
    grad_middle = grad_result + standardize_back(grad_normed_two, standard_two, inverse_two, gain_two)
    grad_attn_own = grad_middle.astype(bf16)
    grad_attn = jnp.concatenate([grad_attn_own, across(grad_attn_own, CORE_BIT)])
    sum_out = weight_sum(mixed, half_of(grad_attn, core, 1))

    partial = matmul(hidden, down_all)
    result = middle + partial[:rows] + across(partial[rows:].astype(bf16), CORE_BIT).astype(f32) + d_bias
    result = result.astype(bf16)
    result = jnp.where(swapped, across_diagonal(result), result)

    grad_mixed = matmul_right_t(grad_attn, half_of(out_weight, core)).astype(bf16)
    grad_qkv = jnp.concatenate(attend_back(qkv, log_total, grad_mixed), axis=1)
    sum_qkv = weight_sum(normed_one, grad_qkv)
    partial = matmul_right_t(grad_qkv, qkv_weight)
    grad_normed_one = partial[:rows] + across(partial[rows:].astype(bf16), CORE_BIT).astype(f32)
    input_grad = grad_middle + standardize_back(grad_normed_one, standard_one, inverse_one, gain_one)
    input_grad = input_grad.astype(bf16)
    input_grad = jnp.where(swapped, across_diagonal(input_grad), input_grad)

    def at_core(value):
        zero = jnp.zeros_like(value)
        return jnp.concatenate([jnp.where(core == 0, value, zero), jnp.where(core == 0, zero, value)], axis=-1)

    qkv_sum = column_sum(grad_qkv).reshape(3, head_width)
    up_sum = at_core(column_sum(grad_up).reshape(2, 1, -1)).reshape(-1)
    sums = [
        jnp.sum(grad_normed_one * standard_one, axis=0),
        jnp.sum(grad_normed_one, axis=0),
        at_core(qkv_sum[0]),
        at_core(qkv_sum[2]),
        column_sum(grad_attn_own),
        jnp.sum(grad_normed_two * standard_two, axis=0),
        jnp.sum(grad_normed_two, axis=0),
        column_sum(grad_own),
        up_sum,
    ]
    sizes = [value.shape[0] for value in sums]
    packed = jnp.concatenate(sums)
    packed = jnp.pad(packed, (0, -packed.shape[0] % 8192)).reshape(-1, 1024)
    down_sum, up_sum, out_sum, *qkv_sum, packed = reduce(*sum_down, *sum_up, *sum_out, *sum_qkv, packed)
    packed = packed.reshape(-1)
    sums = []
    for size in sizes:
        sums.append(half_of(packed[:size], x))
        packed = packed[size:]
    s_gain_one, s_bias_one, s_q_bias, s_v_bias, s_o_bias, s_gain_two, s_bias_two, s_d_bias, s_u_bias = sums

    return (
        result[None],
        input_grad[None],
        s_gain_one,
        s_bias_one,
        qkv_sum[0].astype(f32),
        s_q_bias,
        qkv_sum[1].astype(f32),
        qkv_sum[2].astype(f32),
        s_v_bias,
        out_sum.astype(f32),
        s_o_bias,
        s_gain_two,
        s_bias_two,
        up_sum.astype(f32),
        s_u_bias,
        down_sum.astype(f32),
        s_d_bias,
    )


def chosen(mesh):
    cells, blocks = mesh.shape["cell"], mesh.shape["seq"]

    def per_device(tokens, *rest):
        if blocks == 2 and cells == 16 and tokens.shape == (1, 512, 1280):
            return tuned(tokens, *rest)
        return general(tokens, *rest)

    return per_device


def solution(mesh):
    placed = (
        P("cell", "seq", None),
        P("cell", "seq", None),
        P("cell"),
        P("seq"),
        P("seq"),
        P("seq", None),
        P("seq"),
        P("seq", None),
        P("seq", None),
        P("seq"),
        P("seq", None),
        P("seq"),
        P("seq"),
        P("seq"),
        P("seq", None),
        P("seq"),
        P("seq", None),
        P("seq"),
    )
    return jax.shard_map(
        chosen(mesh),
        mesh=mesh,
        in_specs=placed,
        out_specs=(
            P("cell", "seq", None),
            P("cell", "seq", None),
            P("seq"),
            P("seq"),
            P("seq", None),
            P("seq"),
            P("seq", None),
            P("seq", None),
            P("seq"),
            P("seq", None),
            P("seq"),
            P("seq"),
            P("seq"),
            P("seq", None),
            P("seq"),
            P("seq", None),
            P("seq"),
        ),
        check_vma=False,
    )
```

```python
import jax
import jax.numpy as jnp
from jax import lax
from jax.experimental import pallas as pl
from jax.experimental.pallas import tpu as pltpu
from jax.sharding import PartitionSpec as P

HEADS = 20
HDIM = 64


def from_behind(value, axis, steps):
    count = lax.axis_size(axis)
    pairs = [(source, (source + steps) % count) for source in range(count)]
    return lax.ppermute(value, axis, pairs)


def for_sending(x):
    return jax.tree.map(lambda a: a.astype(jnp.bfloat16) if a.dtype == jnp.float32 else a, x)


def matmul(left, right):
    return jnp.dot(left, right, preferred_element_type=jnp.float32)


def matmul_right_t(left, right):
    return jnp.einsum("to,io->ti", left, right, preferred_element_type=jnp.float32)


def weight_grad(left, right):
    return jnp.einsum("ti,to->io", left, right, preferred_element_type=jnp.float32)


def standardize(values):
    average = jnp.mean(values, axis=-1, keepdims=True)
    centred = values - average
    inverse = lax.rsqrt(jnp.mean(centred * centred, axis=-1, keepdims=True) + 1e-05)
    return (centred * inverse, inverse)


def standardize_back(grad_normed, standard, inverse, gain_vec):
    scaled = grad_normed * gain_vec
    return inverse * (
        scaled
        - jnp.mean(scaled, axis=-1, keepdims=True)
        - standard * jnp.mean(scaled * standard, axis=-1, keepdims=True)
    )


def gelu_value(up_proj):
    return 0.5 * up_proj * (1.0 + lax.erf(up_proj * 0.7071067811865476))


def gelu_slope(up_proj):
    return (
        0.5 * (1.0 + lax.erf(up_proj * 0.7071067811865476))
        + up_proj * jnp.exp(-0.5 * up_proj * up_proj) * 0.3989422804014327
    )


def score_block(queries, key_rows):
    return (
        jnp.einsum("cqhd,ckhd->chqk", queries, key_rows, preferred_element_type=jnp.float32) * 0.125
    )


def column_sum(values):
    return jnp.sum(values.astype(jnp.float32), axis=0)


def general(
    tokens,
    out_grad,
    query_counts,
    first_gain,
    first_bias,
    query_weight,
    query_bias,
    key_weight,
    value_weight,
    value_bias,
    output_weight,
    output_bias,
    second_gain,
    second_bias,
    up_weight,
    up_bias,
    down_weight,
    down_bias,
):
    (
        first_gain,
        first_bias,
        query_weight,
        query_bias,
        key_weight,
        value_weight,
        value_bias,
        output_weight,
        output_bias,
        second_gain,
        second_bias,
        up_weight,
        up_bias,
        down_weight,
        down_bias,
    ) = (
        lax.all_gather(first_gain, "seq", axis=0, tiled=True),
        lax.all_gather(first_bias, "seq", axis=0, tiled=True),
        lax.all_gather(query_weight, "seq", axis=0, tiled=True),
        lax.all_gather(query_bias, "seq", axis=0, tiled=True),
        lax.all_gather(key_weight, "seq", axis=0, tiled=True),
        lax.all_gather(value_weight, "seq", axis=0, tiled=True),
        lax.all_gather(value_bias, "seq", axis=0, tiled=True),
        lax.all_gather(output_weight, "seq", axis=0, tiled=True),
        lax.all_gather(output_bias, "seq", axis=0, tiled=True),
        lax.all_gather(second_gain, "seq", axis=0, tiled=True),
        lax.all_gather(second_bias, "seq", axis=0, tiled=True),
        lax.all_gather(up_weight, "seq", axis=0, tiled=True),
        lax.all_gather(up_bias, "seq", axis=0, tiled=True),
        lax.all_gather(down_weight, "seq", axis=0, tiled=True),
        lax.all_gather(down_bias, "seq", axis=0, tiled=True),
    )
    f32 = jnp.float32
    bf16 = jnp.bfloat16
    gain_first = first_gain.astype(f32)
    gain_second = second_gain.astype(f32)
    cell_count, seg_len, model_width = tokens.shape
    row_count = cell_count * seg_len
    head_shape = (cell_count, seg_len, HEADS, HDIM)
    cycle_size = lax.axis_size("seq")
    flat_input = tokens.reshape(row_count, model_width).astype(f32)
    standard_one, inverse_one = standardize(flat_input)
    normed_one = (standard_one * gain_first + first_bias.astype(f32)).astype(bf16)
    query_heads = (
        (matmul(normed_one, query_weight) + query_bias.astype(f32)).astype(bf16).reshape(head_shape)
    )
    key_heads = matmul(normed_one, key_weight).astype(bf16).reshape(head_shape)
    value_heads = (
        (matmul(normed_one, value_weight) + value_bias.astype(f32)).astype(bf16).reshape(head_shape)
    )
    running_max = jnp.full((cell_count, HEADS, seg_len), -1e30, f32)
    running_sum = jnp.zeros((cell_count, HEADS, seg_len), f32)
    weighted = jnp.zeros((cell_count, HEADS, seg_len, HDIM), f32)
    travel = (key_heads, value_heads)
    for step in range(cycle_size):
        if step > 0:
            travel = from_behind((travel[0], travel[1]), "seq", 1)
        scores = score_block(query_heads, travel[0])
        new_max = jnp.maximum(running_max, jnp.max(scores, axis=-1))
        rescale = jnp.exp(running_max - new_max)
        exp_scores = jnp.exp(scores - new_max[..., None])
        running_sum = running_sum * rescale + jnp.sum(exp_scores, axis=-1)
        weighted = weighted * rescale[..., None] + jnp.einsum(
            "chqk,ckhd->chqd", exp_scores.astype(bf16), travel[1], preferred_element_type=f32
        )
        running_max = new_max
    attended = weighted / running_sum[..., None]
    log_total = running_max + jnp.log(running_sum)
    mixed = attended.transpose(0, 2, 1, 3).reshape(row_count, model_width).astype(bf16)
    middle = flat_input + matmul(mixed, output_weight) + output_bias.astype(f32)
    standard_two, inverse_two = standardize(middle)
    normed_two = (standard_two * gain_second + second_bias.astype(f32)).astype(bf16)
    up_proj = matmul(normed_two, up_weight) + up_bias.astype(f32)
    hidden = gelu_value(up_proj).astype(bf16)
    result = middle + matmul(hidden, down_weight) + down_bias.astype(f32)
    result_out = result.astype(bf16).reshape(cell_count, seg_len, model_width)
    weight_cell = jnp.sqrt(query_counts.astype(f32) / 1000.0)
    grad_result = (out_grad.astype(f32) * weight_cell[:, None, None]).reshape(
        row_count, model_width
    )
    grad_ffn_out = grad_result.astype(bf16)
    grad_down_weight = weight_grad(hidden, grad_ffn_out)
    grad_down_bias = column_sum(grad_ffn_out)
    grad_up = (matmul_right_t(grad_ffn_out, down_weight) * gelu_slope(up_proj)).astype(bf16)
    grad_up_weight = weight_grad(normed_two, grad_up)
    grad_up_bias = column_sum(grad_up)
    grad_normed_two = matmul_right_t(grad_up, up_weight)
    grad_second_gain = jnp.sum(grad_normed_two * standard_two, axis=0)
    grad_second_bias = jnp.sum(grad_normed_two, axis=0)
    grad_middle = grad_result + standardize_back(
        grad_normed_two, standard_two, inverse_two, gain_second
    )
    grad_attn_out = grad_middle.astype(bf16)
    grad_output_weight = weight_grad(mixed, grad_attn_out)
    grad_output_bias = column_sum(grad_attn_out)
    grad_mixed = matmul_right_t(grad_attn_out, output_weight).astype(bf16).reshape(head_shape)
    row_delta = jnp.sum(grad_mixed.astype(f32).transpose(0, 2, 1, 3) * attended, axis=-1)
    grad_query_acc = jnp.zeros(head_shape, f32)
    moving = (jnp.zeros(head_shape, f32), jnp.zeros(head_shape, f32))
    travel = (key_heads, value_heads)
    for step in range(cycle_size):
        if step > 0:
            travel = from_behind((travel[0], travel[1]), "seq", 1)
        block_keys, block_values = travel
        scores = score_block(query_heads, block_keys)
        prob_block = jnp.exp(scores - log_total[..., None])
        part_values = jnp.einsum(
            "chqk,cqhd->ckhd", prob_block.astype(bf16), grad_mixed, preferred_element_type=f32
        )
        grad_probs = jnp.einsum(
            "cqhd,ckhd->chqk", grad_mixed, block_values, preferred_element_type=f32
        )
        grad_scores = (prob_block * (grad_probs - row_delta[..., None])).astype(bf16)
        grad_query_acc = (
            grad_query_acc
            + jnp.einsum("chqk,ckhd->cqhd", grad_scores, block_keys, preferred_element_type=f32)
            * 0.125
        )
        part_keys = (
            jnp.einsum("chqk,cqhd->ckhd", grad_scores, query_heads, preferred_element_type=f32)
            * 0.125
        )
        moving = from_behind(
            (for_sending(moving[0] + part_keys), for_sending(moving[1] + part_values)), "seq", 1
        )
    grad_queries = grad_query_acc.astype(bf16).reshape(row_count, model_width)
    grad_keys = moving[0].astype(bf16).reshape(row_count, model_width)
    grad_values = moving[1].astype(bf16).reshape(row_count, model_width)
    grad_query_weight = weight_grad(normed_one, grad_queries)
    grad_query_bias = column_sum(grad_queries)
    grad_key_weight = weight_grad(normed_one, grad_keys)
    grad_value_weight = weight_grad(normed_one, grad_values)
    grad_value_bias = column_sum(grad_values)
    grad_normed_one = (
        matmul_right_t(grad_queries, query_weight)
        + matmul_right_t(grad_keys, key_weight)
        + matmul_right_t(grad_values, value_weight)
    )
    grad_first_gain = jnp.sum(grad_normed_one * standard_one, axis=0)
    grad_first_bias = jnp.sum(grad_normed_one, axis=0)
    grad_input = grad_middle + standardize_back(
        grad_normed_one, standard_one, inverse_one, gain_first
    )
    input_grad = grad_input.astype(bf16).reshape(cell_count, seg_len, model_width)
    shared_all = (
        lax.psum_scatter(
            grad_first_gain.astype(jnp.bfloat16), "seq", scatter_dimension=0, tiled=True
        ).astype(jnp.float32),
        lax.psum_scatter(
            grad_first_bias.astype(jnp.bfloat16), "seq", scatter_dimension=0, tiled=True
        ).astype(jnp.float32),
        lax.psum_scatter(
            grad_query_weight.astype(jnp.bfloat16), "seq", scatter_dimension=0, tiled=True
        ).astype(jnp.float32),
        lax.psum_scatter(
            grad_query_bias.astype(jnp.bfloat16), "seq", scatter_dimension=0, tiled=True
        ).astype(jnp.float32),
        lax.psum_scatter(
            grad_key_weight.astype(jnp.bfloat16), "seq", scatter_dimension=0, tiled=True
        ).astype(jnp.float32),
        lax.psum_scatter(
            grad_value_weight.astype(jnp.bfloat16), "seq", scatter_dimension=0, tiled=True
        ).astype(jnp.float32),
        lax.psum_scatter(
            grad_value_bias.astype(jnp.bfloat16), "seq", scatter_dimension=0, tiled=True
        ).astype(jnp.float32),
        lax.psum_scatter(
            grad_output_weight.astype(jnp.bfloat16), "seq", scatter_dimension=0, tiled=True
        ).astype(jnp.float32),
        lax.psum_scatter(
            grad_output_bias.astype(jnp.bfloat16), "seq", scatter_dimension=0, tiled=True
        ).astype(jnp.float32),
        lax.psum_scatter(
            grad_second_gain.astype(jnp.bfloat16), "seq", scatter_dimension=0, tiled=True
        ).astype(jnp.float32),
        lax.psum_scatter(
            grad_second_bias.astype(jnp.bfloat16), "seq", scatter_dimension=0, tiled=True
        ).astype(jnp.float32),
        lax.psum_scatter(
            grad_up_weight.astype(jnp.bfloat16), "seq", scatter_dimension=0, tiled=True
        ).astype(jnp.float32),
        lax.psum_scatter(
            grad_up_bias.astype(jnp.bfloat16), "seq", scatter_dimension=0, tiled=True
        ).astype(jnp.float32),
        lax.psum_scatter(
            grad_down_weight.astype(jnp.bfloat16), "seq", scatter_dimension=0, tiled=True
        ).astype(jnp.float32),
        lax.psum_scatter(
            grad_down_bias.astype(jnp.bfloat16), "seq", scatter_dimension=0, tiled=True
        ).astype(jnp.float32),
    )
    (
        grad_first_gain,
        grad_first_bias,
        grad_query_weight,
        grad_query_bias,
        grad_key_weight,
        grad_value_weight,
        grad_value_bias,
        grad_output_weight,
        grad_output_bias,
        grad_second_gain,
        grad_second_bias,
        grad_up_weight,
        grad_up_bias,
        grad_down_weight,
        grad_down_bias,
    ) = shared_all
    (
        grad_first_gain,
        grad_first_bias,
        grad_query_weight,
        grad_query_bias,
        grad_key_weight,
        grad_value_weight,
        grad_value_bias,
        grad_output_weight,
        grad_output_bias,
        grad_second_gain,
        grad_second_bias,
        grad_up_weight,
        grad_up_bias,
        grad_down_weight,
        grad_down_bias,
    ) = (
        lax.psum(grad_first_gain.astype(jnp.bfloat16), "cell").astype(jnp.float32),
        lax.psum(grad_first_bias.astype(jnp.bfloat16), "cell").astype(jnp.float32),
        lax.psum(grad_query_weight.astype(jnp.bfloat16), "cell").astype(jnp.float32),
        lax.psum(grad_query_bias.astype(jnp.bfloat16), "cell").astype(jnp.float32),
        lax.psum(grad_key_weight.astype(jnp.bfloat16), "cell").astype(jnp.float32),
        lax.psum(grad_value_weight.astype(jnp.bfloat16), "cell").astype(jnp.float32),
        lax.psum(grad_value_bias.astype(jnp.bfloat16), "cell").astype(jnp.float32),
        lax.psum(grad_output_weight.astype(jnp.bfloat16), "cell").astype(jnp.float32),
        lax.psum(grad_output_bias.astype(jnp.bfloat16), "cell").astype(jnp.float32),
        lax.psum(grad_second_gain.astype(jnp.bfloat16), "cell").astype(jnp.float32),
        lax.psum(grad_second_bias.astype(jnp.bfloat16), "cell").astype(jnp.float32),
        lax.psum(grad_up_weight.astype(jnp.bfloat16), "cell").astype(jnp.float32),
        lax.psum(grad_up_bias.astype(jnp.bfloat16), "cell").astype(jnp.float32),
        lax.psum(grad_down_weight.astype(jnp.bfloat16), "cell").astype(jnp.float32),
        lax.psum(grad_down_bias.astype(jnp.bfloat16), "cell").astype(jnp.float32),
    )
    return (
        result_out,
        input_grad,
        grad_first_gain,
        grad_first_bias,
        grad_query_weight,
        grad_query_bias,
        grad_key_weight,
        grad_value_weight,
        grad_value_bias,
        grad_output_weight,
        grad_output_bias,
        grad_second_gain,
        grad_second_bias,
        grad_up_weight,
        grad_up_bias,
        grad_down_weight,
        grad_down_bias,
    )


BOTH = ("cell", "seq")
CORE_BIT = 2
Q_BLOCK = 512
VMEM = 48 * 1024 * 1024


def across(value, bit):
    count = lax.axis_size("cell") * lax.axis_size("seq")
    return lax.ppermute(value, BOTH, [(i, i ^ bit) for i in range(count)])


def across_diagonal(value):
    count = lax.axis_size("cell") * lax.axis_size("seq")
    pairs = [(i, i ^ 3) for i in range(count) if (i & 3) in (1, 2)]
    return lax.ppermute(value, BOTH, pairs)


def in_order(first, own, received, axis=0):
    low = jnp.where(first, own, received)
    high = jnp.where(first, received, own)
    return jnp.concatenate([low, high], axis=axis)


def half_of(value, index, axis=0):
    size = value.shape[axis] // 2
    return lax.dynamic_slice_in_dim(value, index * size, size, axis)


MESH = pl.DeviceIdType.MESH
ANY = pl.BlockSpec(memory_space=pl.ANY)
EDGE = 640


class Spot:
    def __init__(self):
        self.x = lax.axis_index("seq")
        self.cell = lax.axis_index("cell")
        self.core = lax.rem(self.cell, 2)
        self.y = lax.rem(self.cell // 2, 2)
        self.low = lax.rem(self.cell // 4, 2)
        self.high = lax.rem(self.cell // 8, 2)

    def flip(self, index, bit):
        return {"cell": self.cell + bit - 2 * bit * index}

    def over(self, name):
        if name == "x":
            return {"seq": 1 - self.x}
        if name == "core":
            return self.flip(self.core, 1)
        if name == "diagonal":
            return {"seq": 1 - self.x, **self.flip(self.core, 1)}
        return self.flip(*{"y": (self.y, 2), "low": (self.low, 4), "high": (self.high, 8)}[name])

    def meet(self, names):
        barrier = pltpu.get_barrier_semaphore()
        for name in names:
            pl.semaphore_signal(barrier, inc=1, device_id=self.over(name), device_id_type=MESH)
        pl.semaphore_wait(barrier, len(names))

    def send(self, name, source, target, send_sem, recv_sem):
        return pltpu.make_async_remote_copy(
            source, target, send_sem, recv_sem, device_id=self.over(name), device_id_type=MESH
        )


def rows_at(start, size):
    return pl.ds(pl.multiple_of(start, 16), size)


def cols(start, size):
    return pl.ds(pl.multiple_of(start, 128), size)


def attend_pair(qkv, mixed, total_ref, pair, base):
    f32, bf16 = jnp.float32, jnp.bfloat16
    rows = qkv.shape[0]
    lane = lax.broadcasted_iota(jnp.int32, (1, 128), 1)
    here = pair * 128
    keys = qkv[:, cols(EDGE + here, 128)]
    values_t = qkv[:, cols(2 * EDGE + here, 128)].T
    for block in range(rows // Q_BLOCK):
        part = pl.ds(block * Q_BLOCK, Q_BLOCK)
        queries = qkv[part, cols(here, 128)] * jnp.asarray(0.125, bf16)
        outs = []
        for head in range(2):
            own = (lane // HDIM) == head
            scores = lax.dot_general(
                keys,
                jnp.where(own, queries, jnp.zeros_like(queries)),
                (((1,), (1,)), ((), ())),
                preferred_element_type=f32,
            )
            largest = jnp.max(scores, axis=0, keepdims=True)
            weights = jnp.exp(scores - largest)
            total = jnp.sum(weights, axis=0, keepdims=True)
            out = jnp.dot(
                values_t[head * HDIM : (head + 1) * HDIM, :],
                weights.astype(bf16),
                preferred_element_type=f32,
            )
            outs.append(out / total)
            total_ref[2 * pair + head, :, part] = largest + jnp.log(total)
        mixed[part, cols(base + here, 128)] = jnp.concatenate(outs, axis=0).T.astype(bf16)


def forward_kernel(
    tokens, out_grad, cell_weight, vectors, wq, wk, wv, wo, wup, wdown,
    own_out, grad_out, weight_out, vectors_out, qkv_w_out, out_w_out, up_w_out, down_w_out,
    normed_one_out, qkv_out, mixed_out, total_out, middle_out, normed_two_out, hidden_out, slope_out, ffn_out,
    tok, grad, scale, vec, qkv_w, out_w, up_w, down_w,
    normed_one, qkv, mixed, totals, middle, normed_two, hidden, slope, ffn,
    send_sems, recv_sems, local_sems, side_send, side_recv, side_local, out_sems,
):
    f32, bf16 = jnp.float32, jnp.bfloat16
    at = Spot()
    x, core = at.x, at.core
    rows = tok.shape[0]
    width = tok.shape[1]
    at.meet(("x", "core", "diagonal", "y", "low", "high"))

    side = [(tokens, tok), (cell_weight, scale), (out_grad, grad)]
    diagonal = [at.send("diagonal", s, t, side_send.at[i], side_recv.at[i]) for i, (s, t) in enumerate(side)]
    straight = [pltpu.make_async_copy(s, t, side_local.at[i]) for i, (s, t) in enumerate(side)]

    def swap(i, remote, local):
        @pl.when(x != core)
        def _():
            remote(diagonal[i])

        @pl.when(x == core)
        def _():
            local(straight[i])

    def swap_start(i):
        swap(i, lambda c: c.start(), lambda c: c.start())

    def swap_wait(i):
        swap(i, lambda c: c.wait(), lambda c: c.wait())

    chunks = []
    for i, ref in enumerate((wq, wk, wv)):
        chunks.append((ref.at[:, cols(core * EDGE, EDGE)], qkv_w, EDGE, 0, i * EDGE))
    for i in range(4):
        start = (i // 2) * 4 * EDGE + core * 2 * EDGE + (i % 2) * EDGE
        chunks.append((wup.at[:, cols(start, EDGE)], up_w, EDGE, 0, i * EDGE))
    for i in range(4):
        source = wdown.at[rows_at(core * 2 * EDGE + (i // 2) * EDGE, EDGE), pl.ds((i % 2) * EDGE, EDGE)]
        chunks.append((source, down_w, 2 * EDGE, (i // 2) * EDGE, (i % 2) * EDGE))
    count = len(chunks)
    eighth = EDGE // 8
    place = at.y * 4 + at.low * 2 + at.high

    def region(k, half, start, size):
        _, ref, stride, row, column = chunks[k]
        return ref.at[rows_at(half * stride + row + start * eighth, size * eighth), pl.ds(column, EDGE)]

    ops = {}
    for k, chunk in enumerate(chunks):
        ops["x", k] = at.send(
            "x", chunk[0].at[rows_at(place * eighth, eighth)], region(k, x, place, 1), send_sems.at[0, k], recv_sems.at[0, k]
        )
        for s, (name, start, size) in enumerate(
            (("high", place, 1), ("low", at.y * 4 + at.low * 2, 2), ("y", at.y * 4, 4))
        ):
            part = region(k, 1 - x, start, size)
            ops[name, k] = at.send(name, part, part, send_sems.at[s + 1, k], recv_sems.at[s + 1, k])
        ops["local", k] = pltpu.make_async_copy(chunk[0], region(k, x, 0, 8), local_sems.at[k])
    half = EDGE // 2
    out_x = at.send(
        "x", wo.at[rows_at(core * half, half)], out_w.at[rows_at(x * EDGE + core * half, half)], side_send.at[4], side_recv.at[4]
    )
    part = out_w.at[rows_at((1 - x) * EDGE + core * half, half)]
    out_core = at.send("core", part, part, side_send.at[5], side_recv.at[5])
    out_local = pltpu.make_async_copy(wo, out_w.at[rows_at(x * EDGE, EDGE)], side_local.at[4])
    vec_x = at.send("x", vectors, vec.at[x], side_send.at[3], side_recv.at[3])
    vec_local = pltpu.make_async_copy(vectors, vec.at[x], side_local.at[3])
    top, bottom = pl.ds(0, rows), pl.ds(rows, rows)

    def core_copy(i, source, target):
        return at.send("core", source, target, side_send.at[i], side_recv.at[i])

    normed_one_core = core_copy(6, normed_one.at[top], normed_one.at[bottom])
    heads = cols(core * EDGE, EDGE)
    mixed_core = [
        core_copy(7, mixed.at[top, heads], mixed.at[bottom, heads]),
        core_copy(8, mixed.at[bottom, heads], mixed.at[top, heads]),
    ]
    normed_two_core = core_copy(9, normed_two.at[top], normed_two.at[bottom])
    ffn_core = core_copy(10, ffn.at[top], ffn.at[bottom])

    outs = []
    early = []

    def put(source, target):
        copy = pltpu.make_async_copy(source, target, out_sems.at[len(outs)])
        copy.start()
        outs.append(copy)
        return copy

    issue = {
        0: [ops["x", 3], ops["x", 4]],
        1: [ops["x", 5], ops["x", 6]],
        2: [out_x, out_local, ops["local", 3], ops["local", 4], ops["local", 5], ops["local", 6]],
        3: [ops["x", 7], ops["x", 8]],
        4: [ops["x", 9], ops["x", 10], ops["local", 7], ops["local", 8], ops["local", 9], ops["local", 10]],
    }

    def tick(t):
        for op in issue.get(t, ()):
            op.start()
        if t == 5:
            swap_start(2)
        for before, name, after in ((3, "y", None), (2, "low", "y"), (1, "high", "low"), (0, "x", "high")):
            k = t - before
            if 0 <= k < count:
                ops[name, k].wait_recv()
                if after:
                    ops[after, k].start()
        if t == 6:
            out_x.wait_recv()
            out_core.start()

    for k in range(3):
        ops["x", k].start()
    vec_x.start()
    swap_start(0)
    swap_start(1)
    vec_local.start()
    for k in range(3):
        ops["local", k].start()
    tick(0)
    tick(1)
    vec_x.wait_recv()
    vec_local.wait()

    def vector(i):
        return jnp.concatenate([vec[0, i : i + 1, :], vec[1, i : i + 1, :]], axis=1)

    def norm(values, gain, bias):
        average = jnp.mean(values, axis=-1, keepdims=True)
        centred = values - average
        inverse = lax.rsqrt(jnp.mean(centred * centred, axis=-1, keepdims=True) + 1e-05)
        return (centred * inverse * gain + bias).astype(bf16)

    swap_wait(0)
    gain_one, bias_one = vector(0), vector(1)

    @pl.loop(0, rows // 64)
    def _(i):
        here = rows_at(i * 64, 64)
        normed_one[here, :] = norm(tok[here, :].astype(f32), gain_one, bias_one)

    normed_one_core.start()
    tick(2)
    put(tok, own_out)
    normed_one_core.wait_recv()
    put(normed_one, normed_one_out)

    for i in range(3):
        tick(3 + i)
        ops["local", i].wait()
        lanes = pl.ds(i * EDGE, EDGE)
        bias = 0.0 if i == 1 else vec[core, 2 + i // 2 : 3 + i // 2, :]

        @pl.loop(0, 2 * rows // 256)
        def _(r):
            here = rows_at(r * 256, 256)
            value = jnp.dot(normed_one[here, :], qkv_w[:, lanes], preferred_element_type=f32)
            qkv[here, lanes] = (value + bias).astype(bf16)

    put(qkv, qkv_out)
    put(qkv_w, qkv_w_out)

    @pl.loop(0, EDGE // 128)
    def _(pair):
        attend_pair(qkv, mixed, totals, pair, core * EDGE)

        @pl.when(pair == 1)
        def _():
            tick(6)

        @pl.when(pair == 3)
        def _():
            tick(7)

    mixed_core[0].start()
    mixed_core[1].start()
    put(totals, total_out)
    tick(8)
    out_local.wait()
    out_core.wait_recv()
    mixed_core[1].wait_recv()
    gain_two, bias_two, out_bias = vector(5), vector(6), vector(4)

    @pl.loop(0, rows // 128)
    def _(r):
        here = rows_at(r * 128, 128)
        value = jnp.dot(mixed[here, :], out_w[...], preferred_element_type=f32)
        value = tok[here, :].astype(f32) + value + out_bias
        middle[here, :] = value
        normed_two[here, :] = norm(value, gain_two, bias_two)

    normed_two_core.start()
    mixed_core[0].wait_recv()
    put(out_w, out_w_out)
    put(mixed, mixed_out)
    put(middle, middle_out)
    tick(9)
    normed_two_core.wait_recv()
    put(normed_two, normed_two_out)
    waits = {}
    for i in range(4):
        ops["local", 3 + i].wait()
        slot = i % 2
        if i >= 2:
            for copy in waits[slot]:
                copy.wait()
                early.append(copy)
        lanes = pl.ds(i * EDGE, EDGE)
        bias = vec[i // 2, pl.ds(8 + core * 2 + i % 2, 1), :]

        @pl.loop(0, 2 * rows // 128)
        def _(r):
            here = rows_at(r * 128, 128)
            up = jnp.dot(normed_two[here, :], up_w[:, lanes], preferred_element_type=f32) + bias
            cdf = 0.5 * (1.0 + lax.erf(up * 0.7071067811865476))
            hidden[slot, here, :] = (up * cdf).astype(bf16)
            slope[slot, here, :] = (cdf + up * jnp.exp(-0.5 * up * up) * 0.3989422804014327).astype(bf16)

        waits[slot] = (
            put(hidden.at[slot], hidden_out.at[:, lanes]),
            put(slope.at[slot], slope_out.at[:, lanes]),
        )
        if i == 1:
            swap_wait(1)
            swap_wait(2)
            weight = scale[0:1, 0:1]

            @pl.loop(0, rows // 64)
            def _(r):
                here = rows_at(r * 64, 64)
                ffn[here, :] = (grad[here, :].astype(f32) * weight).astype(bf16)

            ffn_core.start()
            put(grad, grad_out)
            put(scale, weight_out)
            put(vec, vectors_out)
        tick(10 + i)
    put(up_w, up_w_out)
    ffn_core.wait_recv()
    put(ffn, ffn_out)
    for k in range(7, count):
        ops["local", k].wait()
    put(down_w, down_w_out)
    for k in range(count):
        for name in ("x", "high", "low", "y"):
            ops[name, k].wait_send()
    for op in (out_x, out_core, vec_x, normed_one_core, *mixed_core, normed_two_core, ffn_core):
        op.wait_send()
    for copy in outs:
        if not any(copy is other for other in early):
            copy.wait()


def forward(*args):
    bf16, f32 = jnp.bfloat16, jnp.float32
    shape = jax.ShapeDtypeStruct
    rows, width = args[0].shape
    both = 2 * rows
    arrays = [
        ((rows, width), bf16),
        ((rows, width), bf16),
        (args[2].shape, f32),
        ((2,) + args[3].shape, f32),
        ((width, 3 * EDGE), bf16),
        ((width, width), bf16),
        ((width, 4 * EDGE), bf16),
        ((4 * EDGE, width), bf16),
        ((both, width), bf16),
        ((both, 3 * EDGE), bf16),
        ((both, width), bf16),
        ((EDGE // HDIM, 1, both), f32),
        ((rows, width), f32),
        ((both, width), bf16),
        ((both, 4 * EDGE), bf16),
        ((both, 4 * EDGE), bf16),
        ((both, width), bf16),
    ]
    scratch = [pltpu.VMEM(*array) for array in arrays]
    scratch[14] = scratch[15] = pltpu.VMEM((2, both, EDGE), bf16)
    dma = pltpu.SemaphoreType.DMA
    return pl.pallas_call(
        forward_kernel,
        in_specs=[ANY] * len(args),
        out_specs=[ANY] * len(arrays),
        out_shape=[shape(*array) for array in arrays],
        scratch_shapes=scratch + [dma((4, 11)), dma((4, 11)), dma((11,)), dma((11,)), dma((11,)), dma((5,)), dma((24,))],
        compiler_params=pltpu.CompilerParams(
            collective_id=0, has_side_effects=True, vmem_limit_bytes=60 * 1024 * 1024
        ),
        name="forward",
    )(*args)


def reduce_kernel(
    give_down, keep_down, give_up, keep_up, give_out, keep_out, give_qkv, keep_qkv, vec,
    down_ref, up_ref, out_ref, q_ref, k_ref, v_ref, vec_ref,
    acc, from_x, from_y, from_low, from_high, res, vec_acc, vec_in,
    send_sems, recv_sems, load_sems, store_sems, vec_send, vec_recv, vec_local,
):
    f32, bf16 = jnp.float32, jnp.bfloat16
    at = Spot()
    core = at.core
    at.meet(("x", "core", "y", "low", "high"))
    chunks = []
    for i in range(4):
        part = (pl.ds((i // 2) * EDGE, EDGE), pl.ds((i % 2) * EDGE, EDGE))
        target = down_ref.at[rows_at(core * 2 * EDGE + (i // 2) * EDGE, EDGE), pl.ds((i % 2) * EDGE, EDGE)]
        chunks.append((give_down.at[part], keep_down.at[part], target))
    for i in range(4):
        part = (slice(None), pl.ds(i * EDGE, EDGE))
        target = up_ref.at[:, cols((i // 2) * 4 * EDGE + core * 2 * EDGE + (i % 2) * EDGE, EDGE)]
        chunks.append((give_up.at[part], keep_up.at[part], target))
    mine = cols(core * EDGE, EDGE)
    chunks.append((give_out, keep_out, out_ref.at[:, mine]))
    for i, ref in enumerate((q_ref, k_ref, v_ref)):
        part = (slice(None), pl.ds(i * EDGE, EDGE))
        chunks.append((give_qkv.at[part], keep_qkv.at[part], ref.at[:, mine]))
    count = len(chunks)

    half, quarter, eighth = EDGE // 2, EDGE // 4, EDGE // 8
    y0 = at.y * half
    l0 = y0 + at.low * quarter
    h0 = l0 + at.high * eighth
    ops = {}
    for k, (give, keep, target) in enumerate(chunks):
        hops = (
            ("x", "x", give, from_x.at[k]),
            ("y", "y", acc.at[k, rows_at((1 - at.y) * half, half)], from_y.at[k]),
            ("low", "low", acc.at[k, rows_at(y0 + (1 - at.low) * quarter, quarter)], from_low.at[k]),
            ("high", "high", acc.at[k, rows_at(l0 + (1 - at.high) * eighth, eighth)], from_high.at[k]),
            ("all_high", "high", res.at[k, rows_at(h0, eighth)], res.at[k, rows_at(h0, eighth)]),
            ("all_low", "low", res.at[k, rows_at(l0, quarter)], res.at[k, rows_at(l0, quarter)]),
            ("all_y", "y", res.at[k, rows_at(y0, half)], res.at[k, rows_at(y0, half)]),
            ("core", "core", res.at[k], target),
        )
        for s, (stage, name, source, goal) in enumerate(hops):
            ops[stage, k] = at.send(name, source, goal, send_sems.at[s, k], recv_sems.at[s, k])
        ops["load", k] = pltpu.make_async_copy(keep, acc.at[k], load_sems.at[k])
        ops["store", k] = pltpu.make_async_copy(res.at[k], target, store_sems.at[k])

    def add(k, start, size, other, goal):
        @pl.loop(0, size // 80)
        def _(i):
            here = rows_at(start + i * 80, 80)
            there = rows_at(i * 80, 80)
            goal[k, here, :] = (acc[k, here, :].astype(f32) + other[k, there, :].astype(f32)).astype(bf16)

    for k in range(2):
        ops["x", k].start()
        ops["load", k].start()
    vec_load = pltpu.make_async_copy(vec, vec_acc.at[0], vec_local.at[0])
    vec_load.start()
    vec_load.wait()
    vec_names = ("x", "core", "y", "low", "high")
    vec_ops = [
        at.send(name, vec_acc.at[i], vec_in.at[i], vec_send.at[i], vec_recv.at[i]) for i, name in enumerate(vec_names)
    ]
    vec_ops[0].start()
    after = ("y", "low", "high", "all_high", "all_low", "all_y", "core", None)
    stages = ("x",) + after[:-1]
    for tick in range(count + 7):
        for before, (stage, following) in reversed(list(enumerate(zip(stages, after)))):
            k = tick - before
            if not 0 <= k < count:
                continue
            ops[stage, k].wait_recv()
            if stage == "x":
                if k + 2 < count:
                    ops["x", k + 2].start()
                    ops["load", k + 2].start()
                ops["load", k].wait()
                add(k, 0, EDGE, from_x, acc)
            elif stage == "y":
                add(k, y0, half, from_y, acc)
            elif stage == "low":
                add(k, l0, quarter, from_low, acc)
            elif stage == "high":
                add(k, h0, eighth, from_high, res)
            if following:
                ops[following, k].start()
            if stage == "all_y":
                ops["store", k].start()
        if tick < 5:
            vec_ops[tick].wait_recv()
            vec_acc[tick + 1] = vec_acc[tick] + vec_in[tick]
            if tick < 4:
                vec_ops[tick + 1].start()
    vec_store = pltpu.make_async_copy(vec_acc.at[5], vec_ref, vec_local.at[1])
    vec_store.start()
    vec_store.wait()
    for op in vec_ops:
        op.wait_send()
    for k in range(count):
        for stage in stages:
            ops[stage, k].wait_send()
        ops["store", k].wait()


def reduce(*args):
    bf16, f32 = jnp.bfloat16, jnp.float32
    shape = jax.ShapeDtypeStruct
    vec = args[-1]
    count = 12
    square = shape((EDGE, 2 * EDGE), bf16)
    return pl.pallas_call(
        reduce_kernel,
        in_specs=[ANY] * len(args),
        out_specs=[ANY] * 7,
        out_shape=[
            shape((4 * EDGE, 2 * EDGE), bf16),
            shape((EDGE, 8 * EDGE), bf16),
            square,
            square,
            square,
            square,
            shape(vec.shape, f32),
        ],
        scratch_shapes=[
            pltpu.VMEM((count, EDGE, EDGE), bf16),
            pltpu.VMEM((count, EDGE, EDGE), bf16),
            pltpu.VMEM((count, EDGE // 2, EDGE), bf16),
            pltpu.VMEM((count, EDGE // 4, EDGE), bf16),
            pltpu.VMEM((count, EDGE // 8, EDGE), bf16),
            pltpu.VMEM((count, EDGE, EDGE), bf16),
            pltpu.VMEM((6,) + vec.shape, f32),
            pltpu.VMEM((5,) + vec.shape, f32),
            pltpu.SemaphoreType.DMA((8, count)),
            pltpu.SemaphoreType.DMA((8, count)),
            pltpu.SemaphoreType.DMA((count,)),
            pltpu.SemaphoreType.DMA((count,)),
            pltpu.SemaphoreType.DMA((5,)),
            pltpu.SemaphoreType.DMA((5,)),
            pltpu.SemaphoreType.DMA((2,)),
        ],
        compiler_params=pltpu.CompilerParams(
            collective_id=1, has_side_effects=True, vmem_limit_bytes=56 * 1024 * 1024
        ),
        name="reduce",
    )(*args)


def attend_back_kernel(q_ref, k_ref, v_ref, total_ref, grad_ref, dq_ref, dk_ref, dv_ref, dk_acc, dv_acc):
    f32, bf16 = jnp.float32, jnp.bfloat16
    rows, lanes = q_ref.shape
    lane = lax.broadcasted_iota(jnp.int32, (1, lanes), 1)
    keys = k_ref[...]
    keys_t = keys.T
    values = v_ref[...]
    nt = (((1,), (1,)), ((), ()))
    for block in range(rows // Q_BLOCK):
        part = pl.ds(block * Q_BLOCK, Q_BLOCK)
        queries = q_ref[part, :] * jnp.asarray(0.125, bf16)
        grads = grad_ref[part, :]
        outs = []
        key_part = None
        value_part = None
        for head in range(2):
            own = (lane // HDIM) == head
            q_own = jnp.where(own, queries, jnp.zeros_like(queries))
            g_own = jnp.where(own, grads, jnp.zeros_like(grads))
            scores = lax.dot_general(keys, q_own, nt, preferred_element_type=f32)
            probs = jnp.exp(scores - total_ref[head, :, part])
            grad_probs = lax.dot_general(values, g_own, nt, preferred_element_type=f32)
            delta = jnp.sum(probs * grad_probs, axis=0, keepdims=True)
            grad_scores = (probs * (grad_probs - delta)).astype(bf16)
            one_value = jnp.dot(probs.astype(bf16), g_own, preferred_element_type=f32)
            one_key = jnp.dot(grad_scores, q_own, preferred_element_type=f32)
            value_part = one_value if head == 0 else value_part + one_value
            key_part = one_key if head == 0 else key_part + one_key
            outs.append(
                jnp.dot(
                    keys_t[head * HDIM : (head + 1) * HDIM, :],
                    grad_scores,
                    preferred_element_type=f32,
                )
            )
        dq_ref[part, :] = (jnp.concatenate(outs, axis=0) * 0.125).T.astype(bf16)
        if block == 0:
            dk_acc[...] = key_part
            dv_acc[...] = value_part
        else:
            dk_acc[...] += key_part
            dv_acc[...] += value_part
    dk_ref[...] = dk_acc[...].astype(bf16)
    dv_ref[...] = dv_acc[...].astype(bf16)


def attend_back(qkv, total, grad_mixed):
    rows, width = grad_mixed.shape
    pairs = width // 128
    macs = 5 * rows * rows * width
    block = pl.BlockSpec((rows, 128), lambda p: (0, p))
    return pl.pallas_call(
        attend_back_kernel,
        grid=(pairs,),
        in_specs=[
            block,
            pl.BlockSpec((rows, 128), lambda p: (0, pairs + p)),
            pl.BlockSpec((rows, 128), lambda p: (0, 2 * pairs + p)),
            pl.BlockSpec((2, 1, rows), lambda p: (p, 0, 0)),
            block,
        ],
        out_specs=[block] * 3,
        out_shape=[jax.ShapeDtypeStruct((rows, width), jnp.bfloat16)] * 3,
        scratch_shapes=[pltpu.VMEM((rows, 128), jnp.float32)] * 2,
        compiler_params=pltpu.CompilerParams(vmem_limit_bytes=VMEM),
        cost_estimate=pl.CostEstimate(
            flops=8 * macs, bytes_accessed=14 * rows * width, transcendentals=macs // 320
        ),
        name="attend_back",
    )(qkv, qkv, qkv, total, grad_mixed)


def tuned(
    tokens,
    out_grad,
    query_counts,
    first_gain,
    first_bias,
    query_weight,
    query_bias,
    key_weight,
    value_weight,
    value_bias,
    output_weight,
    output_bias,
    second_gain,
    second_bias,
    up_weight,
    up_bias,
    down_weight,
    down_bias,
):
    f32, bf16 = jnp.float32, jnp.bfloat16
    x = lax.axis_index("seq")
    core = lax.axis_index("cell") % 2
    swapped = x != core
    rows, width = tokens.shape[1:]
    hidden_width = up_weight.shape[1] // 2
    head_width = width // 2

    vectors = (first_gain, first_bias, query_bias, value_bias, output_bias, second_gain, second_bias, down_bias)
    vectors = jnp.concatenate([jnp.stack(vectors), up_bias.reshape(4, -1), jnp.zeros((4, head_width), bf16)])
    cell_weight = jnp.broadcast_to(jnp.sqrt(query_counts.astype(f32) / 1000.0), (8, 128))
    (
        own,
        own_grad,
        cell_weight,
        vectors,
        qkv_weight,
        out_weight,
        up_all,
        down_all,
        normed_one,
        qkv,
        mixed,
        log_total,
        middle,
        normed_two,
        hidden,
        slope,
        grad_ffn,
    ) = forward(
        tokens[0],
        out_grad[0],
        cell_weight,
        vectors.astype(f32),
        query_weight,
        key_weight,
        value_weight,
        output_weight,
        up_weight,
        down_weight,
    )
    gain_one, gain_two, d_bias = (vectors[:, i].reshape(-1) for i in (0, 5, 7))
    standard_one, inverse_one = standardize(own.astype(f32))
    standard_two, inverse_two = standardize(middle)

    grad_result = own_grad.astype(f32) * cell_weight[:1, :1]

    def weight_sum(left, right):
        give = weight_grad(half_of(left, 1 - x, 1), right).astype(bf16)
        keep = weight_grad(half_of(left, x, 1), right).astype(bf16)
        return give, keep

    sum_down = weight_sum(hidden, grad_ffn)
    grad_up = (matmul_right_t(grad_ffn, down_all) * slope.astype(f32)).astype(bf16)
    sum_up = weight_sum(normed_two, grad_up)
    partial = matmul_right_t(grad_up, up_all)
    grad_normed_two = partial[:rows] + across(partial[rows:].astype(bf16), CORE_BIT).astype(f32)
    grad_middle = grad_result + standardize_back(grad_normed_two, standard_two, inverse_two, gain_two)
    grad_attn_own = grad_middle.astype(bf16)
    grad_attn = jnp.concatenate([grad_attn_own, across(grad_attn_own, CORE_BIT)])
    sum_out = weight_sum(mixed, half_of(grad_attn, core, 1))

    partial = matmul(hidden, down_all)
    result = middle + partial[:rows] + across(partial[rows:].astype(bf16), CORE_BIT).astype(f32) + d_bias
    result = result.astype(bf16)
    result = jnp.where(swapped, across_diagonal(result), result)

    grad_mixed = matmul_right_t(grad_attn, half_of(out_weight, core)).astype(bf16)
    grad_qkv = jnp.concatenate(attend_back(qkv, log_total, grad_mixed), axis=1)
    sum_qkv = weight_sum(normed_one, grad_qkv)
    partial = matmul_right_t(grad_qkv, qkv_weight)
    grad_normed_one = partial[:rows] + across(partial[rows:].astype(bf16), CORE_BIT).astype(f32)
    input_grad = grad_middle + standardize_back(grad_normed_one, standard_one, inverse_one, gain_one)
    input_grad = input_grad.astype(bf16)
    input_grad = jnp.where(swapped, across_diagonal(input_grad), input_grad)

    def at_core(value):
        zero = jnp.zeros_like(value)
        return jnp.concatenate([jnp.where(core == 0, value, zero), jnp.where(core == 0, zero, value)], axis=-1)

    qkv_sum = column_sum(grad_qkv).reshape(3, head_width)
    up_sum = at_core(column_sum(grad_up).reshape(2, 1, -1)).reshape(-1)
    sums = [
        jnp.sum(grad_normed_one * standard_one, axis=0),
        jnp.sum(grad_normed_one, axis=0),
        at_core(qkv_sum[0]),
        at_core(qkv_sum[2]),
        column_sum(grad_attn_own),
        jnp.sum(grad_normed_two * standard_two, axis=0),
        jnp.sum(grad_normed_two, axis=0),
        column_sum(grad_ffn[:rows]),
        up_sum,
    ]
    sizes = [value.shape[0] for value in sums]
    packed = jnp.concatenate(sums)
    packed = jnp.pad(packed, (0, -packed.shape[0] % 8192)).reshape(-1, 1024)
    down_sum, up_sum, out_sum, *qkv_sum, packed = reduce(*sum_down, *sum_up, *sum_out, *sum_qkv, packed)
    packed = packed.reshape(-1)
    sums = []
    for size in sizes:
        sums.append(half_of(packed[:size], x))
        packed = packed[size:]
    s_gain_one, s_bias_one, s_q_bias, s_v_bias, s_o_bias, s_gain_two, s_bias_two, s_d_bias, s_u_bias = sums

    return (
        result[None],
        input_grad[None],
        s_gain_one,
        s_bias_one,
        qkv_sum[0].astype(f32),
        s_q_bias,
        qkv_sum[1].astype(f32),
        qkv_sum[2].astype(f32),
        s_v_bias,
        out_sum.astype(f32),
        s_o_bias,
        s_gain_two,
        s_bias_two,
        up_sum.astype(f32),
        s_u_bias,
        down_sum.astype(f32),
        s_d_bias,
    )


def chosen(mesh):
    cells, blocks = mesh.shape["cell"], mesh.shape["seq"]

    def per_device(tokens, *rest):
        if blocks == 2 and cells == 16 and tokens.shape == (1, 512, 1280):
            return tuned(tokens, *rest)
        return general(tokens, *rest)

    return per_device


def solution(mesh):
    placed = (
        P("cell", "seq", None),
        P("cell", "seq", None),
        P("cell"),
        P("seq"),
        P("seq"),
        P("seq", None),
        P("seq"),
        P("seq", None),
        P("seq", None),
        P("seq"),
        P("seq", None),
        P("seq"),
        P("seq"),
        P("seq"),
        P("seq", None),
        P("seq"),
        P("seq", None),
        P("seq"),
    )
    return jax.shard_map(
        chosen(mesh),
        mesh=mesh,
        in_specs=placed,
        out_specs=(
            P("cell", "seq", None),
            P("cell", "seq", None),
            P("seq"),
            P("seq"),
            P("seq", None),
            P("seq"),
            P("seq", None),
            P("seq", None),
            P("seq"),
            P("seq", None),
            P("seq"),
            P("seq"),
            P("seq"),
            P("seq", None),
            P("seq"),
            P("seq", None),
            P("seq"),
        ),
        check_vma=False,
    )
```

```python
import jax
import jax.numpy as jnp
from jax import lax
from jax.experimental import pallas as pl
from jax.experimental.pallas import tpu as pltpu
from jax.sharding import PartitionSpec as P

HEADS = 20
HDIM = 64


def from_behind(value, axis, steps):
    count = lax.axis_size(axis)
    pairs = [(source, (source + steps) % count) for source in range(count)]
    return lax.ppermute(value, axis, pairs)


def for_sending(x):
    return jax.tree.map(lambda a: a.astype(jnp.bfloat16) if a.dtype == jnp.float32 else a, x)


def matmul(left, right):
    return jnp.dot(left, right, preferred_element_type=jnp.float32)


def matmul_right_t(left, right):
    return jnp.einsum("to,io->ti", left, right, preferred_element_type=jnp.float32)


def weight_grad(left, right):
    return jnp.einsum("ti,to->io", left, right, preferred_element_type=jnp.float32)


def standardize(values):
    average = jnp.mean(values, axis=-1, keepdims=True)
    centred = values - average
    inverse = lax.rsqrt(jnp.mean(centred * centred, axis=-1, keepdims=True) + 1e-05)
    return (centred * inverse, inverse)


def standardize_back(grad_normed, standard, inverse, gain_vec):
    scaled = grad_normed * gain_vec
    return inverse * (
        scaled
        - jnp.mean(scaled, axis=-1, keepdims=True)
        - standard * jnp.mean(scaled * standard, axis=-1, keepdims=True)
    )


def gelu_value(up_proj):
    return 0.5 * up_proj * (1.0 + lax.erf(up_proj * 0.7071067811865476))


def gelu_slope(up_proj):
    return (
        0.5 * (1.0 + lax.erf(up_proj * 0.7071067811865476))
        + up_proj * jnp.exp(-0.5 * up_proj * up_proj) * 0.3989422804014327
    )


def score_block(queries, key_rows):
    return (
        jnp.einsum("cqhd,ckhd->chqk", queries, key_rows, preferred_element_type=jnp.float32) * 0.125
    )


def column_sum(values):
    return jnp.sum(values.astype(jnp.float32), axis=0)


def general(
    tokens,
    out_grad,
    query_counts,
    first_gain,
    first_bias,
    query_weight,
    query_bias,
    key_weight,
    value_weight,
    value_bias,
    output_weight,
    output_bias,
    second_gain,
    second_bias,
    up_weight,
    up_bias,
    down_weight,
    down_bias,
):
    (
        first_gain,
        first_bias,
        query_weight,
        query_bias,
        key_weight,
        value_weight,
        value_bias,
        output_weight,
        output_bias,
        second_gain,
        second_bias,
        up_weight,
        up_bias,
        down_weight,
        down_bias,
    ) = (
        lax.all_gather(first_gain, "seq", axis=0, tiled=True),
        lax.all_gather(first_bias, "seq", axis=0, tiled=True),
        lax.all_gather(query_weight, "seq", axis=0, tiled=True),
        lax.all_gather(query_bias, "seq", axis=0, tiled=True),
        lax.all_gather(key_weight, "seq", axis=0, tiled=True),
        lax.all_gather(value_weight, "seq", axis=0, tiled=True),
        lax.all_gather(value_bias, "seq", axis=0, tiled=True),
        lax.all_gather(output_weight, "seq", axis=0, tiled=True),
        lax.all_gather(output_bias, "seq", axis=0, tiled=True),
        lax.all_gather(second_gain, "seq", axis=0, tiled=True),
        lax.all_gather(second_bias, "seq", axis=0, tiled=True),
        lax.all_gather(up_weight, "seq", axis=0, tiled=True),
        lax.all_gather(up_bias, "seq", axis=0, tiled=True),
        lax.all_gather(down_weight, "seq", axis=0, tiled=True),
        lax.all_gather(down_bias, "seq", axis=0, tiled=True),
    )
    f32 = jnp.float32
    bf16 = jnp.bfloat16
    gain_first = first_gain.astype(f32)
    gain_second = second_gain.astype(f32)
    cell_count, seg_len, model_width = tokens.shape
    row_count = cell_count * seg_len
    head_shape = (cell_count, seg_len, HEADS, HDIM)
    cycle_size = lax.axis_size("seq")
    flat_input = tokens.reshape(row_count, model_width).astype(f32)
    standard_one, inverse_one = standardize(flat_input)
    normed_one = (standard_one * gain_first + first_bias.astype(f32)).astype(bf16)
    query_heads = (
        (matmul(normed_one, query_weight) + query_bias.astype(f32)).astype(bf16).reshape(head_shape)
    )
    key_heads = matmul(normed_one, key_weight).astype(bf16).reshape(head_shape)
    value_heads = (
        (matmul(normed_one, value_weight) + value_bias.astype(f32)).astype(bf16).reshape(head_shape)
    )
    running_max = jnp.full((cell_count, HEADS, seg_len), -1e30, f32)
    running_sum = jnp.zeros((cell_count, HEADS, seg_len), f32)
    weighted = jnp.zeros((cell_count, HEADS, seg_len, HDIM), f32)
    travel = (key_heads, value_heads)
    for step in range(cycle_size):
        if step > 0:
            travel = from_behind((travel[0], travel[1]), "seq", 1)
        scores = score_block(query_heads, travel[0])
        new_max = jnp.maximum(running_max, jnp.max(scores, axis=-1))
        rescale = jnp.exp(running_max - new_max)
        exp_scores = jnp.exp(scores - new_max[..., None])
        running_sum = running_sum * rescale + jnp.sum(exp_scores, axis=-1)
        weighted = weighted * rescale[..., None] + jnp.einsum(
            "chqk,ckhd->chqd", exp_scores.astype(bf16), travel[1], preferred_element_type=f32
        )
        running_max = new_max
    attended = weighted / running_sum[..., None]
    log_total = running_max + jnp.log(running_sum)
    mixed = attended.transpose(0, 2, 1, 3).reshape(row_count, model_width).astype(bf16)
    middle = flat_input + matmul(mixed, output_weight) + output_bias.astype(f32)
    standard_two, inverse_two = standardize(middle)
    normed_two = (standard_two * gain_second + second_bias.astype(f32)).astype(bf16)
    up_proj = matmul(normed_two, up_weight) + up_bias.astype(f32)
    hidden = gelu_value(up_proj).astype(bf16)
    result = middle + matmul(hidden, down_weight) + down_bias.astype(f32)
    result_out = result.astype(bf16).reshape(cell_count, seg_len, model_width)
    weight_cell = jnp.sqrt(query_counts.astype(f32) / 1000.0)
    grad_result = (out_grad.astype(f32) * weight_cell[:, None, None]).reshape(
        row_count, model_width
    )
    grad_ffn_out = grad_result.astype(bf16)
    grad_down_weight = weight_grad(hidden, grad_ffn_out)
    grad_down_bias = column_sum(grad_ffn_out)
    grad_up = (matmul_right_t(grad_ffn_out, down_weight) * gelu_slope(up_proj)).astype(bf16)
    grad_up_weight = weight_grad(normed_two, grad_up)
    grad_up_bias = column_sum(grad_up)
    grad_normed_two = matmul_right_t(grad_up, up_weight)
    grad_second_gain = jnp.sum(grad_normed_two * standard_two, axis=0)
    grad_second_bias = jnp.sum(grad_normed_two, axis=0)
    grad_middle = grad_result + standardize_back(
        grad_normed_two, standard_two, inverse_two, gain_second
    )
    grad_attn_out = grad_middle.astype(bf16)
    grad_output_weight = weight_grad(mixed, grad_attn_out)
    grad_output_bias = column_sum(grad_attn_out)
    grad_mixed = matmul_right_t(grad_attn_out, output_weight).astype(bf16).reshape(head_shape)
    row_delta = jnp.sum(grad_mixed.astype(f32).transpose(0, 2, 1, 3) * attended, axis=-1)
    grad_query_acc = jnp.zeros(head_shape, f32)
    moving = (jnp.zeros(head_shape, f32), jnp.zeros(head_shape, f32))
    travel = (key_heads, value_heads)
    for step in range(cycle_size):
        if step > 0:
            travel = from_behind((travel[0], travel[1]), "seq", 1)
        block_keys, block_values = travel
        scores = score_block(query_heads, block_keys)
        prob_block = jnp.exp(scores - log_total[..., None])
        part_values = jnp.einsum(
            "chqk,cqhd->ckhd", prob_block.astype(bf16), grad_mixed, preferred_element_type=f32
        )
        grad_probs = jnp.einsum(
            "cqhd,ckhd->chqk", grad_mixed, block_values, preferred_element_type=f32
        )
        grad_scores = (prob_block * (grad_probs - row_delta[..., None])).astype(bf16)
        grad_query_acc = (
            grad_query_acc
            + jnp.einsum("chqk,ckhd->cqhd", grad_scores, block_keys, preferred_element_type=f32)
            * 0.125
        )
        part_keys = (
            jnp.einsum("chqk,cqhd->ckhd", grad_scores, query_heads, preferred_element_type=f32)
            * 0.125
        )
        moving = from_behind(
            (for_sending(moving[0] + part_keys), for_sending(moving[1] + part_values)), "seq", 1
        )
    grad_queries = grad_query_acc.astype(bf16).reshape(row_count, model_width)
    grad_keys = moving[0].astype(bf16).reshape(row_count, model_width)
    grad_values = moving[1].astype(bf16).reshape(row_count, model_width)
    grad_query_weight = weight_grad(normed_one, grad_queries)
    grad_query_bias = column_sum(grad_queries)
    grad_key_weight = weight_grad(normed_one, grad_keys)
    grad_value_weight = weight_grad(normed_one, grad_values)
    grad_value_bias = column_sum(grad_values)
    grad_normed_one = (
        matmul_right_t(grad_queries, query_weight)
        + matmul_right_t(grad_keys, key_weight)
        + matmul_right_t(grad_values, value_weight)
    )
    grad_first_gain = jnp.sum(grad_normed_one * standard_one, axis=0)
    grad_first_bias = jnp.sum(grad_normed_one, axis=0)
    grad_input = grad_middle + standardize_back(
        grad_normed_one, standard_one, inverse_one, gain_first
    )
    input_grad = grad_input.astype(bf16).reshape(cell_count, seg_len, model_width)
    shared_all = (
        lax.psum_scatter(
            grad_first_gain.astype(jnp.bfloat16), "seq", scatter_dimension=0, tiled=True
        ).astype(jnp.float32),
        lax.psum_scatter(
            grad_first_bias.astype(jnp.bfloat16), "seq", scatter_dimension=0, tiled=True
        ).astype(jnp.float32),
        lax.psum_scatter(
            grad_query_weight.astype(jnp.bfloat16), "seq", scatter_dimension=0, tiled=True
        ).astype(jnp.float32),
        lax.psum_scatter(
            grad_query_bias.astype(jnp.bfloat16), "seq", scatter_dimension=0, tiled=True
        ).astype(jnp.float32),
        lax.psum_scatter(
            grad_key_weight.astype(jnp.bfloat16), "seq", scatter_dimension=0, tiled=True
        ).astype(jnp.float32),
        lax.psum_scatter(
            grad_value_weight.astype(jnp.bfloat16), "seq", scatter_dimension=0, tiled=True
        ).astype(jnp.float32),
        lax.psum_scatter(
            grad_value_bias.astype(jnp.bfloat16), "seq", scatter_dimension=0, tiled=True
        ).astype(jnp.float32),
        lax.psum_scatter(
            grad_output_weight.astype(jnp.bfloat16), "seq", scatter_dimension=0, tiled=True
        ).astype(jnp.float32),
        lax.psum_scatter(
            grad_output_bias.astype(jnp.bfloat16), "seq", scatter_dimension=0, tiled=True
        ).astype(jnp.float32),
        lax.psum_scatter(
            grad_second_gain.astype(jnp.bfloat16), "seq", scatter_dimension=0, tiled=True
        ).astype(jnp.float32),
        lax.psum_scatter(
            grad_second_bias.astype(jnp.bfloat16), "seq", scatter_dimension=0, tiled=True
        ).astype(jnp.float32),
        lax.psum_scatter(
            grad_up_weight.astype(jnp.bfloat16), "seq", scatter_dimension=0, tiled=True
        ).astype(jnp.float32),
        lax.psum_scatter(
            grad_up_bias.astype(jnp.bfloat16), "seq", scatter_dimension=0, tiled=True
        ).astype(jnp.float32),
        lax.psum_scatter(
            grad_down_weight.astype(jnp.bfloat16), "seq", scatter_dimension=0, tiled=True
        ).astype(jnp.float32),
        lax.psum_scatter(
            grad_down_bias.astype(jnp.bfloat16), "seq", scatter_dimension=0, tiled=True
        ).astype(jnp.float32),
    )
    (
        grad_first_gain,
        grad_first_bias,
        grad_query_weight,
        grad_query_bias,
        grad_key_weight,
        grad_value_weight,
        grad_value_bias,
        grad_output_weight,
        grad_output_bias,
        grad_second_gain,
        grad_second_bias,
        grad_up_weight,
        grad_up_bias,
        grad_down_weight,
        grad_down_bias,
    ) = shared_all
    (
        grad_first_gain,
        grad_first_bias,
        grad_query_weight,
        grad_query_bias,
        grad_key_weight,
        grad_value_weight,
        grad_value_bias,
        grad_output_weight,
        grad_output_bias,
        grad_second_gain,
        grad_second_bias,
        grad_up_weight,
        grad_up_bias,
        grad_down_weight,
        grad_down_bias,
    ) = (
        lax.psum(grad_first_gain.astype(jnp.bfloat16), "cell").astype(jnp.float32),
        lax.psum(grad_first_bias.astype(jnp.bfloat16), "cell").astype(jnp.float32),
        lax.psum(grad_query_weight.astype(jnp.bfloat16), "cell").astype(jnp.float32),
        lax.psum(grad_query_bias.astype(jnp.bfloat16), "cell").astype(jnp.float32),
        lax.psum(grad_key_weight.astype(jnp.bfloat16), "cell").astype(jnp.float32),
        lax.psum(grad_value_weight.astype(jnp.bfloat16), "cell").astype(jnp.float32),
        lax.psum(grad_value_bias.astype(jnp.bfloat16), "cell").astype(jnp.float32),
        lax.psum(grad_output_weight.astype(jnp.bfloat16), "cell").astype(jnp.float32),
        lax.psum(grad_output_bias.astype(jnp.bfloat16), "cell").astype(jnp.float32),
        lax.psum(grad_second_gain.astype(jnp.bfloat16), "cell").astype(jnp.float32),
        lax.psum(grad_second_bias.astype(jnp.bfloat16), "cell").astype(jnp.float32),
        lax.psum(grad_up_weight.astype(jnp.bfloat16), "cell").astype(jnp.float32),
        lax.psum(grad_up_bias.astype(jnp.bfloat16), "cell").astype(jnp.float32),
        lax.psum(grad_down_weight.astype(jnp.bfloat16), "cell").astype(jnp.float32),
        lax.psum(grad_down_bias.astype(jnp.bfloat16), "cell").astype(jnp.float32),
    )
    return (
        result_out,
        input_grad,
        grad_first_gain,
        grad_first_bias,
        grad_query_weight,
        grad_query_bias,
        grad_key_weight,
        grad_value_weight,
        grad_value_bias,
        grad_output_weight,
        grad_output_bias,
        grad_second_gain,
        grad_second_bias,
        grad_up_weight,
        grad_up_bias,
        grad_down_weight,
        grad_down_bias,
    )


Q_BLOCK = 512


MESH = pl.DeviceIdType.MESH
ANY = pl.BlockSpec(memory_space=pl.ANY)
EDGE = 640


class Spot:
    def __init__(self):
        self.x = lax.axis_index("seq")
        self.cell = lax.axis_index("cell")
        self.core = lax.rem(self.cell, 2)
        self.y = lax.rem(self.cell // 2, 2)
        self.low = lax.rem(self.cell // 4, 2)
        self.high = lax.rem(self.cell // 8, 2)

    def flip(self, index, bit):
        return {"cell": self.cell + bit - 2 * bit * index}

    def over(self, name):
        if name == "x":
            return {"seq": 1 - self.x}
        if name == "core":
            return self.flip(self.core, 1)
        if name == "diagonal":
            return {"seq": 1 - self.x, **self.flip(self.core, 1)}
        return self.flip(*{"y": (self.y, 2), "low": (self.low, 4), "high": (self.high, 8)}[name])

    def meet(self, names):
        barrier = pltpu.get_barrier_semaphore()
        for name in names:
            pl.semaphore_signal(barrier, inc=1, device_id=self.over(name), device_id_type=MESH)
        pl.semaphore_wait(barrier, len(names))

    def send(self, name, source, target, send_sem, recv_sem):
        return pltpu.make_async_remote_copy(
            source, target, send_sem, recv_sem, device_id=self.over(name), device_id_type=MESH
        )


def rows_at(start, size):
    return pl.ds(pl.multiple_of(start, 16), size)


def cols(start, size):
    return pl.ds(pl.multiple_of(start, 128), size)


def attend_pair(qkv, mixed, total_ref, pair, base):
    f32, bf16 = jnp.float32, jnp.bfloat16
    rows = qkv.shape[0]
    lane = lax.broadcasted_iota(jnp.int32, (1, 128), 1)
    here = pair * 128
    keys = qkv[:, cols(EDGE + here, 128)]
    values_t = qkv[:, cols(2 * EDGE + here, 128)].T
    for block in range(rows // Q_BLOCK):
        part = pl.ds(block * Q_BLOCK, Q_BLOCK)
        queries = qkv[part, cols(here, 128)] * jnp.asarray(0.125, bf16)
        outs = []
        for head in range(2):
            own = (lane // HDIM) == head
            scores = lax.dot_general(
                keys,
                jnp.where(own, queries, jnp.zeros_like(queries)),
                (((1,), (1,)), ((), ())),
                preferred_element_type=f32,
            )
            largest = jnp.max(scores, axis=0, keepdims=True)
            weights = jnp.exp(scores - largest)
            total = jnp.sum(weights, axis=0, keepdims=True)
            out = jnp.dot(
                values_t[head * HDIM : (head + 1) * HDIM, :],
                weights.astype(bf16),
                preferred_element_type=f32,
            )
            outs.append(out / total)
            total_ref[2 * pair + head, :, part] = largest + jnp.log(total)
        mixed[part, cols(base + here, 128)] = jnp.concatenate(outs, axis=0).T.astype(bf16)


def forward_kernel(
    tokens, out_grad, cell_weight, vectors, wq, wk, wv, wo, wup, wdown,
    own_out, grad_out, weight_out, vectors_out, qkv_w_out, out_w_out, up_w_out, down_w_out,
    normed_one_out, qkv_out, mixed_out, total_out, middle_out, normed_two_out, hidden_out, slope_out, ffn_out,
    tok, grad, scale, vec, qkv_w, out_w, up_w, down_w,
    normed_one, qkv, mixed, totals, middle, normed_two, hidden, slope, ffn,
    send_sems, recv_sems, local_sems, side_send, side_recv, side_local, out_sems,
):
    f32, bf16 = jnp.float32, jnp.bfloat16
    at = Spot()
    x, core = at.x, at.core
    rows = tok.shape[0]
    width = tok.shape[1]
    at.meet(("x", "core", "diagonal", "y", "low", "high"))

    side = [(tokens, tok), (cell_weight, scale), (out_grad, grad)]
    diagonal = [at.send("diagonal", s, t, side_send.at[i], side_recv.at[i]) for i, (s, t) in enumerate(side)]
    straight = [pltpu.make_async_copy(s, t, side_local.at[i]) for i, (s, t) in enumerate(side)]

    def swap(i, remote, local):
        @pl.when(x != core)
        def _():
            remote(diagonal[i])

        @pl.when(x == core)
        def _():
            local(straight[i])

    def swap_start(i):
        swap(i, lambda c: c.start(), lambda c: c.start())

    def swap_wait(i):
        swap(i, lambda c: c.wait(), lambda c: c.wait())

    chunks = []
    for i, ref in enumerate((wq, wk, wv)):
        chunks.append((ref.at[:, cols(core * EDGE, EDGE)], qkv_w, EDGE, 0, i * EDGE))
    for i in range(4):
        start = (i // 2) * 4 * EDGE + core * 2 * EDGE + (i % 2) * EDGE
        chunks.append((wup.at[:, cols(start, EDGE)], up_w, EDGE, 0, i * EDGE))
    for i in range(4):
        source = wdown.at[rows_at(core * 2 * EDGE + (i // 2) * EDGE, EDGE), pl.ds((i % 2) * EDGE, EDGE)]
        chunks.append((source, down_w, 2 * EDGE, (i // 2) * EDGE, (i % 2) * EDGE))
    count = len(chunks)
    eighth = EDGE // 8
    place = at.y * 4 + at.low * 2 + at.high

    def region(k, half, start, size):
        _, ref, stride, row, column = chunks[k]
        return ref.at[rows_at(half * stride + row + start * eighth, size * eighth), pl.ds(column, EDGE)]

    ops = {}
    for k, chunk in enumerate(chunks):
        ops["x", k] = at.send(
            "x", chunk[0].at[rows_at(place * eighth, eighth)], region(k, x, place, 1), send_sems.at[0, k], recv_sems.at[0, k]
        )
        for s, (name, start, size) in enumerate(
            (("high", place, 1), ("low", at.y * 4 + at.low * 2, 2), ("y", at.y * 4, 4))
        ):
            part = region(k, 1 - x, start, size)
            ops[name, k] = at.send(name, part, part, send_sems.at[s + 1, k], recv_sems.at[s + 1, k])
        ops["local", k] = pltpu.make_async_copy(chunk[0], region(k, x, 0, 8), local_sems.at[k])
    half = EDGE // 2
    out_x = at.send(
        "x", wo.at[rows_at(core * half, half)], out_w.at[rows_at(x * EDGE + core * half, half)], side_send.at[4], side_recv.at[4]
    )
    part = out_w.at[rows_at((1 - x) * EDGE + core * half, half)]
    out_core = at.send("core", part, part, side_send.at[5], side_recv.at[5])
    out_local = pltpu.make_async_copy(wo, out_w.at[rows_at(x * EDGE, EDGE)], side_local.at[4])
    vec_x = at.send("x", vectors, vec.at[x], side_send.at[3], side_recv.at[3])
    vec_local = pltpu.make_async_copy(vectors, vec.at[x], side_local.at[3])
    top, bottom = pl.ds(0, rows), pl.ds(rows, rows)

    def core_copy(i, source, target):
        return at.send("core", source, target, side_send.at[i], side_recv.at[i])

    normed_one_core = core_copy(6, normed_one.at[top], normed_one.at[bottom])
    heads = cols(core * EDGE, EDGE)
    mixed_core = [
        core_copy(7, mixed.at[top, heads], mixed.at[bottom, heads]),
        core_copy(8, mixed.at[bottom, heads], mixed.at[top, heads]),
    ]
    normed_two_core = core_copy(9, normed_two.at[top], normed_two.at[bottom])
    ffn_core = core_copy(10, ffn.at[top], ffn.at[bottom])

    outs = []
    early = []

    def put(source, target):
        copy = pltpu.make_async_copy(source, target, out_sems.at[len(outs)])
        copy.start()
        outs.append(copy)
        return copy

    issue = {
        0: [ops["x", 3], ops["x", 4]],
        1: [ops["x", 5], ops["x", 6]],
        2: [out_x, out_local, ops["local", 3], ops["local", 4], ops["local", 5], ops["local", 6]],
        3: [ops["x", 7], ops["x", 8]],
        4: [ops["x", 9], ops["x", 10], ops["local", 7], ops["local", 8], ops["local", 9], ops["local", 10]],
    }

    def tick(t):
        for op in issue.get(t, ()):
            op.start()
        if t == 5:
            swap_start(2)
        for before, name, after in ((3, "y", None), (2, "low", "y"), (1, "high", "low"), (0, "x", "high")):
            k = t - before
            if 0 <= k < count:
                ops[name, k].wait_recv()
                if after:
                    ops[after, k].start()
        if t == 6:
            out_x.wait_recv()
            out_core.start()

    for k in range(3):
        ops["x", k].start()
    vec_x.start()
    swap_start(0)
    swap_start(1)
    vec_local.start()
    for k in range(3):
        ops["local", k].start()
    tick(0)
    tick(1)
    vec_x.wait_recv()
    vec_local.wait()

    def vector(i):
        return jnp.concatenate([vec[0, i : i + 1, :], vec[1, i : i + 1, :]], axis=1)

    def norm(values, gain, bias):
        average = jnp.mean(values, axis=-1, keepdims=True)
        centred = values - average
        inverse = lax.rsqrt(jnp.mean(centred * centred, axis=-1, keepdims=True) + 1e-05)
        return (centred * inverse * gain + bias).astype(bf16)

    swap_wait(0)
    gain_one, bias_one = vector(0), vector(1)

    @pl.loop(0, rows // 64)
    def _(i):
        here = rows_at(i * 64, 64)
        normed_one[here, :] = norm(tok[here, :].astype(f32), gain_one, bias_one)

    normed_one_core.start()
    tick(2)
    put(tok, own_out)
    normed_one_core.wait_recv()
    put(normed_one, normed_one_out)

    for i in range(3):
        tick(3 + i)
        ops["local", i].wait()
        lanes = pl.ds(i * EDGE, EDGE)
        bias = 0.0 if i == 1 else vec[core, 2 + i // 2 : 3 + i // 2, :]

        @pl.loop(0, 2 * rows // 256)
        def _(r):
            here = rows_at(r * 256, 256)
            value = jnp.dot(normed_one[here, :], qkv_w[:, lanes], preferred_element_type=f32)
            qkv[here, lanes] = (value + bias).astype(bf16)

    put(qkv, qkv_out)
    put(qkv_w, qkv_w_out)

    @pl.loop(0, EDGE // 128)
    def _(pair):
        attend_pair(qkv, mixed, totals, pair, core * EDGE)

        @pl.when(pair == 1)
        def _():
            tick(6)

        @pl.when(pair == 3)
        def _():
            tick(7)

    mixed_core[0].start()
    mixed_core[1].start()
    put(totals, total_out)
    tick(8)
    out_local.wait()
    out_core.wait_recv()
    mixed_core[1].wait_recv()
    gain_two, bias_two, out_bias = vector(5), vector(6), vector(4)

    @pl.loop(0, rows // 128)
    def _(r):
        here = rows_at(r * 128, 128)
        value = jnp.dot(mixed[here, :], out_w[...], preferred_element_type=f32)
        value = tok[here, :].astype(f32) + value + out_bias
        middle[here, :] = value
        normed_two[here, :] = norm(value, gain_two, bias_two)

    normed_two_core.start()
    mixed_core[0].wait_recv()
    put(out_w, out_w_out)
    put(mixed, mixed_out)
    put(middle, middle_out)
    tick(9)
    normed_two_core.wait_recv()
    put(normed_two, normed_two_out)
    waits = {}
    for i in range(4):
        ops["local", 3 + i].wait()
        slot = i % 2
        if i >= 2:
            for copy in waits[slot]:
                copy.wait()
                early.append(copy)
        lanes = pl.ds(i * EDGE, EDGE)
        bias = vec[i // 2, pl.ds(8 + core * 2 + i % 2, 1), :]

        @pl.loop(0, 2 * rows // 128)
        def _(r):
            here = rows_at(r * 128, 128)
            up = jnp.dot(normed_two[here, :], up_w[:, lanes], preferred_element_type=f32) + bias
            cdf = 0.5 * (1.0 + lax.erf(up * 0.7071067811865476))
            hidden[slot, here, :] = (up * cdf).astype(bf16)
            slope[slot, here, :] = (cdf + up * jnp.exp(-0.5 * up * up) * 0.3989422804014327).astype(bf16)

        waits[slot] = (
            put(hidden.at[slot], hidden_out.at[:, lanes]),
            put(slope.at[slot], slope_out.at[:, lanes]),
        )
        if i == 1:
            swap_wait(1)
            swap_wait(2)
            weight = scale[0:1, 0:1]

            @pl.loop(0, rows // 64)
            def _(r):
                here = rows_at(r * 64, 64)
                ffn[here, :] = (grad[here, :].astype(f32) * weight).astype(bf16)

            ffn_core.start()
            put(grad, grad_out)
            put(scale, weight_out)
            put(vec, vectors_out)
        tick(10 + i)
    put(up_w, up_w_out)
    ffn_core.wait_recv()
    put(ffn, ffn_out)
    for k in range(7, count):
        ops["local", k].wait()
    put(down_w, down_w_out)
    for k in range(count):
        for name in ("x", "high", "low", "y"):
            ops[name, k].wait_send()
    for op in (out_x, out_core, vec_x, normed_one_core, *mixed_core, normed_two_core, ffn_core):
        op.wait_send()
    for copy in outs:
        if not any(copy is other for other in early):
            copy.wait()


def forward(*args):
    bf16, f32 = jnp.bfloat16, jnp.float32
    shape = jax.ShapeDtypeStruct
    rows, width = args[0].shape
    both = 2 * rows
    arrays = [
        ((rows, width), bf16),
        ((rows, width), bf16),
        (args[2].shape, f32),
        ((2,) + args[3].shape, f32),
        ((width, 3 * EDGE), bf16),
        ((width, width), bf16),
        ((width, 4 * EDGE), bf16),
        ((4 * EDGE, width), bf16),
        ((both, width), bf16),
        ((both, 3 * EDGE), bf16),
        ((both, width), bf16),
        ((EDGE // HDIM, 1, both), f32),
        ((rows, width), f32),
        ((both, width), bf16),
        ((both, 4 * EDGE), bf16),
        ((both, 4 * EDGE), bf16),
        ((both, width), bf16),
    ]
    scratch = [pltpu.VMEM(*array) for array in arrays]
    scratch[14] = scratch[15] = pltpu.VMEM((2, both, EDGE), bf16)
    dma = pltpu.SemaphoreType.DMA
    return pl.pallas_call(
        forward_kernel,
        in_specs=[ANY] * len(args),
        out_specs=[ANY] * len(arrays),
        out_shape=[shape(*array) for array in arrays],
        scratch_shapes=scratch + [dma((4, 11)), dma((4, 11)), dma((11,)), dma((11,)), dma((11,)), dma((5,)), dma((24,))],
        compiler_params=pltpu.CompilerParams(
            collective_id=0, has_side_effects=True, vmem_limit_bytes=60 * 1024 * 1024
        ),
        name="forward",
    )(*args)


def attend_back_pair(qkv, totals, keys_acc, values_acc, pair):
    f32, bf16 = jnp.float32, jnp.bfloat16
    rows = qkv.shape[0]
    size = Q_BLOCK // 2
    lane = lax.broadcasted_iota(jnp.int32, (1, 128), 1)
    here, key_lanes, value_lanes, grad_lanes = (cols(i * EDGE + pair * 128, 128) for i in range(4))
    keys = qkv[:, key_lanes]
    keys_t = keys.T
    nt = (((1,), (1,)), ((), ()))
    keys_acc[...] = jnp.zeros_like(keys_acc)
    values_acc[...] = jnp.zeros_like(values_acc)

    @pl.loop(0, rows // size)
    def _(block):
        part = rows_at(block * size, size)
        queries = qkv[part, here] * jnp.asarray(0.125, bf16)
        grads = qkv[part, grad_lanes]
        values = qkv[:, value_lanes]
        outs = []
        key_part = value_part = 0.0
        for head in range(2):
            own = (lane // HDIM) == head
            q_own = jnp.where(own, queries, jnp.zeros_like(queries))
            g_own = jnp.where(own, grads, jnp.zeros_like(grads))
            scores = lax.dot_general(keys, q_own, nt, preferred_element_type=f32)
            probs = jnp.exp(scores - totals[2 * pair + head, :, cols(block * size, size)])
            grad_probs = lax.dot_general(values, g_own, nt, preferred_element_type=f32)
            delta = jnp.sum(probs * grad_probs, axis=0, keepdims=True)
            grad_scores = (probs * (grad_probs - delta)).astype(bf16)
            value_part += jnp.dot(probs.astype(bf16), g_own, preferred_element_type=f32)
            key_part += jnp.dot(grad_scores, q_own, preferred_element_type=f32)
            outs.append(jnp.dot(keys_t[head * HDIM : (head + 1) * HDIM, :], grad_scores, preferred_element_type=f32))
        qkv[part, here] = (jnp.concatenate(outs, axis=0) * 0.125).T.astype(bf16)
        keys_acc[...] += key_part
        values_acc[...] += value_part

    qkv[:, key_lanes] = keys_acc[...].astype(bf16)
    qkv[:, value_lanes] = values_acc[...].astype(bf16)


def backward_kernel(
    own, own_grad, cell_weight, vectors, qkv_w, out_w, up_w, down_w,
    normed_one, qkv, mixed, totals, middle, normed_two, hidden, slope, ffn,
    result_ref, input_ref, down_ref, up_ref, out_ref, q_ref, k_ref, v_ref, vec_ref,
    wide, grad_up, normed, pair_buf, ffn_buf, down_buf, up_buf, part_buf, taken, given, mid, tot, vec, scale, keys_acc, values_acc,
    blocks, from_x, from_y, from_low, from_high, res, sums,
    send_sems, recv_sems, store_sems, load_sems, core_send, core_recv, swap_send, swap_recv, swap_local, vec_send, vec_recv, vec_local,
):
    f32, bf16 = jnp.float32, jnp.bfloat16
    at = Spot()
    x, core = at.x, at.core
    rows, width = own.shape
    both = 2 * rows
    top, bottom = pl.ds(0, rows), pl.ds(rows, rows)
    nt = (((1,), (1,)), ((), ()))
    tn = (((0,), (0,)), ((), ()))
    loads = {}

    def load(name, source, target):
        copy = pltpu.make_async_copy(source, target, load_sems.at[len(loads)])
        copy.start()
        loads[name] = copy

    load("hidden", hidden, wide)
    load("ffn", ffn, ffn_buf)
    load("down_w", down_w, down_buf)
    slopes = [(slope.at[:, pl.ds(i * EDGE, EDGE)], pair_buf.at[:, pl.ds((i % 2) * EDGE, EDGE)]) for i in range(4)]
    load("slope0", *slopes[0])
    load("slope1", *slopes[1])
    load("up_w", up_w, up_buf)
    load("normed_two", normed_two, normed)
    load("middle", middle, mid)
    load("vectors", vectors, vec)
    load("scale", cell_weight, scale)
    load("totals", totals, tot)
    sums[0] = jnp.zeros(sums.shape[1:], f32)
    at.meet(("x", "core", "diagonal", "y", "low", "high"))

    chunks = []
    for i in range(4):
        target = down_ref.at[rows_at(core * 2 * EDGE + (i // 2) * EDGE, EDGE), pl.ds((i % 2) * EDGE, EDGE)]
        chunks.append((wide, 2 * EDGE, (i // 2) * EDGE, ffn_buf, (i % 2) * EDGE, target))
    for i in range(4):
        target = up_ref.at[:, cols((i // 2) * 4 * EDGE + core * 2 * EDGE + (i % 2) * EDGE, EDGE)]
        chunks.append((normed, EDGE, 0, grad_up, i * EDGE, target))
    mine = cols(core * EDGE, EDGE)
    mixed_rows = pl.ds(EDGE, both)
    chunks.append((down_buf.at[mixed_rows], EDGE, 0, ffn_buf, core * EDGE, out_ref.at[:, mine]))
    for i, ref in enumerate((q_ref, k_ref, v_ref)):
        chunks.append((normed, EDGE, 0, wide, i * EDGE, ref.at[:, mine]))
    count = len(chunks)

    half, quarter, eighth = EDGE // 2, EDGE // 4, EDGE // 8
    y0 = at.y * half
    l0 = y0 + at.low * quarter
    h0 = l0 + at.high * eighth
    ops = {}
    for k, chunk in enumerate(chunks):
        acc, two, slot = k % 5, k % 2, k % 5
        hops = (
            ("x", "x", blocks.at[5 + k % 3], from_x.at[k % 4]),
            ("y", "y", blocks.at[acc, rows_at((1 - at.y) * half, half)], from_y.at[two]),
            ("low", "low", blocks.at[acc, rows_at(y0 + (1 - at.low) * quarter, quarter)], from_low.at[two]),
            ("high", "high", blocks.at[acc, rows_at(l0 + (1 - at.high) * eighth, eighth)], from_high.at[two]),
            ("all_high", "high", res.at[slot, rows_at(h0, eighth)], res.at[slot, rows_at(h0, eighth)]),
            ("all_low", "low", res.at[slot, rows_at(l0, quarter)], res.at[slot, rows_at(l0, quarter)]),
            ("all_y", "y", res.at[slot, rows_at(y0, half)], res.at[slot, rows_at(y0, half)]),
            ("core", "core", res.at[slot], chunk[5]),
        )
        for s, (stage, name, source, goal) in enumerate(hops):
            ops[stage, k] = at.send(name, source, goal, send_sems.at[s, k], recv_sems.at[s, k])
        ops["store", k] = pltpu.make_async_copy(res.at[slot], chunk[5], store_sems.at[k])

    def make(k):
        left, stride, left_at, right, right_at, _ = chunks[k]

        @pl.loop(0, 2)
        def _(j):
            of = j * x + (1 - j) * (1 - x)
            slot = j * (k % 5) + (1 - j) * (5 + k % 3)
            lanes = right_at if isinstance(right_at, int) else pl.multiple_of(right_at, 128)
            product = lax.dot_general(
                left[:, cols(of * stride + left_at, EDGE)], right[:, pl.ds(lanes, EDGE)], tn, preferred_element_type=f32
            )
            blocks[slot] = product.astype(bf16)

        ops["x", k].start()

    def add(k, start, size, other, goal, goal_slot):
        @pl.loop(0, size // 80)
        def _(i):
            here = rows_at(start + i * 80, 80)
            there = rows_at(i * 80, 80)
            total = blocks[k % 5, here, :].astype(f32) + other[there, :].astype(f32)
            goal[goal_slot, here, :] = total.astype(bf16)

    def tick(t):
        k = t - 7
        if 0 <= k < count:
            ops["core", k].wait_recv()
            for stage in ("all_high", "all_low", "all_y", "core"):
                ops[stage, k].wait_send()
            ops["store", k].wait()
        for before, stage, after in ((6, "all_y", "core"), (5, "all_low", "all_y"), (4, "all_high", "all_low")):
            k = t - before
            if 0 <= k < count:
                ops[stage, k].wait_recv()
                ops[after, k].start()
                if after == "core":
                    ops["store", k].start()
        k = t - 3
        if 0 <= k < count:
            ops["high", k].wait_recv()
            add(k, h0, eighth, from_high.at[k % 2], res, k % 5)
            ops["all_high", k].start()
            for stage in ("y", "low", "high"):
                ops[stage, k].wait_send()
        k = t - 2
        if 0 <= k < count:
            ops["low", k].wait_recv()
            add(k, l0, quarter, from_low.at[k % 2], blocks, k % 5)
            ops["high", k].start()
        k = t - 1
        if 0 <= k < count:
            ops["y", k].wait_recv()
            add(k, y0, half, from_y.at[k % 2], blocks, k % 5)
            ops["low", k].start()
        k = t
        if 0 <= k < count:
            ops["x", k].wait_recv()
            add(k, 0, EDGE, from_x.at[k % 4], blocks, k % 5)
            ops["y", k].start()
            ops["x", k].wait_send()
            if k + 2 < count:
                make(k + 2)

    def core_copy(i, source, target):
        return at.send("core", source, target, core_send.at[i], core_recv.at[i])

    two_copy = core_copy(0, given.at[0], taken.at[0])
    result_copy = core_copy(1, given.at[1], taken.at[1])
    attn_copy = core_copy(2, ffn_buf.at[top], ffn_buf.at[bottom])
    one_copy = core_copy(3, given.at[0], taken.at[0])
    swaps = []
    for i, target in enumerate((result_ref, input_ref)):
        source = taken.at[1 - i]
        swaps.append(
            (
                at.send("diagonal", source, target, swap_send.at[i], swap_recv.at[i]),
                pltpu.make_async_copy(source, target, swap_local.at[i]),
            )
        )

    def swap(i, act):
        @pl.when(x != core)
        def _():
            act(swaps[i][0])

        @pl.when(x == core)
        def _():
            act(swaps[i][1])

    def vector(i):
        return jnp.concatenate([vec[0, i : i + 1, :], vec[1, i : i + 1, :]], axis=1)

    def add_vector(i, value):
        total = jnp.sum(value, axis=0, keepdims=True)
        sums[0, 2 * i : 2 * i + 1, :] += total[:, :EDGE]
        sums[0, 2 * i + 1 : 2 * i + 2, :] += total[:, EDGE:]

    def norm_back(values, grad_normed, gain):
        average = jnp.mean(values, axis=-1, keepdims=True)
        centred = values - average
        inverse = lax.rsqrt(jnp.mean(centred * centred, axis=-1, keepdims=True) + 1e-05)
        standard = centred * inverse
        scaled = grad_normed * gain
        back = inverse * (
            scaled
            - jnp.mean(scaled, axis=-1, keepdims=True)
            - standard * jnp.mean(scaled * standard, axis=-1, keepdims=True)
        )
        return standard, back

    loads["hidden"].wait()
    loads["ffn"].wait()
    make(0)
    make(1)
    loads["down_w"].wait()
    for i in range(4):
        loads["slope%d" % i].wait()
        lanes = pl.ds(i * EDGE, EDGE)
        row = pl.ds(16 + (i // 2) * 4 + core * 2 + i % 2, 1)

        @pl.loop(0, both // 256)
        def _(r):
            here = rows_at(r * 256, 256)
            value = lax.dot_general(ffn_buf[here, :], down_buf[lanes, :], nt, preferred_element_type=f32)
            value = (value * pair_buf[here, pl.ds((i % 2) * EDGE, EDGE)].astype(f32)).astype(bf16)
            grad_up[here, lanes] = value
            sums[0, row, :] += jnp.sum(value.astype(f32), axis=0, keepdims=True)

        if i < 2:
            load("slope%d" % (i + 2), *slopes[i + 2])
    load("own_grad", own_grad, pair_buf.at[top])
    load("own", own, pair_buf.at[bottom])
    loads["normed_two"].wait()
    tick(0)
    loads["up_w"].wait()

    @pl.loop(0, rows // 256)
    def _(r):
        value = lax.dot_general(grad_up[rows_at(rows + r * 256, 256), :], up_buf[...], nt, preferred_element_type=f32)
        given[0, rows_at(r * 256, 256), :] = value.astype(bf16)

    two_copy.start()

    @pl.loop(0, rows // 256)
    def _(r):
        value = lax.dot_general(grad_up[rows_at(r * 256, 256), :], up_buf[...], nt, preferred_element_type=f32)
        part_buf[rows_at(r * 256, 256), :] = value

    tick(1)

    @pl.loop(0, rows // 256)
    def _(r):
        value = jnp.dot(wide[rows_at(rows + r * 256, 256), :], down_buf[...], preferred_element_type=f32)
        given[1, rows_at(r * 256, 256), :] = value.astype(bf16)

    result_copy.start()
    two_copy.wait_recv()
    for name in ("middle", "vectors", "scale", "own_grad", "totals"):
        loads[name].wait()
    result_copy.wait_recv()
    down_bias, gain_two, gain_one = vector(7), vector(5), vector(0)

    @pl.loop(0, rows // 128)
    def _(r):
        here = rows_at(r * 128, 128)
        value = jnp.dot(wide[here, :], down_buf[...], preferred_element_type=f32)
        value = mid[here, :] + value + taken[1, here, :].astype(f32) + down_bias
        taken[1, here, :] = value.astype(bf16)

    swap(0, lambda copy: copy.start())
    load("qkv", qkv, wide.at[:, pl.ds(0, 3 * EDGE)])
    load("mixed", mixed, down_buf.at[mixed_rows])
    load("out_w", out_w.at[rows_at(core * EDGE, EDGE)], down_buf.at[pl.ds(0, EDGE)])
    load("qkv_w", qkv_w, up_buf.at[:, pl.ds(0, 3 * EDGE)])
    weight = scale[0:1, 0:1]

    @pl.loop(0, rows // 32)
    def _(r):
        here = rows_at(r * 32, 32)
        add_vector(7, ffn_buf[here, :].astype(f32))
        grad_normed = part_buf[here, :] + taken[0, here, :].astype(f32)
        standard, back = norm_back(mid[here, :], grad_normed, gain_two)
        add_vector(5, grad_normed * standard)
        add_vector(6, grad_normed)
        value = pair_buf[here, :].astype(f32) * weight + back
        mid[here, :] = value
        value = value.astype(bf16)
        ffn_buf[here, :] = value
        add_vector(4, value.astype(f32))

    attn_copy.start()
    two_copy.wait_send()
    tick(2)
    loads["out_w"].wait()
    attn_copy.wait_recv()

    @pl.loop(0, both // 256)
    def _(r):
        here = rows_at(r * 256, 256)
        value = lax.dot_general(ffn_buf[here, :], down_buf[0:EDGE, :], nt, preferred_element_type=f32)
        wide[here, pl.ds(3 * EDGE, EDGE)] = value.astype(bf16)

    loads["qkv"].wait()

    @pl.loop(0, EDGE // 128)
    def _(pair):
        attend_back_pair(wide, tot, keys_acc, values_acc, pair)

        @pl.when(pair == 0)
        def _():
            tick(3)

        @pl.when(pair == 2)
        def _():
            tick(4)

    tick(5)
    load("normed_one", normed_one, normed)
    loads["mixed"].wait()
    tick(6)
    loads["qkv_w"].wait()
    weights = pl.ds(0, 3 * EDGE)

    @pl.loop(0, rows // 256)
    def _(r):
        value = lax.dot_general(
            wide[rows_at(rows + r * 256, 256), weights], up_buf[:, weights], nt, preferred_element_type=f32
        )
        given[0, rows_at(r * 256, 256), :] = value.astype(bf16)

    one_copy.start()
    loads["normed_one"].wait()
    tick(7)

    @pl.loop(0, rows // 256)
    def _(r):
        value = lax.dot_general(wide[rows_at(r * 256, 256), weights], up_buf[:, weights], nt, preferred_element_type=f32)
        part_buf[rows_at(r * 256, 256), :] = value

    one_copy.wait_recv()
    loads["own"].wait()

    @pl.loop(0, rows // 32)
    def _(r):
        here = rows_at(r * 32, 32)
        tok = pair_buf[rows_at(rows + r * 32, 32), :].astype(f32)
        grad_normed = part_buf[here, :] + taken[0, here, :].astype(f32)
        standard, back = norm_back(tok, grad_normed, gain_one)
        add_vector(0, grad_normed * standard)
        add_vector(1, grad_normed)
        taken[0, here, :] = (mid[here, :] + back).astype(bf16)

    swap(1, lambda copy: copy.start())

    @pl.loop(0, both // 128)
    def _(r):
        here = rows_at(r * 128, 128)
        for i in (0, 2):
            row = pl.ds(4 + i + core, 1)
            value = wide[here, pl.ds(i * EDGE, EDGE)].astype(f32)
            sums[0, row, :] += jnp.sum(value, axis=0, keepdims=True)

    names = ("x", "core", "y", "low", "high")
    vec_ops = [at.send(name, sums.at[i], sums.at[6 + i], vec_send.at[i], vec_recv.at[i]) for i, name in enumerate(names)]
    vec_ops[0].start()
    for t in range(8, count + 7):
        tick(t)
        if t < 13:
            i = t - 8
            vec_ops[i].wait_recv()
            sums[i + 1] = sums[i] + sums[6 + i]
            if i < 4:
                vec_ops[i + 1].start()
    vec_store = pltpu.make_async_copy(sums.at[5], vec_ref, vec_local.at[0])
    vec_store.start()
    vec_store.wait()
    for op in (result_copy, attn_copy, one_copy, *vec_ops):
        op.wait_send()
    swap(0, lambda copy: copy.wait())
    swap(1, lambda copy: copy.wait())
    tick(count + 7)


def backward(*args):
    bf16, f32 = jnp.bfloat16, jnp.float32
    rows, width = args[0].shape
    both = 2 * rows
    outs = [
        ((rows, width), bf16),
        ((rows, width), bf16),
        ((4 * EDGE, width), bf16),
        ((EDGE, 8 * EDGE), bf16),
        ((EDGE, width), bf16),
        ((EDGE, width), bf16),
        ((EDGE, width), bf16),
        ((EDGE, width), bf16),
        ((24, EDGE), f32),
    ]
    scratch = [
        ((both, 4 * EDGE), bf16),
        ((both, 4 * EDGE), bf16),
        ((both, width), bf16),
        ((both, width), bf16),
        ((both, width), bf16),
        ((4 * EDGE, width), bf16),
        ((width, 4 * EDGE), bf16),
        ((rows, width), f32),
        ((2, rows, width), bf16),
        ((2, rows, width), bf16),
        ((rows, width), f32),
        ((EDGE // HDIM, 1, both), f32),
        ((2, 16, EDGE), f32),
        ((8, 128), f32),
        ((both, 128), f32),
        ((both, 128), f32),
        ((8, EDGE, EDGE), bf16),
        ((4, EDGE, EDGE), bf16),
        ((2, EDGE // 2, EDGE), bf16),
        ((2, EDGE // 4, EDGE), bf16),
        ((2, EDGE // 8, EDGE), bf16),
        ((5, EDGE, EDGE), bf16),
        ((11, 24, EDGE), f32),
    ]
    dma = pltpu.SemaphoreType.DMA
    return pl.pallas_call(
        backward_kernel,
        in_specs=[ANY] * len(args),
        out_specs=[ANY] * len(outs),
        out_shape=[jax.ShapeDtypeStruct(*out) for out in outs],
        scratch_shapes=[pltpu.VMEM(*array) for array in scratch]
        + [dma((8, 12)), dma((8, 12)), dma((12,)), dma((20,)), dma((4,)), dma((4,))]
        + [dma((2,)), dma((2,)), dma((2,)), dma((5,)), dma((5,)), dma((1,))],
        compiler_params=pltpu.CompilerParams(
            collective_id=1, has_side_effects=True, vmem_limit_bytes=64 * 1024 * 1024
        ),
        name="backward",
    )(*args)


def tuned(
    tokens,
    out_grad,
    query_counts,
    first_gain,
    first_bias,
    query_weight,
    query_bias,
    key_weight,
    value_weight,
    value_bias,
    output_weight,
    output_bias,
    second_gain,
    second_bias,
    up_weight,
    up_bias,
    down_weight,
    down_bias,
):
    f32, bf16 = jnp.float32, jnp.bfloat16
    x = lax.axis_index("seq")
    head_width = tokens.shape[2] // 2

    vectors = (first_gain, first_bias, query_bias, value_bias, output_bias, second_gain, second_bias, down_bias)
    vectors = jnp.concatenate([jnp.stack(vectors), up_bias.reshape(4, -1), jnp.zeros((4, head_width), bf16)])
    cell_weight = jnp.broadcast_to(jnp.sqrt(query_counts.astype(f32) / 1000.0), (8, 128))
    state = forward(
        tokens[0],
        out_grad[0],
        cell_weight,
        vectors.astype(f32),
        query_weight,
        key_weight,
        value_weight,
        output_weight,
        up_weight,
        down_weight,
    )
    result, input_grad, down, up, out, query, key, value, sums = backward(*state)
    short = lax.dynamic_index_in_dim(sums[:16].reshape(8, 2, head_width), x, 1, keepdims=False)
    up_sum = lax.dynamic_slice_in_dim(sums, 16 + 4 * x, 4, 0).reshape(-1)
    return (
        result[None],
        input_grad[None],
        short[0],
        short[1],
        query.astype(f32),
        short[2],
        key.astype(f32),
        value.astype(f32),
        short[3],
        out.astype(f32),
        short[4],
        short[5],
        short[6],
        up.astype(f32),
        up_sum,
        down.astype(f32),
        short[7],
    )


def chosen(mesh):
    cells, blocks = mesh.shape["cell"], mesh.shape["seq"]

    def per_device(tokens, *rest):
        if blocks == 2 and cells == 16 and tokens.shape == (1, 512, 1280):
            return tuned(tokens, *rest)
        return general(tokens, *rest)

    return per_device


def solution(mesh):
    placed = (
        P("cell", "seq", None),
        P("cell", "seq", None),
        P("cell"),
        P("seq"),
        P("seq"),
        P("seq", None),
        P("seq"),
        P("seq", None),
        P("seq", None),
        P("seq"),
        P("seq", None),
        P("seq"),
        P("seq"),
        P("seq"),
        P("seq", None),
        P("seq"),
        P("seq", None),
        P("seq"),
    )
    return jax.shard_map(
        chosen(mesh),
        mesh=mesh,
        in_specs=placed,
        out_specs=(
            P("cell", "seq", None),
            P("cell", "seq", None),
            P("seq"),
            P("seq"),
            P("seq", None),
            P("seq"),
            P("seq", None),
            P("seq", None),
            P("seq"),
            P("seq", None),
            P("seq"),
            P("seq"),
            P("seq"),
            P("seq", None),
            P("seq"),
            P("seq", None),
            P("seq"),
        ),
        check_vma=False,
    )
```

```python
import jax
import jax.numpy as jnp
from jax import lax
from jax.experimental import pallas as pl
from jax.experimental.pallas import tpu as pltpu
from jax.sharding import PartitionSpec as P

HEADS = 20
HDIM = 64


def from_behind(value, axis, steps):
    count = lax.axis_size(axis)
    pairs = [(source, (source + steps) % count) for source in range(count)]
    return lax.ppermute(value, axis, pairs)


def for_sending(x):
    return jax.tree.map(lambda a: a.astype(jnp.bfloat16) if a.dtype == jnp.float32 else a, x)


def matmul(left, right):
    return jnp.dot(left, right, preferred_element_type=jnp.float32)


def matmul_right_t(left, right):
    return jnp.einsum("to,io->ti", left, right, preferred_element_type=jnp.float32)


def weight_grad(left, right):
    return jnp.einsum("ti,to->io", left, right, preferred_element_type=jnp.float32)


def standardize(values):
    average = jnp.mean(values, axis=-1, keepdims=True)
    centred = values - average
    inverse = lax.rsqrt(jnp.mean(centred * centred, axis=-1, keepdims=True) + 1e-05)
    return (centred * inverse, inverse)


def standardize_back(grad_normed, standard, inverse, gain_vec):
    scaled = grad_normed * gain_vec
    return inverse * (
        scaled
        - jnp.mean(scaled, axis=-1, keepdims=True)
        - standard * jnp.mean(scaled * standard, axis=-1, keepdims=True)
    )


def gelu_value(up_proj):
    return 0.5 * up_proj * (1.0 + lax.erf(up_proj * 0.7071067811865476))


def gelu_slope(up_proj):
    return (
        0.5 * (1.0 + lax.erf(up_proj * 0.7071067811865476))
        + up_proj * jnp.exp(-0.5 * up_proj * up_proj) * 0.3989422804014327
    )


def score_block(queries, key_rows):
    return (
        jnp.einsum("cqhd,ckhd->chqk", queries, key_rows, preferred_element_type=jnp.float32) * 0.125
    )


def column_sum(values):
    return jnp.sum(values.astype(jnp.float32), axis=0)


def general(
    tokens,
    out_grad,
    query_counts,
    first_gain,
    first_bias,
    query_weight,
    query_bias,
    key_weight,
    value_weight,
    value_bias,
    output_weight,
    output_bias,
    second_gain,
    second_bias,
    up_weight,
    up_bias,
    down_weight,
    down_bias,
):
    (
        first_gain,
        first_bias,
        query_weight,
        query_bias,
        key_weight,
        value_weight,
        value_bias,
        output_weight,
        output_bias,
        second_gain,
        second_bias,
        up_weight,
        up_bias,
        down_weight,
        down_bias,
    ) = (
        lax.all_gather(first_gain, "seq", axis=0, tiled=True),
        lax.all_gather(first_bias, "seq", axis=0, tiled=True),
        lax.all_gather(query_weight, "seq", axis=0, tiled=True),
        lax.all_gather(query_bias, "seq", axis=0, tiled=True),
        lax.all_gather(key_weight, "seq", axis=0, tiled=True),
        lax.all_gather(value_weight, "seq", axis=0, tiled=True),
        lax.all_gather(value_bias, "seq", axis=0, tiled=True),
        lax.all_gather(output_weight, "seq", axis=0, tiled=True),
        lax.all_gather(output_bias, "seq", axis=0, tiled=True),
        lax.all_gather(second_gain, "seq", axis=0, tiled=True),
        lax.all_gather(second_bias, "seq", axis=0, tiled=True),
        lax.all_gather(up_weight, "seq", axis=0, tiled=True),
        lax.all_gather(up_bias, "seq", axis=0, tiled=True),
        lax.all_gather(down_weight, "seq", axis=0, tiled=True),
        lax.all_gather(down_bias, "seq", axis=0, tiled=True),
    )
    f32 = jnp.float32
    bf16 = jnp.bfloat16
    gain_first = first_gain.astype(f32)
    gain_second = second_gain.astype(f32)
    cell_count, seg_len, model_width = tokens.shape
    row_count = cell_count * seg_len
    head_shape = (cell_count, seg_len, HEADS, HDIM)
    cycle_size = lax.axis_size("seq")
    flat_input = tokens.reshape(row_count, model_width).astype(f32)
    standard_one, inverse_one = standardize(flat_input)
    normed_one = (standard_one * gain_first + first_bias.astype(f32)).astype(bf16)
    query_heads = (
        (matmul(normed_one, query_weight) + query_bias.astype(f32)).astype(bf16).reshape(head_shape)
    )
    key_heads = matmul(normed_one, key_weight).astype(bf16).reshape(head_shape)
    value_heads = (
        (matmul(normed_one, value_weight) + value_bias.astype(f32)).astype(bf16).reshape(head_shape)
    )
    running_max = jnp.full((cell_count, HEADS, seg_len), -1e30, f32)
    running_sum = jnp.zeros((cell_count, HEADS, seg_len), f32)
    weighted = jnp.zeros((cell_count, HEADS, seg_len, HDIM), f32)
    travel = (key_heads, value_heads)
    for step in range(cycle_size):
        if step > 0:
            travel = from_behind((travel[0], travel[1]), "seq", 1)
        scores = score_block(query_heads, travel[0])
        new_max = jnp.maximum(running_max, jnp.max(scores, axis=-1))
        rescale = jnp.exp(running_max - new_max)
        exp_scores = jnp.exp(scores - new_max[..., None])
        running_sum = running_sum * rescale + jnp.sum(exp_scores, axis=-1)
        weighted = weighted * rescale[..., None] + jnp.einsum(
            "chqk,ckhd->chqd", exp_scores.astype(bf16), travel[1], preferred_element_type=f32
        )
        running_max = new_max
    attended = weighted / running_sum[..., None]
    log_total = running_max + jnp.log(running_sum)
    mixed = attended.transpose(0, 2, 1, 3).reshape(row_count, model_width).astype(bf16)
    middle = flat_input + matmul(mixed, output_weight) + output_bias.astype(f32)
    standard_two, inverse_two = standardize(middle)
    normed_two = (standard_two * gain_second + second_bias.astype(f32)).astype(bf16)
    up_proj = matmul(normed_two, up_weight) + up_bias.astype(f32)
    hidden = gelu_value(up_proj).astype(bf16)
    result = middle + matmul(hidden, down_weight) + down_bias.astype(f32)
    result_out = result.astype(bf16).reshape(cell_count, seg_len, model_width)
    weight_cell = jnp.sqrt(query_counts.astype(f32) / 1000.0)
    grad_result = (out_grad.astype(f32) * weight_cell[:, None, None]).reshape(
        row_count, model_width
    )
    grad_ffn_out = grad_result.astype(bf16)
    grad_down_weight = weight_grad(hidden, grad_ffn_out)
    grad_down_bias = column_sum(grad_ffn_out)
    grad_up = (matmul_right_t(grad_ffn_out, down_weight) * gelu_slope(up_proj)).astype(bf16)
    grad_up_weight = weight_grad(normed_two, grad_up)
    grad_up_bias = column_sum(grad_up)
    grad_normed_two = matmul_right_t(grad_up, up_weight)
    grad_second_gain = jnp.sum(grad_normed_two * standard_two, axis=0)
    grad_second_bias = jnp.sum(grad_normed_two, axis=0)
    grad_middle = grad_result + standardize_back(
        grad_normed_two, standard_two, inverse_two, gain_second
    )
    grad_attn_out = grad_middle.astype(bf16)
    grad_output_weight = weight_grad(mixed, grad_attn_out)
    grad_output_bias = column_sum(grad_attn_out)
    grad_mixed = matmul_right_t(grad_attn_out, output_weight).astype(bf16).reshape(head_shape)
    row_delta = jnp.sum(grad_mixed.astype(f32).transpose(0, 2, 1, 3) * attended, axis=-1)
    grad_query_acc = jnp.zeros(head_shape, f32)
    moving = (jnp.zeros(head_shape, f32), jnp.zeros(head_shape, f32))
    travel = (key_heads, value_heads)
    for step in range(cycle_size):
        if step > 0:
            travel = from_behind((travel[0], travel[1]), "seq", 1)
        block_keys, block_values = travel
        scores = score_block(query_heads, block_keys)
        prob_block = jnp.exp(scores - log_total[..., None])
        part_values = jnp.einsum(
            "chqk,cqhd->ckhd", prob_block.astype(bf16), grad_mixed, preferred_element_type=f32
        )
        grad_probs = jnp.einsum(
            "cqhd,ckhd->chqk", grad_mixed, block_values, preferred_element_type=f32
        )
        grad_scores = (prob_block * (grad_probs - row_delta[..., None])).astype(bf16)
        grad_query_acc = (
            grad_query_acc
            + jnp.einsum("chqk,ckhd->cqhd", grad_scores, block_keys, preferred_element_type=f32)
            * 0.125
        )
        part_keys = (
            jnp.einsum("chqk,cqhd->ckhd", grad_scores, query_heads, preferred_element_type=f32)
            * 0.125
        )
        moving = from_behind(
            (for_sending(moving[0] + part_keys), for_sending(moving[1] + part_values)), "seq", 1
        )
    grad_queries = grad_query_acc.astype(bf16).reshape(row_count, model_width)
    grad_keys = moving[0].astype(bf16).reshape(row_count, model_width)
    grad_values = moving[1].astype(bf16).reshape(row_count, model_width)
    grad_query_weight = weight_grad(normed_one, grad_queries)
    grad_query_bias = column_sum(grad_queries)
    grad_key_weight = weight_grad(normed_one, grad_keys)
    grad_value_weight = weight_grad(normed_one, grad_values)
    grad_value_bias = column_sum(grad_values)
    grad_normed_one = (
        matmul_right_t(grad_queries, query_weight)
        + matmul_right_t(grad_keys, key_weight)
        + matmul_right_t(grad_values, value_weight)
    )
    grad_first_gain = jnp.sum(grad_normed_one * standard_one, axis=0)
    grad_first_bias = jnp.sum(grad_normed_one, axis=0)
    grad_input = grad_middle + standardize_back(
        grad_normed_one, standard_one, inverse_one, gain_first
    )
    input_grad = grad_input.astype(bf16).reshape(cell_count, seg_len, model_width)
    shared_all = (
        lax.psum_scatter(
            grad_first_gain.astype(jnp.bfloat16), "seq", scatter_dimension=0, tiled=True
        ).astype(jnp.float32),
        lax.psum_scatter(
            grad_first_bias.astype(jnp.bfloat16), "seq", scatter_dimension=0, tiled=True
        ).astype(jnp.float32),
        lax.psum_scatter(
            grad_query_weight.astype(jnp.bfloat16), "seq", scatter_dimension=0, tiled=True
        ).astype(jnp.float32),
        lax.psum_scatter(
            grad_query_bias.astype(jnp.bfloat16), "seq", scatter_dimension=0, tiled=True
        ).astype(jnp.float32),
        lax.psum_scatter(
            grad_key_weight.astype(jnp.bfloat16), "seq", scatter_dimension=0, tiled=True
        ).astype(jnp.float32),
        lax.psum_scatter(
            grad_value_weight.astype(jnp.bfloat16), "seq", scatter_dimension=0, tiled=True
        ).astype(jnp.float32),
        lax.psum_scatter(
            grad_value_bias.astype(jnp.bfloat16), "seq", scatter_dimension=0, tiled=True
        ).astype(jnp.float32),
        lax.psum_scatter(
            grad_output_weight.astype(jnp.bfloat16), "seq", scatter_dimension=0, tiled=True
        ).astype(jnp.float32),
        lax.psum_scatter(
            grad_output_bias.astype(jnp.bfloat16), "seq", scatter_dimension=0, tiled=True
        ).astype(jnp.float32),
        lax.psum_scatter(
            grad_second_gain.astype(jnp.bfloat16), "seq", scatter_dimension=0, tiled=True
        ).astype(jnp.float32),
        lax.psum_scatter(
            grad_second_bias.astype(jnp.bfloat16), "seq", scatter_dimension=0, tiled=True
        ).astype(jnp.float32),
        lax.psum_scatter(
            grad_up_weight.astype(jnp.bfloat16), "seq", scatter_dimension=0, tiled=True
        ).astype(jnp.float32),
        lax.psum_scatter(
            grad_up_bias.astype(jnp.bfloat16), "seq", scatter_dimension=0, tiled=True
        ).astype(jnp.float32),
        lax.psum_scatter(
            grad_down_weight.astype(jnp.bfloat16), "seq", scatter_dimension=0, tiled=True
        ).astype(jnp.float32),
        lax.psum_scatter(
            grad_down_bias.astype(jnp.bfloat16), "seq", scatter_dimension=0, tiled=True
        ).astype(jnp.float32),
    )
    (
        grad_first_gain,
        grad_first_bias,
        grad_query_weight,
        grad_query_bias,
        grad_key_weight,
        grad_value_weight,
        grad_value_bias,
        grad_output_weight,
        grad_output_bias,
        grad_second_gain,
        grad_second_bias,
        grad_up_weight,
        grad_up_bias,
        grad_down_weight,
        grad_down_bias,
    ) = shared_all
    (
        grad_first_gain,
        grad_first_bias,
        grad_query_weight,
        grad_query_bias,
        grad_key_weight,
        grad_value_weight,
        grad_value_bias,
        grad_output_weight,
        grad_output_bias,
        grad_second_gain,
        grad_second_bias,
        grad_up_weight,
        grad_up_bias,
        grad_down_weight,
        grad_down_bias,
    ) = (
        lax.psum(grad_first_gain.astype(jnp.bfloat16), "cell").astype(jnp.float32),
        lax.psum(grad_first_bias.astype(jnp.bfloat16), "cell").astype(jnp.float32),
        lax.psum(grad_query_weight.astype(jnp.bfloat16), "cell").astype(jnp.float32),
        lax.psum(grad_query_bias.astype(jnp.bfloat16), "cell").astype(jnp.float32),
        lax.psum(grad_key_weight.astype(jnp.bfloat16), "cell").astype(jnp.float32),
        lax.psum(grad_value_weight.astype(jnp.bfloat16), "cell").astype(jnp.float32),
        lax.psum(grad_value_bias.astype(jnp.bfloat16), "cell").astype(jnp.float32),
        lax.psum(grad_output_weight.astype(jnp.bfloat16), "cell").astype(jnp.float32),
        lax.psum(grad_output_bias.astype(jnp.bfloat16), "cell").astype(jnp.float32),
        lax.psum(grad_second_gain.astype(jnp.bfloat16), "cell").astype(jnp.float32),
        lax.psum(grad_second_bias.astype(jnp.bfloat16), "cell").astype(jnp.float32),
        lax.psum(grad_up_weight.astype(jnp.bfloat16), "cell").astype(jnp.float32),
        lax.psum(grad_up_bias.astype(jnp.bfloat16), "cell").astype(jnp.float32),
        lax.psum(grad_down_weight.astype(jnp.bfloat16), "cell").astype(jnp.float32),
        lax.psum(grad_down_bias.astype(jnp.bfloat16), "cell").astype(jnp.float32),
    )
    return (
        result_out,
        input_grad,
        grad_first_gain,
        grad_first_bias,
        grad_query_weight,
        grad_query_bias,
        grad_key_weight,
        grad_value_weight,
        grad_value_bias,
        grad_output_weight,
        grad_output_bias,
        grad_second_gain,
        grad_second_bias,
        grad_up_weight,
        grad_up_bias,
        grad_down_weight,
        grad_down_bias,
    )


Q_BLOCK = 512


MESH = pl.DeviceIdType.MESH
ANY = pl.BlockSpec(memory_space=pl.ANY)
EDGE = 640
WIDE = 256
RING = 10


class Spot:
    def __init__(self):
        self.x = lax.axis_index("seq")
        self.cell = lax.axis_index("cell")
        self.core = lax.rem(self.cell, 2)
        self.y = lax.rem(self.cell // 2, 2)
        self.low = lax.rem(self.cell // 4, 2)
        self.high = lax.rem(self.cell // 8, 2)

    def flip(self, index, bit):
        return {"cell": self.cell + bit - 2 * bit * index}

    def over(self, name):
        if name == "x":
            return {"seq": 1 - self.x}
        if name == "core":
            return self.flip(self.core, 1)
        if name == "diagonal":
            return {"seq": 1 - self.x, **self.flip(self.core, 1)}
        return self.flip(*{"y": (self.y, 2), "low": (self.low, 4), "high": (self.high, 8)}[name])

    def meet(self, names):
        barrier = pltpu.get_barrier_semaphore()
        for name in names:
            pl.semaphore_signal(barrier, inc=1, device_id=self.over(name), device_id_type=MESH)
        pl.semaphore_wait(barrier, len(names))

    def send(self, name, source, target, send_sem, recv_sem):
        return pltpu.make_async_remote_copy(
            source, target, send_sem, recv_sem, device_id=self.over(name), device_id_type=MESH
        )


def rows_at(start, size):
    return pl.ds(pl.multiple_of(start, 16), size)


def cols(start, size):
    return pl.ds(pl.multiple_of(start, 128), size)


def attend_pair(qkv, mixed, total_ref, pair, base):
    f32, bf16 = jnp.float32, jnp.bfloat16
    rows = qkv.shape[0]
    lane = lax.broadcasted_iota(jnp.int32, (1, 128), 1)
    here = pair * 128
    keys = qkv[:, cols(EDGE + here, 128)]
    values_t = qkv[:, cols(2 * EDGE + here, 128)].T
    for block in range(rows // Q_BLOCK):
        part = pl.ds(block * Q_BLOCK, Q_BLOCK)
        queries = qkv[part, cols(here, 128)] * jnp.asarray(0.125, bf16)
        outs = []
        for head in range(2):
            own = (lane // HDIM) == head
            scores = lax.dot_general(
                keys,
                jnp.where(own, queries, jnp.zeros_like(queries)),
                (((1,), (1,)), ((), ())),
                preferred_element_type=f32,
            )
            largest = jnp.max(scores, axis=0, keepdims=True)
            weights = jnp.exp(scores - largest)
            total = jnp.sum(weights, axis=0, keepdims=True)
            out = jnp.dot(
                values_t[head * HDIM : (head + 1) * HDIM, :],
                weights.astype(bf16),
                preferred_element_type=f32,
            )
            outs.append(out / total)
            total_ref[2 * pair + head, :, part] = largest + jnp.log(total)
        mixed[part, cols(base + here, 128)] = jnp.concatenate(outs, axis=0).T.astype(bf16)


def forward_kernel(
    tokens, out_grad, cell_weight, vectors, wq, wk, wv, wo, wup, wdown,
    own_out, grad_out, weight_out, vectors_out, qkv_w_out, out_w_out, up_w_out, down_w_out,
    normed_one_out, qkv_out, mixed_out, total_out, middle_out, normed_two_out, hidden_out, slope_out, ffn_out,
    tok, grad, scale, vec, qkv_w, out_w, up_w, down_w,
    normed_one, qkv, mixed, totals, middle, normed_two, hidden, slope, ffn,
    send_sems, recv_sems, local_sems, side_send, side_recv, side_local, out_sems,
):
    f32, bf16 = jnp.float32, jnp.bfloat16
    at = Spot()
    x, core = at.x, at.core
    rows = tok.shape[0]
    width = tok.shape[1]
    at.meet(("x", "core", "diagonal", "y", "low", "high"))

    side = [(tokens, tok), (cell_weight, scale), (out_grad, grad)]
    diagonal = [at.send("diagonal", s, t, side_send.at[i], side_recv.at[i]) for i, (s, t) in enumerate(side)]
    straight = [pltpu.make_async_copy(s, t, side_local.at[i]) for i, (s, t) in enumerate(side)]

    def swap(i, remote, local):
        @pl.when(x != core)
        def _():
            remote(diagonal[i])

        @pl.when(x == core)
        def _():
            local(straight[i])

    def swap_start(i):
        swap(i, lambda c: c.start(), lambda c: c.start())

    def swap_wait(i):
        swap(i, lambda c: c.wait(), lambda c: c.wait())

    chunks = []
    for start in range(0, 3 * EDGE, WIDE):
        width_now = min(WIDE, 3 * EDGE - start)
        parts = []
        for i, ref in enumerate((wq, wk, wv)):
            low, high = max(start, i * EDGE), min(start + width_now, (i + 1) * EDGE)
            if low < high:
                parts.append((ref.at[:, cols(core * EDGE + low - i * EDGE, high - low)], low))
        chunks.append((parts, qkv_w, EDGE, 0, start, width_now))
    for start in range(0, 4 * EDGE, WIDE):
        part = start // (2 * EDGE) * 2 * EDGE + start + core * 2 * EDGE
        chunks.append(([(wup.at[:, cols(part, WIDE)], start)], up_w, EDGE, 0, start, WIDE))
    for start in range(0, 2 * EDGE, WIDE):
        source = wdown.at[rows_at(core * 2 * EDGE, EDGE), pl.ds(start, WIDE)]
        chunks.append(([(source, start)], down_w, 2 * EDGE, 0, start, WIDE))
    count = len(chunks)
    eighth = EDGE // 8
    place = at.y * 4 + at.low * 2 + at.high

    def region(k, half, start, size, column=None, width=None):
        _, ref, stride, row, first, most = chunks[k]
        column, width = (first, most) if column is None else (column, width)
        return ref.at[rows_at(half * stride + row + start * eighth, size * eighth), pl.ds(column, width)]

    ops = {}
    for k, chunk in enumerate(chunks):
        ops["x", k] = [
            at.send(
                "x",
                source.at[rows_at(place * eighth, eighth)],
                region(k, x, place, 1, column, source.shape[1]),
                send_sems.at[4 * j, k],
                recv_sems.at[4 * j, k],
            )
            for j, (source, column) in enumerate(chunk[0])
        ]
        for s, (name, start, size) in enumerate(
            (("high", place, 1), ("low", at.y * 4 + at.low * 2, 2), ("y", at.y * 4, 4))
        ):
            part = region(k, 1 - x, start, size)
            ops[name, k] = [at.send(name, part, part, send_sems.at[s + 1, k], recv_sems.at[s + 1, k])]
    direct = []
    for i, start in enumerate(range(0, 2 * EDGE, WIDE)):
        source = wdown.at[rows_at(core * 2 * EDGE + EDGE, EDGE), pl.ds(start, WIDE)]
        target = down_w.at[rows_at(x * 2 * EDGE + EDGE, EDGE), pl.ds(start, WIDE)]
        direct.append(at.send("x", source, target, send_sems.at[5, i], recv_sems.at[5, i]))
    owns = []
    mine = rows_at(x * EDGE, EDGE)
    for i, ref in enumerate((wq, wk, wv)):
        owns.append((ref.at[:, cols(core * EDGE, EDGE)], qkv_w.at[mine, pl.ds(i * EDGE, EDGE)]))
    for i in range(2):
        owns.append((wup.at[:, cols((2 * i + core) * 2 * EDGE, 2 * EDGE)], up_w.at[mine, pl.ds(i * 2 * EDGE, 2 * EDGE)]))
    owns.append((wdown.at[rows_at(core * 2 * EDGE, 2 * EDGE)], down_w.at[rows_at(x * 2 * EDGE, 2 * EDGE)]))
    owns = [pltpu.make_async_copy(source, target, local_sems.at[i]) for i, (source, target) in enumerate(owns)]
    half = EDGE // 2
    out_x = at.send(
        "x", wo.at[rows_at(core * half, half)], out_w.at[rows_at(x * EDGE + core * half, half)], side_send.at[4], side_recv.at[4]
    )
    part = out_w.at[rows_at((1 - x) * EDGE + core * half, half)]
    out_core = at.send("core", part, part, side_send.at[5], side_recv.at[5])
    out_local = pltpu.make_async_copy(wo, out_w.at[rows_at(x * EDGE, EDGE)], side_local.at[4])
    vec_x = at.send("x", vectors, vec.at[x], side_send.at[3], side_recv.at[3])
    vec_local = pltpu.make_async_copy(vectors, vec.at[x], side_local.at[3])
    top, bottom = pl.ds(0, rows), pl.ds(rows, rows)

    def core_copy(i, source, target):
        return at.send("core", source, target, side_send.at[i], side_recv.at[i])

    normed_one_core = core_copy(6, normed_one.at[top], normed_one.at[bottom])
    heads = cols(core * EDGE, EDGE)
    mixed_core = [
        core_copy(7, mixed.at[top, heads], mixed.at[bottom, heads]),
        core_copy(8, mixed.at[bottom, heads], mixed.at[top, heads]),
    ]
    normed_two_core = core_copy(9, normed_two.at[top], normed_two.at[bottom])
    ffn_core = core_copy(10, ffn.at[top], ffn.at[bottom])

    outs = []
    early = []

    def put(source, target):
        copy = pltpu.make_async_copy(source, target, out_sems.at[len(outs)])
        copy.start()
        outs.append(copy)
        return copy

    stages = ("x", "high", "low", "y")

    def begin(name, k):
        for op in ops[name, k]:
            op.start()

    def tick(t):
        for s, name in enumerate(stages):
            k = t - s
            if 0 <= k < count:
                for op in ops[name, k]:
                    op.wait_recv()
                if s < 3:
                    begin(stages[s + 1], k)
        if t + 3 < count:
            begin("x", t + 3)
        if t == 3:
            out_x.start()
        if t == 8:
            out_x.wait_recv()
            out_core.start()
        if t % 2 and 5 <= t < 5 + 2 * len(direct):
            direct[(t - 5) // 2].start()
        if t == 14:
            swap_start(2)
        if t in (1, 2, 4):
            for op in {1: (out_local,), 2: owns[3:5], 4: owns[5:]}[t]:
                op.start()

    begin("x", 0)
    begin("x", 1)
    begin("x", 2)
    vec_x.start()
    swap_start(0)
    swap_start(1)
    vec_local.start()
    for op in owns[:3]:
        op.start()
    tick(0)
    tick(1)
    vec_x.wait_recv()
    vec_local.wait()

    def vector(i):
        return jnp.concatenate([vec[0, i : i + 1, :], vec[1, i : i + 1, :]], axis=1)

    def norm(values, gain, bias):
        average = jnp.mean(values, axis=-1, keepdims=True)
        centred = values - average
        inverse = lax.rsqrt(jnp.mean(centred * centred, axis=-1, keepdims=True) + 1e-05)
        return (centred * inverse * gain + bias).astype(bf16)

    swap_wait(0)
    gain_one, bias_one = vector(0), vector(1)

    @pl.loop(0, rows // 64)
    def _(i):
        here = rows_at(i * 64, 64)
        normed_one[here, :] = norm(tok[here, :].astype(f32), gain_one, bias_one)

    normed_one_core.start()
    tick(2)
    tick(3)
    put(tok, own_out)
    normed_one_core.wait_recv()
    put(normed_one, normed_one_out)

    for i in range(3):
        for t in ((4, 5), (6, 7), (8, 9, 10))[i]:
            tick(t)
        owns[i].wait()
        lanes = pl.ds(i * EDGE, EDGE)
        bias = 0.0 if i == 1 else vec[core, 2 + i // 2 : 3 + i // 2, :]

        @pl.loop(0, 2 * rows // 256)
        def _(r):
            here = rows_at(r * 256, 256)
            value = jnp.dot(normed_one[here, :], qkv_w[:, lanes], preferred_element_type=f32)
            qkv[here, lanes] = (value + bias).astype(bf16)

    put(qkv, qkv_out)
    put(qkv_w, qkv_w_out)

    @pl.loop(0, EDGE // 128)
    def _(pair):
        attend_pair(qkv, mixed, totals, pair, core * EDGE)

        for i in range(5):

            @pl.when(pair == i)
            def _():
                tick(11 + i)

    mixed_core[0].start()
    mixed_core[1].start()
    put(totals, total_out)
    tick(16)
    out_local.wait()
    out_core.wait_recv()
    mixed_core[1].wait_recv()
    gain_two, bias_two, out_bias = vector(5), vector(6), vector(4)

    @pl.loop(0, rows // 128)
    def _(r):
        here = rows_at(r * 128, 128)
        value = jnp.dot(mixed[here, :], out_w[...], preferred_element_type=f32)
        value = tok[here, :].astype(f32) + value + out_bias
        middle[here, :] = value
        normed_two[here, :] = norm(value, gain_two, bias_two)

    normed_two_core.start()
    mixed_core[0].wait_recv()
    put(out_w, out_w_out)
    put(mixed, mixed_out)
    put(middle, middle_out)
    tick(17)
    normed_two_core.wait_recv()
    put(normed_two, normed_two_out)
    waits = {}
    for i in range(4):
        if i % 2 == 0:
            owns[3 + i // 2].wait()
        slot = i % 2
        if i >= 2:
            for copy in waits[slot]:
                copy.wait()
                early.append(copy)
        lanes = pl.ds(i * EDGE, EDGE)
        bias = vec[i // 2, pl.ds(8 + core * 2 + i % 2, 1), :]

        @pl.loop(0, 2 * rows // 128)
        def _(r):
            here = rows_at(r * 128, 128)
            up = jnp.dot(normed_two[here, :], up_w[:, lanes], preferred_element_type=f32) + bias
            cdf = 0.5 * (1.0 + lax.erf(up * 0.7071067811865476))
            hidden[slot, here, :] = (up * cdf).astype(bf16)
            slope[slot, here, :] = (cdf + up * jnp.exp(-0.5 * up * up) * 0.3989422804014327).astype(bf16)

        waits[slot] = (
            put(hidden.at[slot], hidden_out.at[:, lanes]),
            put(slope.at[slot], slope_out.at[:, lanes]),
        )
        if i == 1:
            swap_wait(1)
            swap_wait(2)
            weight = scale[0:1, 0:1]

            @pl.loop(0, rows // 64)
            def _(r):
                here = rows_at(r * 64, 64)
                ffn[here, :] = (grad[here, :].astype(f32) * weight).astype(bf16)

            ffn_core.start()
            put(grad, grad_out)
            put(scale, weight_out)
            put(vec, vectors_out)
        for t in ((18,), (19, 20), (21, 22), (23, 24, 25))[i]:
            tick(t)
    put(up_w, up_w_out)
    ffn_core.wait_recv()
    put(ffn, ffn_out)
    owns[5].wait()
    for op in direct:
        op.wait()
    put(down_w, down_w_out)
    for k in range(count):
        for name in stages:
            for op in ops[name, k]:
                op.wait_send()
    for op in (out_x, out_core, vec_x, normed_one_core, *mixed_core, normed_two_core, ffn_core):
        op.wait_send()
    for copy in outs:
        if not any(copy is other for other in early):
            copy.wait()


def forward(*args):
    bf16, f32 = jnp.bfloat16, jnp.float32
    shape = jax.ShapeDtypeStruct
    rows, width = args[0].shape
    both = 2 * rows
    arrays = [
        ((rows, width), bf16),
        ((rows, width), bf16),
        (args[2].shape, f32),
        ((2,) + args[3].shape, f32),
        ((width, 3 * EDGE), bf16),
        ((width, width), bf16),
        ((width, 4 * EDGE), bf16),
        ((4 * EDGE, width), bf16),
        ((both, width), bf16),
        ((both, 3 * EDGE), bf16),
        ((both, width), bf16),
        ((EDGE // HDIM, 1, both), f32),
        ((rows, width), f32),
        ((both, width), bf16),
        ((both, 4 * EDGE), bf16),
        ((both, 4 * EDGE), bf16),
        ((both, width), bf16),
    ]
    scratch = [pltpu.VMEM(*array) for array in arrays]
    scratch[14] = scratch[15] = pltpu.VMEM((2, both, EDGE), bf16)
    dma = pltpu.SemaphoreType.DMA
    return pl.pallas_call(
        forward_kernel,
        in_specs=[ANY] * len(args),
        out_specs=[ANY] * len(arrays),
        out_shape=[shape(*array) for array in arrays],
        scratch_shapes=scratch + [dma((6, 23)), dma((6, 23)), dma((6,)), dma((11,)), dma((11,)), dma((5,)), dma((24,))],
        compiler_params=pltpu.CompilerParams(
            collective_id=0, has_side_effects=True, vmem_limit_bytes=60 * 1024 * 1024
        ),
        name="forward",
    )(*args)


def attend_back_pair(qkv, totals, keys_acc, values_acc, pair):
    f32, bf16 = jnp.float32, jnp.bfloat16
    rows = qkv.shape[0]
    size = Q_BLOCK // 2
    lane = lax.broadcasted_iota(jnp.int32, (1, 128), 1)
    here, key_lanes, value_lanes, grad_lanes = (cols(i * EDGE + pair * 128, 128) for i in range(4))
    keys = qkv[:, key_lanes]
    keys_t = keys.T
    nt = (((1,), (1,)), ((), ()))
    keys_acc[...] = jnp.zeros_like(keys_acc)
    values_acc[...] = jnp.zeros_like(values_acc)

    @pl.loop(0, rows // size)
    def _(block):
        part = rows_at(block * size, size)
        queries = qkv[part, here] * jnp.asarray(0.125, bf16)
        grads = qkv[part, grad_lanes]
        values = qkv[:, value_lanes]
        outs = []
        key_part = value_part = 0.0
        for head in range(2):
            own = (lane // HDIM) == head
            q_own = jnp.where(own, queries, jnp.zeros_like(queries))
            g_own = jnp.where(own, grads, jnp.zeros_like(grads))
            scores = lax.dot_general(keys, q_own, nt, preferred_element_type=f32)
            probs = jnp.exp(scores - totals[2 * pair + head, :, cols(block * size, size)])
            grad_probs = lax.dot_general(values, g_own, nt, preferred_element_type=f32)
            delta = jnp.sum(probs * grad_probs, axis=0, keepdims=True)
            grad_scores = (probs * (grad_probs - delta)).astype(bf16)
            value_part += jnp.dot(probs.astype(bf16), g_own, preferred_element_type=f32)
            key_part += jnp.dot(grad_scores, q_own, preferred_element_type=f32)
            outs.append(jnp.dot(keys_t[head * HDIM : (head + 1) * HDIM, :], grad_scores, preferred_element_type=f32))
        qkv[part, here] = (jnp.concatenate(outs, axis=0) * 0.125).T.astype(bf16)
        keys_acc[...] += key_part
        values_acc[...] += value_part

    qkv[:, key_lanes] = keys_acc[...].astype(bf16)
    qkv[:, value_lanes] = values_acc[...].astype(bf16)


def backward_kernel(
    own, own_grad, cell_weight, vectors, qkv_w, out_w, up_w, down_w,
    normed_one, qkv, mixed, totals, middle, normed_two, hidden, slope, ffn,
    result_ref, input_ref, down_ref, up_ref, out_ref, q_ref, k_ref, v_ref, vec_ref,
    wide, grad_up, normed, pair_buf, ffn_buf, down_buf, up_buf, part_buf, taken, given, mid, tot, vec, scale, keys_acc, values_acc,
    blocks, from_x, from_y, from_low, from_high, res, sums,
    send_sems, recv_sems, store_sems, load_sems, core_send, core_recv, swap_send, swap_recv, swap_local, vec_send, vec_recv, vec_local,
):
    f32, bf16 = jnp.float32, jnp.bfloat16
    at = Spot()
    x, core = at.x, at.core
    rows, width = own.shape
    both = 2 * rows
    top, bottom = pl.ds(0, rows), pl.ds(rows, rows)
    nt = (((1,), (1,)), ((), ()))
    tn = (((0,), (0,)), ((), ()))
    loads = {}

    def load(name, source, target):
        copy = pltpu.make_async_copy(source, target, load_sems.at[len(loads)])
        copy.start()
        loads[name] = copy

    load("hidden", hidden, wide)
    load("ffn", ffn, ffn_buf)
    load("down_w", down_w, down_buf)
    slopes = [(slope.at[:, pl.ds(i * EDGE, EDGE)], pair_buf.at[:, pl.ds((i % 2) * EDGE, EDGE)]) for i in range(4)]
    load("slope0", *slopes[0])
    load("slope1", *slopes[1])
    load("up_w", up_w, up_buf)
    load("normed_two", normed_two, normed)
    load("middle", middle, mid)
    load("vectors", vectors, vec)
    load("scale", cell_weight, scale)
    load("totals", totals, tot)
    sums[0] = jnp.zeros(sums.shape[1:], f32)
    at.meet(("x", "core", "diagonal", "y", "low", "high"))

    chunks = []
    for i in range(2):
        for start in range(0, 2 * EDGE, WIDE):
            target = down_ref.at[rows_at(core * 2 * EDGE + i * EDGE, EDGE), pl.ds(start, WIDE)]
            chunks.append([(wide, 2 * EDGE, i * EDGE, ffn_buf, start, WIDE, target)])
    for start in range(0, 4 * EDGE, WIDE):
        target = up_ref.at[:, cols(start // (2 * EDGE) * 2 * EDGE + start + core * 2 * EDGE, WIDE)]
        chunks.append([(normed, EDGE, 0, grad_up, start, WIDE, target)])
    mixed_rows = pl.ds(EDGE, both)

    def out_part(start, width):
        target = out_ref.at[:, cols(core * EDGE + start, width)]
        return (down_buf.at[mixed_rows], EDGE, 0, ffn_buf, core * EDGE + start, width, target)

    last = EDGE % WIDE
    chunks += [[out_part(start, WIDE)] for start in range(0, EDGE - last, WIDE)]
    for start in range(0, 3 * EDGE, WIDE):
        parts = []
        for i, ref in enumerate((q_ref, k_ref, v_ref)):
            first, end = max(start, i * EDGE), min(start + WIDE, (i + 1) * EDGE)
            if first < end:
                target = ref.at[:, cols(core * EDGE + first - i * EDGE, end - first)]
                parts.append((normed, EDGE, 0, wide, first, end - first, target))
        chunks.append(parts)
    chunks[-1].append(out_part(EDGE - last, last))
    count = len(chunks)

    half, quarter, eighth = EDGE // 2, EDGE // 4, EDGE // 8
    y0 = at.y * half
    l0 = y0 + at.low * quarter
    h0 = l0 + at.high * eighth
    ops = {}
    for k, parts in enumerate(chunks):
        acc, four, slot, sem = k % 6, k % 4, k % 7, k % RING
        hops = (
            ("x", "x", blocks.at[6 + k % 3], from_x.at[four]),
            ("y", "y", blocks.at[acc, rows_at((1 - at.y) * half, half)], from_y.at[four]),
            ("low", "low", blocks.at[acc, rows_at(y0 + (1 - at.low) * quarter, quarter)], from_low.at[four]),
            ("high", "high", blocks.at[acc, rows_at(l0 + (1 - at.high) * eighth, eighth)], from_high.at[four]),
            ("all_high", "high", res.at[slot, rows_at(h0, eighth)], res.at[slot, rows_at(h0, eighth)]),
            ("all_low", "low", res.at[slot, rows_at(l0, quarter)], res.at[slot, rows_at(l0, quarter)]),
            ("all_y", "y", res.at[slot, rows_at(y0, half)], res.at[slot, rows_at(y0, half)]),
        )
        for s, (stage, name, source, goal) in enumerate(hops):
            ops[stage, k] = [at.send(name, source, goal, send_sems.at[s, sem], recv_sems.at[s, sem])]
        ops["core", k] = []
        ops["store", k] = []
        start = 0
        for s, part in enumerate(parts):
            source = res.at[slot, :, pl.ds(start, part[5])]
            ops["core", k].append(at.send("core", source, part[6], send_sems.at[7 + s, sem], recv_sems.at[7 + s, sem]))
            ops["store", k].append(pltpu.make_async_copy(source, part[6], store_sems.at[s, sem]))
            start += part[5]

    def begin(stage, k):
        for op in ops[stage, k]:
            op.start()

    def came(stage, k):
        for op in ops[stage, k]:
            op.wait_recv()

    def left_here(stage, k):
        for op in ops[stage, k]:
            op.wait_send()

    def make(k):
        @pl.loop(0, 2)
        def _(j):
            of = j * x + (1 - j) * (1 - x)
            slot = j * (k % 6) + (1 - j) * (6 + k % 3)
            start = 0
            for left, stride, left_at, right, right_at, width_now, _ in chunks[k]:
                lanes = right_at if isinstance(right_at, int) else pl.multiple_of(right_at, 128)
                product = lax.dot_general(
                    left[:, cols(of * stride + left_at, EDGE)],
                    right[:, pl.ds(lanes, width_now)],
                    tn,
                    preferred_element_type=f32,
                )
                blocks[slot, :, start : start + width_now] = product.astype(bf16)
                start += width_now

        begin("x", k)

    def add(k, start, size, other, goal, goal_slot):
        @pl.loop(0, size // 80)
        def _(i):
            here = rows_at(start + i * 80, 80)
            there = rows_at(i * 80, 80)
            total = blocks[k % 6, here, :].astype(f32) + other[there, :].astype(f32)
            goal[goal_slot, here, :] = total.astype(bf16)

    def tick(t):
        k = t
        if 0 <= k < count:
            came("x", k)
            add(k, 0, EDGE, from_x.at[k % 4], blocks, k % 6)
            begin("y", k)
            if k >= 1:
                left_here("x", k - 1)
            if k + 2 < count:
                make(k + 2)
        k = t - 1
        if 0 <= k < count:
            came("y", k)
            add(k, y0, half, from_y.at[k % 4], blocks, k % 6)
            begin("low", k)
        k = t - 2
        if 0 <= k < count:
            came("low", k)
            add(k, l0, quarter, from_low.at[k % 4], blocks, k % 6)
            begin("high", k)
        k = t - 3
        if 0 <= k < count:
            came("high", k)
            add(k, h0, eighth, from_high.at[k % 4], res, k % 7)
            begin("all_high", k)
            for stage in ("y", "low", "high"):
                left_here(stage, k)
        for before, stage, after in ((4, "all_high", "all_low"), (5, "all_low", "all_y"), (6, "all_y", "core")):
            k = t - before
            if 0 <= k < count:
                came(stage, k)
                begin(after, k)
                if after == "core":
                    begin("store", k)
        k = t - 7
        if 0 <= k < count:
            came("core", k)
            for stage in ("all_high", "all_low", "all_y", "core"):
                left_here(stage, k)
            for op in ops["store", k]:
                op.wait()

    def core_copy(i, source, target):
        return at.send("core", source, target, core_send.at[i], core_recv.at[i])

    two_copy = core_copy(0, given.at[0], taken.at[0])
    result_copy = core_copy(1, given.at[1], taken.at[1])
    attn_copy = core_copy(2, ffn_buf.at[top], ffn_buf.at[bottom])
    one_copy = core_copy(3, given.at[0], taken.at[0])
    swaps = []
    for i, target in enumerate((result_ref, input_ref)):
        source = taken.at[1 - i]
        swaps.append(
            (
                at.send("diagonal", source, target, swap_send.at[i], swap_recv.at[i]),
                pltpu.make_async_copy(source, target, swap_local.at[i]),
            )
        )

    def swap(i, act):
        @pl.when(x != core)
        def _():
            act(swaps[i][0])

        @pl.when(x == core)
        def _():
            act(swaps[i][1])

    def vector(i):
        return jnp.concatenate([vec[0, i : i + 1, :], vec[1, i : i + 1, :]], axis=1)

    def add_vector(i, value):
        total = jnp.sum(value, axis=0, keepdims=True)
        sums[0, 2 * i : 2 * i + 1, :] += total[:, :EDGE]
        sums[0, 2 * i + 1 : 2 * i + 2, :] += total[:, EDGE:]

    def norm_back(values, grad_normed, gain):
        average = jnp.mean(values, axis=-1, keepdims=True)
        centred = values - average
        inverse = lax.rsqrt(jnp.mean(centred * centred, axis=-1, keepdims=True) + 1e-05)
        standard = centred * inverse
        scaled = grad_normed * gain
        back = inverse * (
            scaled
            - jnp.mean(scaled, axis=-1, keepdims=True)
            - standard * jnp.mean(scaled * standard, axis=-1, keepdims=True)
        )
        return standard, back

    loads["hidden"].wait()
    loads["ffn"].wait()
    make(0)
    make(1)
    loads["down_w"].wait()
    for i in range(4):
        loads["slope%d" % i].wait()
        lanes = pl.ds(i * EDGE, EDGE)
        row = pl.ds(16 + (i // 2) * 4 + core * 2 + i % 2, 1)

        @pl.loop(0, both // 256)
        def _(r):
            here = rows_at(r * 256, 256)
            value = lax.dot_general(ffn_buf[here, :], down_buf[lanes, :], nt, preferred_element_type=f32)
            value = (value * pair_buf[here, pl.ds((i % 2) * EDGE, EDGE)].astype(f32)).astype(bf16)
            grad_up[here, lanes] = value
            sums[0, row, :] += jnp.sum(value.astype(f32), axis=0, keepdims=True)

        if i < 2:
            load("slope%d" % (i + 2), *slopes[i + 2])
        if i == 1:
            loads["normed_two"].wait()
        tick(i)
    load("own_grad", own_grad, pair_buf.at[top])
    load("own", own, pair_buf.at[bottom])
    loads["up_w"].wait()

    @pl.loop(0, rows // 256)
    def _(r):
        value = lax.dot_general(grad_up[rows_at(rows + r * 256, 256), :], up_buf[...], nt, preferred_element_type=f32)
        given[0, rows_at(r * 256, 256), :] = value.astype(bf16)

    two_copy.start()
    tick(4)

    @pl.loop(0, rows // 256)
    def _(r):
        value = lax.dot_general(grad_up[rows_at(r * 256, 256), :], up_buf[...], nt, preferred_element_type=f32)
        part_buf[rows_at(r * 256, 256), :] = value

    tick(5)

    @pl.loop(0, rows // 256)
    def _(r):
        value = jnp.dot(wide[rows_at(rows + r * 256, 256), :], down_buf[...], preferred_element_type=f32)
        given[1, rows_at(r * 256, 256), :] = value.astype(bf16)

    tick(6)
    tick(7)
    result_copy.start()
    two_copy.wait_recv()
    for name in ("middle", "vectors", "scale", "own_grad", "totals"):
        loads[name].wait()
    result_copy.wait_recv()
    down_bias, gain_two, gain_one = vector(7), vector(5), vector(0)

    @pl.loop(0, rows // 128)
    def _(r):
        here = rows_at(r * 128, 128)
        value = jnp.dot(wide[here, :], down_buf[...], preferred_element_type=f32)
        value = mid[here, :] + value + taken[1, here, :].astype(f32) + down_bias
        taken[1, here, :] = value.astype(bf16)

    swap(0, lambda copy: copy.start())
    load("qkv", qkv, wide.at[:, pl.ds(0, 3 * EDGE)])
    load("mixed", mixed, down_buf.at[mixed_rows])
    load("out_w", out_w.at[rows_at(core * EDGE, EDGE)], down_buf.at[pl.ds(0, EDGE)])
    load("qkv_w", qkv_w, up_buf.at[:, pl.ds(0, 3 * EDGE)])
    weight = scale[0:1, 0:1]
    tick(8)

    @pl.loop(0, rows // 32)
    def _(r):
        here = rows_at(r * 32, 32)
        add_vector(7, ffn_buf[here, :].astype(f32))
        grad_normed = part_buf[here, :] + taken[0, here, :].astype(f32)
        standard, back = norm_back(mid[here, :], grad_normed, gain_two)
        add_vector(5, grad_normed * standard)
        add_vector(6, grad_normed)
        value = pair_buf[here, :].astype(f32) * weight + back
        mid[here, :] = value
        value = value.astype(bf16)
        ffn_buf[here, :] = value
        add_vector(4, value.astype(f32))

    attn_copy.start()
    two_copy.wait_send()
    tick(9)
    loads["out_w"].wait()
    attn_copy.wait_recv()

    @pl.loop(0, both // 256)
    def _(r):
        here = rows_at(r * 256, 256)
        value = lax.dot_general(ffn_buf[here, :], down_buf[0:EDGE, :], nt, preferred_element_type=f32)
        wide[here, pl.ds(3 * EDGE, EDGE)] = value.astype(bf16)

    loads["qkv"].wait()
    tick(10)

    @pl.loop(0, EDGE // 128)
    def _(pair):
        attend_back_pair(wide, tot, keys_acc, values_acc, pair)
        for i in range(5):

            @pl.when(pair == i)
            def _():
                tick(11 + i)

    loads["qkv_w"].wait()
    weights = pl.ds(0, 3 * EDGE)

    @pl.loop(0, rows // 256)
    def _(r):
        value = lax.dot_general(
            wide[rows_at(rows + r * 256, 256), weights], up_buf[:, weights], nt, preferred_element_type=f32
        )
        given[0, rows_at(r * 256, 256), :] = value.astype(bf16)

    one_copy.start()
    tick(16)
    tick(17)
    load("normed_one", normed_one, normed)
    loads["mixed"].wait()

    @pl.loop(0, rows // 256)
    def _(r):
        value = lax.dot_general(wide[rows_at(r * 256, 256), weights], up_buf[:, weights], nt, preferred_element_type=f32)
        part_buf[rows_at(r * 256, 256), :] = value

    tick(18)
    one_copy.wait_recv()
    loads["own"].wait()

    @pl.loop(0, rows // 32)
    def _(r):
        here = rows_at(r * 32, 32)
        tok = pair_buf[rows_at(rows + r * 32, 32), :].astype(f32)
        grad_normed = part_buf[here, :] + taken[0, here, :].astype(f32)
        standard, back = norm_back(tok, grad_normed, gain_one)
        add_vector(0, grad_normed * standard)
        add_vector(1, grad_normed)
        taken[0, here, :] = (mid[here, :] + back).astype(bf16)

    swap(1, lambda copy: copy.start())
    tick(19)
    loads["normed_one"].wait()

    @pl.loop(0, both // 128)
    def _(r):
        here = rows_at(r * 128, 128)
        for i in (0, 2):
            row = pl.ds(4 + i + core, 1)
            value = wide[here, pl.ds(i * EDGE, EDGE)].astype(f32)
            sums[0, row, :] += jnp.sum(value, axis=0, keepdims=True)

    names = ("x", "core", "y", "low", "high")
    vec_ops = [at.send(name, sums.at[i], sums.at[6 + i], vec_send.at[i], vec_recv.at[i]) for i, name in enumerate(names)]
    vec_ops[0].start()
    for t in range(20, count + 7):
        tick(t)
        if t < 25:
            i = t - 20
            vec_ops[i].wait_recv()
            sums[i + 1] = sums[i] + sums[6 + i]
            if i < 4:
                vec_ops[i + 1].start()
    vec_store = pltpu.make_async_copy(sums.at[5], vec_ref, vec_local.at[0])
    vec_store.start()
    vec_store.wait()
    for op in (result_copy, attn_copy, one_copy, *vec_ops):
        op.wait_send()
    swap(0, lambda copy: copy.wait())
    swap(1, lambda copy: copy.wait())
    left_here("x", count - 1)


def backward(*args):
    bf16, f32 = jnp.bfloat16, jnp.float32
    rows, width = args[0].shape
    both = 2 * rows
    outs = [
        ((rows, width), bf16),
        ((rows, width), bf16),
        ((4 * EDGE, width), bf16),
        ((EDGE, 8 * EDGE), bf16),
        ((EDGE, width), bf16),
        ((EDGE, width), bf16),
        ((EDGE, width), bf16),
        ((EDGE, width), bf16),
        ((24, EDGE), f32),
    ]
    scratch = [
        ((both, 4 * EDGE), bf16),
        ((both, 4 * EDGE), bf16),
        ((both, width), bf16),
        ((both, width), bf16),
        ((both, width), bf16),
        ((4 * EDGE, width), bf16),
        ((width, 4 * EDGE), bf16),
        ((rows, width), f32),
        ((2, rows, width), bf16),
        ((2, rows, width), bf16),
        ((rows, width), f32),
        ((EDGE // HDIM, 1, both), f32),
        ((2, 16, EDGE), f32),
        ((8, 128), f32),
        ((both, 128), f32),
        ((both, 128), f32),
        ((9, EDGE, WIDE), bf16),
        ((4, EDGE, WIDE), bf16),
        ((4, EDGE // 2, WIDE), bf16),
        ((4, EDGE // 4, WIDE), bf16),
        ((4, EDGE // 8, WIDE), bf16),
        ((7, EDGE, WIDE), bf16),
        ((11, 24, EDGE), f32),
    ]
    dma = pltpu.SemaphoreType.DMA
    return pl.pallas_call(
        backward_kernel,
        in_specs=[ANY] * len(args),
        out_specs=[ANY] * len(outs),
        out_shape=[jax.ShapeDtypeStruct(*out) for out in outs],
        scratch_shapes=[pltpu.VMEM(*array) for array in scratch]
        + [dma((9, RING)), dma((9, RING)), dma((2, RING)), dma((20,)), dma((4,)), dma((4,))]
        + [dma((2,)), dma((2,)), dma((2,)), dma((5,)), dma((5,)), dma((1,))],
        compiler_params=pltpu.CompilerParams(
            collective_id=1, has_side_effects=True, vmem_limit_bytes=64 * 1024 * 1024
        ),
        name="backward",
    )(*args)


def tuned(
    tokens,
    out_grad,
    query_counts,
    first_gain,
    first_bias,
    query_weight,
    query_bias,
    key_weight,
    value_weight,
    value_bias,
    output_weight,
    output_bias,
    second_gain,
    second_bias,
    up_weight,
    up_bias,
    down_weight,
    down_bias,
):
    f32, bf16 = jnp.float32, jnp.bfloat16
    x = lax.axis_index("seq")
    head_width = tokens.shape[2] // 2

    vectors = (first_gain, first_bias, query_bias, value_bias, output_bias, second_gain, second_bias, down_bias)
    vectors = jnp.concatenate([jnp.stack(vectors), up_bias.reshape(4, -1), jnp.zeros((4, head_width), bf16)])
    cell_weight = jnp.broadcast_to(jnp.sqrt(query_counts.astype(f32) / 1000.0), (8, 128))
    state = forward(
        tokens[0],
        out_grad[0],
        cell_weight,
        vectors.astype(f32),
        query_weight,
        key_weight,
        value_weight,
        output_weight,
        up_weight,
        down_weight,
    )
    result, input_grad, down, up, out, query, key, value, sums = backward(*state)
    short = lax.dynamic_index_in_dim(sums[:16].reshape(8, 2, head_width), x, 1, keepdims=False)
    up_sum = lax.dynamic_slice_in_dim(sums, 16 + 4 * x, 4, 0).reshape(-1)
    return (
        result[None],
        input_grad[None],
        short[0],
        short[1],
        query.astype(f32),
        short[2],
        key.astype(f32),
        value.astype(f32),
        short[3],
        out.astype(f32),
        short[4],
        short[5],
        short[6],
        up.astype(f32),
        up_sum,
        down.astype(f32),
        short[7],
    )


def chosen(mesh):
    cells, blocks = mesh.shape["cell"], mesh.shape["seq"]

    def per_device(tokens, *rest):
        if blocks == 2 and cells == 16 and tokens.shape == (1, 512, 1280):
            return tuned(tokens, *rest)
        return general(tokens, *rest)

    return per_device


def solution(mesh):
    placed = (
        P("cell", "seq", None),
        P("cell", "seq", None),
        P("cell"),
        P("seq"),
        P("seq"),
        P("seq", None),
        P("seq"),
        P("seq", None),
        P("seq", None),
        P("seq"),
        P("seq", None),
        P("seq"),
        P("seq"),
        P("seq"),
        P("seq", None),
        P("seq"),
        P("seq", None),
        P("seq"),
    )
    return jax.shard_map(
        chosen(mesh),
        mesh=mesh,
        in_specs=placed,
        out_specs=(
            P("cell", "seq", None),
            P("cell", "seq", None),
            P("seq"),
            P("seq"),
            P("seq", None),
            P("seq"),
            P("seq", None),
            P("seq", None),
            P("seq"),
            P("seq", None),
            P("seq"),
            P("seq"),
            P("seq"),
            P("seq", None),
            P("seq"),
            P("seq", None),
            P("seq"),
        ),
        check_vma=False,
    )
```

```python
import jax
import jax.numpy as jnp
from jax import lax
from jax.experimental import pallas as pl
from jax.experimental.pallas import tpu as pltpu
from jax.sharding import PartitionSpec as P

HEADS = 20
HDIM = 64


def from_behind(value, axis, steps):
    count = lax.axis_size(axis)
    pairs = [(source, (source + steps) % count) for source in range(count)]
    return lax.ppermute(value, axis, pairs)


def for_sending(x):
    return jax.tree.map(lambda a: a.astype(jnp.bfloat16) if a.dtype == jnp.float32 else a, x)


def matmul(left, right):
    return jnp.dot(left, right, preferred_element_type=jnp.float32)


def matmul_right_t(left, right):
    return jnp.einsum("to,io->ti", left, right, preferred_element_type=jnp.float32)


def weight_grad(left, right):
    return jnp.einsum("ti,to->io", left, right, preferred_element_type=jnp.float32)


def standardize(values):
    average = jnp.mean(values, axis=-1, keepdims=True)
    centred = values - average
    inverse = lax.rsqrt(jnp.mean(centred * centred, axis=-1, keepdims=True) + 1e-05)
    return (centred * inverse, inverse)


def standardize_back(grad_normed, standard, inverse, gain_vec):
    scaled = grad_normed * gain_vec
    return inverse * (
        scaled
        - jnp.mean(scaled, axis=-1, keepdims=True)
        - standard * jnp.mean(scaled * standard, axis=-1, keepdims=True)
    )


def gelu_value(up_proj):
    return 0.5 * up_proj * (1.0 + lax.erf(up_proj * 0.7071067811865476))


def gelu_slope(up_proj):
    return (
        0.5 * (1.0 + lax.erf(up_proj * 0.7071067811865476))
        + up_proj * jnp.exp(-0.5 * up_proj * up_proj) * 0.3989422804014327
    )


def score_block(queries, key_rows):
    return (
        jnp.einsum("cqhd,ckhd->chqk", queries, key_rows, preferred_element_type=jnp.float32) * 0.125
    )


def column_sum(values):
    return jnp.sum(values.astype(jnp.float32), axis=0)


def general(
    tokens,
    out_grad,
    query_counts,
    first_gain,
    first_bias,
    query_weight,
    query_bias,
    key_weight,
    value_weight,
    value_bias,
    output_weight,
    output_bias,
    second_gain,
    second_bias,
    up_weight,
    up_bias,
    down_weight,
    down_bias,
):
    (
        first_gain,
        first_bias,
        query_weight,
        query_bias,
        key_weight,
        value_weight,
        value_bias,
        output_weight,
        output_bias,
        second_gain,
        second_bias,
        up_weight,
        up_bias,
        down_weight,
        down_bias,
    ) = (
        lax.all_gather(first_gain, "seq", axis=0, tiled=True),
        lax.all_gather(first_bias, "seq", axis=0, tiled=True),
        lax.all_gather(query_weight, "seq", axis=0, tiled=True),
        lax.all_gather(query_bias, "seq", axis=0, tiled=True),
        lax.all_gather(key_weight, "seq", axis=0, tiled=True),
        lax.all_gather(value_weight, "seq", axis=0, tiled=True),
        lax.all_gather(value_bias, "seq", axis=0, tiled=True),
        lax.all_gather(output_weight, "seq", axis=0, tiled=True),
        lax.all_gather(output_bias, "seq", axis=0, tiled=True),
        lax.all_gather(second_gain, "seq", axis=0, tiled=True),
        lax.all_gather(second_bias, "seq", axis=0, tiled=True),
        lax.all_gather(up_weight, "seq", axis=0, tiled=True),
        lax.all_gather(up_bias, "seq", axis=0, tiled=True),
        lax.all_gather(down_weight, "seq", axis=0, tiled=True),
        lax.all_gather(down_bias, "seq", axis=0, tiled=True),
    )
    f32 = jnp.float32
    bf16 = jnp.bfloat16
    gain_first = first_gain.astype(f32)
    gain_second = second_gain.astype(f32)
    cell_count, seg_len, model_width = tokens.shape
    row_count = cell_count * seg_len
    head_shape = (cell_count, seg_len, HEADS, HDIM)
    cycle_size = lax.axis_size("seq")
    flat_input = tokens.reshape(row_count, model_width).astype(f32)
    standard_one, inverse_one = standardize(flat_input)
    normed_one = (standard_one * gain_first + first_bias.astype(f32)).astype(bf16)
    query_heads = (
        (matmul(normed_one, query_weight) + query_bias.astype(f32)).astype(bf16).reshape(head_shape)
    )
    key_heads = matmul(normed_one, key_weight).astype(bf16).reshape(head_shape)
    value_heads = (
        (matmul(normed_one, value_weight) + value_bias.astype(f32)).astype(bf16).reshape(head_shape)
    )
    running_max = jnp.full((cell_count, HEADS, seg_len), -1e30, f32)
    running_sum = jnp.zeros((cell_count, HEADS, seg_len), f32)
    weighted = jnp.zeros((cell_count, HEADS, seg_len, HDIM), f32)
    travel = (key_heads, value_heads)
    for step in range(cycle_size):
        if step > 0:
            travel = from_behind((travel[0], travel[1]), "seq", 1)
        scores = score_block(query_heads, travel[0])
        new_max = jnp.maximum(running_max, jnp.max(scores, axis=-1))
        rescale = jnp.exp(running_max - new_max)
        exp_scores = jnp.exp(scores - new_max[..., None])
        running_sum = running_sum * rescale + jnp.sum(exp_scores, axis=-1)
        weighted = weighted * rescale[..., None] + jnp.einsum(
            "chqk,ckhd->chqd", exp_scores.astype(bf16), travel[1], preferred_element_type=f32
        )
        running_max = new_max
    attended = weighted / running_sum[..., None]
    log_total = running_max + jnp.log(running_sum)
    mixed = attended.transpose(0, 2, 1, 3).reshape(row_count, model_width).astype(bf16)
    middle = flat_input + matmul(mixed, output_weight) + output_bias.astype(f32)
    standard_two, inverse_two = standardize(middle)
    normed_two = (standard_two * gain_second + second_bias.astype(f32)).astype(bf16)
    up_proj = matmul(normed_two, up_weight) + up_bias.astype(f32)
    hidden = gelu_value(up_proj).astype(bf16)
    result = middle + matmul(hidden, down_weight) + down_bias.astype(f32)
    result_out = result.astype(bf16).reshape(cell_count, seg_len, model_width)
    weight_cell = jnp.sqrt(query_counts.astype(f32) / 1000.0)
    grad_result = (out_grad.astype(f32) * weight_cell[:, None, None]).reshape(
        row_count, model_width
    )
    grad_ffn_out = grad_result.astype(bf16)
    grad_down_weight = weight_grad(hidden, grad_ffn_out)
    grad_down_bias = column_sum(grad_ffn_out)
    grad_up = (matmul_right_t(grad_ffn_out, down_weight) * gelu_slope(up_proj)).astype(bf16)
    grad_up_weight = weight_grad(normed_two, grad_up)
    grad_up_bias = column_sum(grad_up)
    grad_normed_two = matmul_right_t(grad_up, up_weight)
    grad_second_gain = jnp.sum(grad_normed_two * standard_two, axis=0)
    grad_second_bias = jnp.sum(grad_normed_two, axis=0)
    grad_middle = grad_result + standardize_back(
        grad_normed_two, standard_two, inverse_two, gain_second
    )
    grad_attn_out = grad_middle.astype(bf16)
    grad_output_weight = weight_grad(mixed, grad_attn_out)
    grad_output_bias = column_sum(grad_attn_out)
    grad_mixed = matmul_right_t(grad_attn_out, output_weight).astype(bf16).reshape(head_shape)
    row_delta = jnp.sum(grad_mixed.astype(f32).transpose(0, 2, 1, 3) * attended, axis=-1)
    grad_query_acc = jnp.zeros(head_shape, f32)
    moving = (jnp.zeros(head_shape, f32), jnp.zeros(head_shape, f32))
    travel = (key_heads, value_heads)
    for step in range(cycle_size):
        if step > 0:
            travel = from_behind((travel[0], travel[1]), "seq", 1)
        block_keys, block_values = travel
        scores = score_block(query_heads, block_keys)
        prob_block = jnp.exp(scores - log_total[..., None])
        part_values = jnp.einsum(
            "chqk,cqhd->ckhd", prob_block.astype(bf16), grad_mixed, preferred_element_type=f32
        )
        grad_probs = jnp.einsum(
            "cqhd,ckhd->chqk", grad_mixed, block_values, preferred_element_type=f32
        )
        grad_scores = (prob_block * (grad_probs - row_delta[..., None])).astype(bf16)
        grad_query_acc = (
            grad_query_acc
            + jnp.einsum("chqk,ckhd->cqhd", grad_scores, block_keys, preferred_element_type=f32)
            * 0.125
        )
        part_keys = (
            jnp.einsum("chqk,cqhd->ckhd", grad_scores, query_heads, preferred_element_type=f32)
            * 0.125
        )
        moving = from_behind(
            (for_sending(moving[0] + part_keys), for_sending(moving[1] + part_values)), "seq", 1
        )
    grad_queries = grad_query_acc.astype(bf16).reshape(row_count, model_width)
    grad_keys = moving[0].astype(bf16).reshape(row_count, model_width)
    grad_values = moving[1].astype(bf16).reshape(row_count, model_width)
    grad_query_weight = weight_grad(normed_one, grad_queries)
    grad_query_bias = column_sum(grad_queries)
    grad_key_weight = weight_grad(normed_one, grad_keys)
    grad_value_weight = weight_grad(normed_one, grad_values)
    grad_value_bias = column_sum(grad_values)
    grad_normed_one = (
        matmul_right_t(grad_queries, query_weight)
        + matmul_right_t(grad_keys, key_weight)
        + matmul_right_t(grad_values, value_weight)
    )
    grad_first_gain = jnp.sum(grad_normed_one * standard_one, axis=0)
    grad_first_bias = jnp.sum(grad_normed_one, axis=0)
    grad_input = grad_middle + standardize_back(
        grad_normed_one, standard_one, inverse_one, gain_first
    )
    input_grad = grad_input.astype(bf16).reshape(cell_count, seg_len, model_width)
    shared_all = (
        lax.psum_scatter(
            grad_first_gain.astype(jnp.bfloat16), "seq", scatter_dimension=0, tiled=True
        ).astype(jnp.float32),
        lax.psum_scatter(
            grad_first_bias.astype(jnp.bfloat16), "seq", scatter_dimension=0, tiled=True
        ).astype(jnp.float32),
        lax.psum_scatter(
            grad_query_weight.astype(jnp.bfloat16), "seq", scatter_dimension=0, tiled=True
        ).astype(jnp.float32),
        lax.psum_scatter(
            grad_query_bias.astype(jnp.bfloat16), "seq", scatter_dimension=0, tiled=True
        ).astype(jnp.float32),
        lax.psum_scatter(
            grad_key_weight.astype(jnp.bfloat16), "seq", scatter_dimension=0, tiled=True
        ).astype(jnp.float32),
        lax.psum_scatter(
            grad_value_weight.astype(jnp.bfloat16), "seq", scatter_dimension=0, tiled=True
        ).astype(jnp.float32),
        lax.psum_scatter(
            grad_value_bias.astype(jnp.bfloat16), "seq", scatter_dimension=0, tiled=True
        ).astype(jnp.float32),
        lax.psum_scatter(
            grad_output_weight.astype(jnp.bfloat16), "seq", scatter_dimension=0, tiled=True
        ).astype(jnp.float32),
        lax.psum_scatter(
            grad_output_bias.astype(jnp.bfloat16), "seq", scatter_dimension=0, tiled=True
        ).astype(jnp.float32),
        lax.psum_scatter(
            grad_second_gain.astype(jnp.bfloat16), "seq", scatter_dimension=0, tiled=True
        ).astype(jnp.float32),
        lax.psum_scatter(
            grad_second_bias.astype(jnp.bfloat16), "seq", scatter_dimension=0, tiled=True
        ).astype(jnp.float32),
        lax.psum_scatter(
            grad_up_weight.astype(jnp.bfloat16), "seq", scatter_dimension=0, tiled=True
        ).astype(jnp.float32),
        lax.psum_scatter(
            grad_up_bias.astype(jnp.bfloat16), "seq", scatter_dimension=0, tiled=True
        ).astype(jnp.float32),
        lax.psum_scatter(
            grad_down_weight.astype(jnp.bfloat16), "seq", scatter_dimension=0, tiled=True
        ).astype(jnp.float32),
        lax.psum_scatter(
            grad_down_bias.astype(jnp.bfloat16), "seq", scatter_dimension=0, tiled=True
        ).astype(jnp.float32),
    )
    (
        grad_first_gain,
        grad_first_bias,
        grad_query_weight,
        grad_query_bias,
        grad_key_weight,
        grad_value_weight,
        grad_value_bias,
        grad_output_weight,
        grad_output_bias,
        grad_second_gain,
        grad_second_bias,
        grad_up_weight,
        grad_up_bias,
        grad_down_weight,
        grad_down_bias,
    ) = shared_all
    (
        grad_first_gain,
        grad_first_bias,
        grad_query_weight,
        grad_query_bias,
        grad_key_weight,
        grad_value_weight,
        grad_value_bias,
        grad_output_weight,
        grad_output_bias,
        grad_second_gain,
        grad_second_bias,
        grad_up_weight,
        grad_up_bias,
        grad_down_weight,
        grad_down_bias,
    ) = (
        lax.psum(grad_first_gain.astype(jnp.bfloat16), "cell").astype(jnp.float32),
        lax.psum(grad_first_bias.astype(jnp.bfloat16), "cell").astype(jnp.float32),
        lax.psum(grad_query_weight.astype(jnp.bfloat16), "cell").astype(jnp.float32),
        lax.psum(grad_query_bias.astype(jnp.bfloat16), "cell").astype(jnp.float32),
        lax.psum(grad_key_weight.astype(jnp.bfloat16), "cell").astype(jnp.float32),
        lax.psum(grad_value_weight.astype(jnp.bfloat16), "cell").astype(jnp.float32),
        lax.psum(grad_value_bias.astype(jnp.bfloat16), "cell").astype(jnp.float32),
        lax.psum(grad_output_weight.astype(jnp.bfloat16), "cell").astype(jnp.float32),
        lax.psum(grad_output_bias.astype(jnp.bfloat16), "cell").astype(jnp.float32),
        lax.psum(grad_second_gain.astype(jnp.bfloat16), "cell").astype(jnp.float32),
        lax.psum(grad_second_bias.astype(jnp.bfloat16), "cell").astype(jnp.float32),
        lax.psum(grad_up_weight.astype(jnp.bfloat16), "cell").astype(jnp.float32),
        lax.psum(grad_up_bias.astype(jnp.bfloat16), "cell").astype(jnp.float32),
        lax.psum(grad_down_weight.astype(jnp.bfloat16), "cell").astype(jnp.float32),
        lax.psum(grad_down_bias.astype(jnp.bfloat16), "cell").astype(jnp.float32),
    )
    return (
        result_out,
        input_grad,
        grad_first_gain,
        grad_first_bias,
        grad_query_weight,
        grad_query_bias,
        grad_key_weight,
        grad_value_weight,
        grad_value_bias,
        grad_output_weight,
        grad_output_bias,
        grad_second_gain,
        grad_second_bias,
        grad_up_weight,
        grad_up_bias,
        grad_down_weight,
        grad_down_bias,
    )


Q_BLOCK = 256


MESH = pl.DeviceIdType.MESH
ANY = pl.BlockSpec(memory_space=pl.ANY)
EDGE = 640
WIDE = 256
RING = 10


class Spot:
    def __init__(self):
        self.x = lax.axis_index("seq")
        self.cell = lax.axis_index("cell")
        self.core = lax.rem(self.cell, 2)
        self.y = lax.rem(self.cell // 2, 2)
        self.low = lax.rem(self.cell // 4, 2)
        self.high = lax.rem(self.cell // 8, 2)

    def flip(self, index, bit):
        return {"cell": self.cell + bit - 2 * bit * index}

    def over(self, name):
        if name == "x":
            return {"seq": 1 - self.x}
        if name == "core":
            return self.flip(self.core, 1)
        if name == "diagonal":
            return {"seq": 1 - self.x, **self.flip(self.core, 1)}
        return self.flip(*{"y": (self.y, 2), "low": (self.low, 4), "high": (self.high, 8)}[name])

    def meet(self, names):
        barrier = pltpu.get_barrier_semaphore()
        for name in names:
            pl.semaphore_signal(barrier, inc=1, device_id=self.over(name), device_id_type=MESH)
        pl.semaphore_wait(barrier, len(names))

    def send(self, name, source, target, send_sem, recv_sem):
        return pltpu.make_async_remote_copy(
            source, target, send_sem, recv_sem, device_id=self.over(name), device_id_type=MESH
        )


def rows_at(start, size):
    return pl.ds(pl.multiple_of(start, 16), size)


def cols(start, size):
    return pl.ds(pl.multiple_of(start, 128), size)


def attend_pair(qkv, mixed, total_ref, pair, base):
    f32, bf16 = jnp.float32, jnp.bfloat16
    rows = qkv.shape[0]
    lane = lax.broadcasted_iota(jnp.int32, (1, 128), 1)
    here = pair * 128
    keys = qkv[:, cols(EDGE + here, 128)]
    values_t = qkv[:, cols(2 * EDGE + here, 128)].T
    for block in range(rows // Q_BLOCK):
        part = pl.ds(block * Q_BLOCK, Q_BLOCK)
        queries = qkv[part, cols(here, 128)] * jnp.asarray(0.125, bf16)
        outs = []
        for head in range(2):
            own = (lane // HDIM) == head
            scores = lax.dot_general(
                keys,
                jnp.where(own, queries, jnp.zeros_like(queries)),
                (((1,), (1,)), ((), ())),
                preferred_element_type=f32,
            )
            largest = jnp.max(scores, axis=0, keepdims=True)
            weights = jnp.exp(scores - largest)
            total = jnp.sum(weights, axis=0, keepdims=True)
            out = jnp.dot(
                values_t[head * HDIM : (head + 1) * HDIM, :],
                weights.astype(bf16),
                preferred_element_type=f32,
            )
            outs.append(out / total)
            total_ref[2 * pair + head, :, part] = largest + jnp.log(total)
        mixed[part, cols(base + here, 128)] = jnp.concatenate(outs, axis=0).T.astype(bf16)


def attend_back_pair(qkv, totals, keys_acc, values_acc, pair):
    f32, bf16 = jnp.float32, jnp.bfloat16
    rows = qkv.shape[0]
    size = Q_BLOCK
    lane = lax.broadcasted_iota(jnp.int32, (1, 128), 1)
    here, key_lanes, value_lanes, grad_lanes = (cols(i * EDGE + pair * 128, 128) for i in range(4))
    keys = qkv[:, key_lanes]
    keys_t = keys.T
    nt = (((1,), (1,)), ((), ()))
    keys_acc[...] = jnp.zeros_like(keys_acc)
    values_acc[...] = jnp.zeros_like(values_acc)

    @pl.loop(0, rows // size)
    def _(block):
        part = rows_at(block * size, size)
        queries = qkv[part, here] * jnp.asarray(0.125, bf16)
        grads = qkv[part, grad_lanes]
        values = qkv[:, value_lanes]
        outs = []
        key_part = value_part = 0.0
        for head in range(2):
            own = (lane // HDIM) == head
            q_own = jnp.where(own, queries, jnp.zeros_like(queries))
            g_own = jnp.where(own, grads, jnp.zeros_like(grads))
            scores = lax.dot_general(keys, q_own, nt, preferred_element_type=f32)
            probs = jnp.exp(scores - totals[2 * pair + head, :, cols(block * size, size)])
            grad_probs = lax.dot_general(values, g_own, nt, preferred_element_type=f32)
            delta = jnp.sum(probs * grad_probs, axis=0, keepdims=True)
            grad_scores = (probs * (grad_probs - delta)).astype(bf16)
            value_part += jnp.dot(probs.astype(bf16), g_own, preferred_element_type=f32)
            key_part += jnp.dot(grad_scores, q_own, preferred_element_type=f32)
            outs.append(jnp.dot(keys_t[head * HDIM : (head + 1) * HDIM, :], grad_scores, preferred_element_type=f32))
        qkv[part, here] = (jnp.concatenate(outs, axis=0) * 0.125).T.astype(bf16)
        keys_acc[...] += key_part
        values_acc[...] += value_part

    qkv[:, key_lanes] = keys_acc[...].astype(bf16)
    qkv[:, value_lanes] = values_acc[...].astype(bf16)


def layer_kernel(
    tokens, out_grad, counts, wq, wk, wv, wo, wup, wdown, v0, v1, v2, v3, v4, v5, v6, v7, v8,
    result_ref, input_ref, down_ref, up_ref, out_ref, q_ref, k_ref, v_ref, vec_ref, normed_spill, qkv_spill, mixed_spill,
    pair, scale, vec, qkv_w, out_w, up_w, down_w, normed, wide, grad_up, ffn, mid, partial_sum, taken, given, tot,
    keys_acc, values_acc, blocks, from_x, from_y, from_low, from_high, res, sums,
    cell_weight, vectors, send_sems, recv_sems, local_sems, side_send, side_recv, side_local, out_sems,
    sum_send, sum_recv, store_sems, load_sems, swap_send, swap_recv, swap_local, vec_send, vec_recv, vec_store_sem,
):
    f32, bf16 = jnp.float32, jnp.bfloat16
    at = Spot()
    x, core = at.x, at.core
    rows, width = tokens.shape
    both = 2 * rows
    top, bottom = pl.ds(0, rows), pl.ds(rows, rows)
    grad, tok = pair.at[top], pair.at[bottom]
    nt = (((1,), (1,)), ((), ()))
    tn = (((0,), (0,)), ((), ()))
    sums[0] = jnp.zeros(sums.shape[1:], f32)
    for i, ref in enumerate((v0, v1, v2, v3, v4, v5, v6, v7)):
        vectors[i : i + 1, :] = ref[...].astype(f32).reshape(1, EDGE)
    for i in range(4):
        vectors[8 + i : 9 + i, :] = v8[i * EDGE : (i + 1) * EDGE].astype(f32).reshape(1, EDGE)
    vectors[12:16, :] = jnp.zeros((4, EDGE), f32)
    cell_weight[...] = jnp.sqrt(jnp.full(cell_weight.shape, counts[0], jnp.int32).astype(f32) / 1000.0)
    at.meet(("x", "core", "diagonal", "y", "low", "high"))

    side = [(tokens, tok), (cell_weight, scale), (out_grad, grad)]
    diagonal = [at.send("diagonal", s, t, side_send.at[i], side_recv.at[i]) for i, (s, t) in enumerate(side)]
    straight = [pltpu.make_async_copy(s, t, side_local.at[i]) for i, (s, t) in enumerate(side)]

    def swap(i, remote, local):
        @pl.when(x != core)
        def _():
            remote(diagonal[i])

        @pl.when(x == core)
        def _():
            local(straight[i])

    def swap_start(i):
        swap(i, lambda c: c.start(), lambda c: c.start())

    def swap_wait(i):
        swap(i, lambda c: c.wait(), lambda c: c.wait())

    chunks = []
    for start in range(0, 3 * EDGE, WIDE):
        width_now = min(WIDE, 3 * EDGE - start)
        parts = []
        for i, ref in enumerate((wq, wk, wv)):
            low, high = max(start, i * EDGE), min(start + width_now, (i + 1) * EDGE)
            if low < high:
                parts.append((ref.at[:, cols(core * EDGE + low - i * EDGE, high - low)], low))
        chunks.append((parts, qkv_w, EDGE, 0, start, width_now))
    for start in range(0, 4 * EDGE, WIDE):
        part = start // (2 * EDGE) * 2 * EDGE + start + core * 2 * EDGE
        chunks.append(([(wup.at[:, cols(part, WIDE)], start)], up_w, EDGE, 0, start, WIDE))
    for start in range(0, 2 * EDGE, WIDE):
        source = wdown.at[rows_at(core * 2 * EDGE, EDGE), pl.ds(start, WIDE)]
        chunks.append(([(source, start)], down_w, 2 * EDGE, 0, start, WIDE))
    count = len(chunks)
    eighth = EDGE // 8
    place = at.y * 4 + at.low * 2 + at.high

    def region(k, half, start, size, column=None, width=None):
        _, ref, stride, row, first, most = chunks[k]
        column, width = (first, most) if column is None else (column, width)
        return ref.at[rows_at(half * stride + row + start * eighth, size * eighth), pl.ds(column, width)]

    ops = {}
    for k, chunk in enumerate(chunks):
        ops["x", k] = [
            at.send(
                "x",
                source.at[rows_at(place * eighth, eighth)],
                region(k, x, place, 1, column, source.shape[1]),
                send_sems.at[4 * j, k],
                recv_sems.at[4 * j, k],
            )
            for j, (source, column) in enumerate(chunk[0])
        ]
        for s, (name, start, size) in enumerate(
            (("high", place, 1), ("low", at.y * 4 + at.low * 2, 2), ("y", at.y * 4, 4))
        ):
            part = region(k, 1 - x, start, size)
            ops[name, k] = [at.send(name, part, part, send_sems.at[s + 1, k], recv_sems.at[s + 1, k])]
    direct = []
    for i, start in enumerate(range(0, 2 * EDGE, WIDE)):
        source = wdown.at[rows_at(core * 2 * EDGE + EDGE, EDGE), pl.ds(start, WIDE)]
        target = down_w.at[rows_at(x * 2 * EDGE + EDGE, EDGE), pl.ds(start, WIDE)]
        direct.append(at.send("x", source, target, send_sems.at[5, i], recv_sems.at[5, i]))
    owns = []
    mine = rows_at(x * EDGE, EDGE)
    for i, ref in enumerate((wq, wk, wv)):
        owns.append((ref.at[:, cols(core * EDGE, EDGE)], qkv_w.at[mine, pl.ds(i * EDGE, EDGE)]))
    for i in range(2):
        owns.append((wup.at[:, cols((2 * i + core) * 2 * EDGE, 2 * EDGE)], up_w.at[mine, pl.ds(i * 2 * EDGE, 2 * EDGE)]))
    owns.append((wdown.at[rows_at(core * 2 * EDGE, 2 * EDGE)], down_w.at[rows_at(x * 2 * EDGE, 2 * EDGE)]))
    owns = [pltpu.make_async_copy(source, target, local_sems.at[i]) for i, (source, target) in enumerate(owns)]
    half = EDGE // 2
    out_x = at.send(
        "x", wo.at[rows_at(core * half, half)], out_w.at[rows_at(x * EDGE + core * half, half)], side_send.at[4], side_recv.at[4]
    )
    part = out_w.at[rows_at((1 - x) * EDGE + core * half, half)]
    out_core = at.send("core", part, part, side_send.at[5], side_recv.at[5])
    out_local = pltpu.make_async_copy(wo, out_w.at[rows_at(x * EDGE, EDGE)], side_local.at[4])
    vec_x = at.send("x", vectors, vec.at[x], side_send.at[3], side_recv.at[3])
    vec_local = pltpu.make_async_copy(vectors, vec.at[x], side_local.at[3])
    def core_copy(i, source, target):
        return at.send("core", source, target, side_send.at[i], side_recv.at[i])

    normed_one_core = core_copy(6, normed.at[top], normed.at[bottom])
    heads = cols(core * EDGE, EDGE)
    mixed_core = [
        core_copy(7, ffn.at[top, heads], ffn.at[bottom, heads]),
        core_copy(8, ffn.at[bottom, heads], ffn.at[top, heads]),
    ]
    normed_two_core = core_copy(9, normed.at[top], normed.at[bottom])
    ffn_core = core_copy(10, ffn.at[top], ffn.at[bottom])

    spills = {}

    def put(name, source, target):
        spills[name] = pltpu.make_async_copy(source, target, out_sems.at[len(spills)])
        spills[name].start()

    stages = ("x", "high", "low", "y")

    def fetch(name, k):
        for op in ops[name, k]:
            op.start()

    def bring(t):
        for s, name in enumerate(stages):
            k = t - s
            if 0 <= k < count:
                for op in ops[name, k]:
                    op.wait_recv()
                if s < 3:
                    fetch(stages[s + 1], k)
        if t + 3 < count:
            fetch("x", t + 3)
        if t == 3:
            out_x.start()
        if t == 8:
            out_x.wait_recv()
            out_core.start()
        if t % 2 and 5 <= t < 5 + 2 * len(direct):
            direct[(t - 5) // 2].start()
        if t == 14:
            swap_start(2)
        if t in (1, 2, 4):
            for op in {1: (out_local,), 2: owns[3:5], 4: owns[5:]}[t]:
                op.start()

    fetch("x", 0)
    fetch("x", 1)
    fetch("x", 2)
    vec_x.start()
    swap_start(0)
    swap_start(1)
    vec_local.start()
    for op in owns[:3]:
        op.start()
    bring(0)
    bring(1)
    vec_x.wait_recv()
    vec_local.wait()

    def vector(i):
        return jnp.concatenate([vec[0, i : i + 1, :], vec[1, i : i + 1, :]], axis=1)

    def norm(values, gain, bias):
        average = jnp.mean(values, axis=-1, keepdims=True)
        centred = values - average
        inverse = lax.rsqrt(jnp.mean(centred * centred, axis=-1, keepdims=True) + 1e-05)
        return (centred * inverse * gain + bias).astype(bf16)

    swap_wait(0)
    gain_one, bias_one = vector(0), vector(1)

    @pl.loop(0, rows // 64)
    def _(i):
        here = rows_at(i * 64, 64)
        normed[here, :] = norm(tok[here, :].astype(f32), gain_one, bias_one)

    normed_one_core.start()
    bring(2)
    bring(3)
    normed_one_core.wait_recv()
    put("normed_one", normed, normed_spill)

    for i in range(3):
        for t in ((4, 5), (6, 7), (8, 9, 10))[i]:
            bring(t)
        owns[i].wait()
        lanes = pl.ds(i * EDGE, EDGE)
        bias = 0.0 if i == 1 else vec[core, 2 + i // 2 : 3 + i // 2, :]

        @pl.loop(0, 2 * rows // 256)
        def _(r):
            here = rows_at(r * 256, 256)
            value = jnp.dot(normed[here, :], qkv_w[:, lanes], preferred_element_type=f32)
            wide[here, lanes] = (value + bias).astype(bf16)

    put("qkv", wide.at[:, pl.ds(0, 3 * EDGE)], qkv_spill)

    @pl.loop(0, EDGE // 128)
    def _(two):
        attend_pair(wide, ffn, tot, two, core * EDGE)

        for i in range(5):

            @pl.when(two == i)
            def _():
                bring(11 + i)

    spills["normed_one"].wait()
    normed_one_core.wait_send()
    mixed_core[0].start()
    mixed_core[1].start()
    bring(16)
    out_local.wait()
    out_core.wait_recv()
    mixed_core[1].wait_recv()
    mixed_core[0].wait_recv()
    put("mixed", ffn, mixed_spill)
    gain_two, bias_two, out_bias = vector(5), vector(6), vector(4)

    @pl.loop(0, rows // 128)
    def _(r):
        here = rows_at(r * 128, 128)
        value = jnp.dot(ffn[here, :], out_w[...], preferred_element_type=f32)
        value = tok[here, :].astype(f32) + value + out_bias
        mid[here, :] = value
        normed[here, :] = norm(value, gain_two, bias_two)

    spills["mixed"].wait()
    spills["qkv"].wait()
    for op in mixed_core:
        op.wait_send()
    normed_two_core.start()
    bring(17)
    normed_two_core.wait_recv()
    up_bias = jnp.concatenate([vec[h, pl.ds(8 + core * 2 + i, 1), :] for h in range(2) for i in range(2)], axis=1)
    for i in range(4):
        if i % 2 == 0:
            owns[3 + i // 2].wait()
        lanes = pl.ds(i * EDGE, EDGE)
        bias = up_bias[:, i * EDGE : (i + 1) * EDGE]

        @pl.loop(0, both // 128)
        def _(r):
            here = rows_at(r * 128, 128)
            up = jnp.dot(normed[here, :], up_w[:, lanes], preferred_element_type=f32) + bias
            cdf = 0.5 * (1.0 + lax.erf(up * 0.7071067811865476))
            wide[here, lanes] = (up * cdf).astype(bf16)
            grad_up[here, lanes] = (cdf + up * jnp.exp(-0.5 * up * up) * 0.3989422804014327).astype(bf16)

        if i == 0:
            swap_wait(1)
            swap_wait(2)
            weight = scale[0:1, 0:1]

            @pl.loop(0, rows // 64)
            def _(r):
                here = rows_at(r * 64, 64)
                ffn[here, :] = (grad[here, :].astype(f32) * weight).astype(bf16)

            ffn_core.start()
        for t in ((18,), (19, 20), (21,), (22,))[i]:
            bring(t)
    ffn_core.wait_recv()

    pieces = []
    for i in range(2):
        for start in range(0, 2 * EDGE, WIDE):
            target = down_ref.at[rows_at(core * 2 * EDGE + i * EDGE, EDGE), pl.ds(start, WIDE)]
            pieces.append([(wide, 2 * EDGE, i * EDGE, ffn, start, WIDE, target)])
    for start in range(0, 4 * EDGE, WIDE):
        target = up_ref.at[:, cols(start // (2 * EDGE) * 2 * EDGE + start + core * 2 * EDGE, WIDE)]
        pieces.append([(normed, EDGE, 0, grad_up, start, WIDE, target)])
    mixed_rows = pl.ds(EDGE, both)

    def out_part(start, width):
        target = out_ref.at[:, cols(core * EDGE + start, width)]
        return (down_w.at[mixed_rows], EDGE, 0, ffn, core * EDGE + start, width, target)

    last = EDGE % WIDE
    pieces += [[out_part(start, WIDE)] for start in range(0, EDGE - last, WIDE)]
    for start in range(0, 3 * EDGE, WIDE):
        parts = []
        for i, ref in enumerate((q_ref, k_ref, v_ref)):
            first, end = max(start, i * EDGE), min(start + WIDE, (i + 1) * EDGE)
            if first < end:
                target = ref.at[:, cols(core * EDGE + first - i * EDGE, end - first)]
                parts.append((normed, EDGE, 0, wide, first, end - first, target))
        pieces.append(parts)
    pieces[-1].append(out_part(EDGE - last, last))
    total_count = len(pieces)

    half, quarter, eighth = EDGE // 2, EDGE // 4, EDGE // 8
    y0 = at.y * half
    l0 = y0 + at.low * quarter
    h0 = l0 + at.high * eighth
    sum_ops = {}
    for k, parts in enumerate(pieces):
        acc, four, slot, sem = k % 6, k % 4, k % 7, k % RING
        hops = (
            ("x", "x", blocks.at[6 + k % 3], from_x.at[four]),
            ("y", "y", blocks.at[acc, rows_at((1 - at.y) * half, half)], from_y.at[four]),
            ("low", "low", blocks.at[acc, rows_at(y0 + (1 - at.low) * quarter, quarter)], from_low.at[four]),
            ("high", "high", blocks.at[acc, rows_at(l0 + (1 - at.high) * eighth, eighth)], from_high.at[four]),
            ("all_high", "high", res.at[slot, rows_at(h0, eighth)], res.at[slot, rows_at(h0, eighth)]),
            ("all_low", "low", res.at[slot, rows_at(l0, quarter)], res.at[slot, rows_at(l0, quarter)]),
            ("all_y", "y", res.at[slot, rows_at(y0, half)], res.at[slot, rows_at(y0, half)]),
        )
        for s, (stage, name, source, goal) in enumerate(hops):
            sum_ops[stage, k] = [at.send(name, source, goal, sum_send.at[s, sem], sum_recv.at[s, sem])]
        sum_ops["core", k] = []
        sum_ops["store", k] = []
        start = 0
        for s, part in enumerate(parts):
            source = res.at[slot, :, pl.ds(start, part[5])]
            sum_ops["core", k].append(at.send("core", source, part[6], sum_send.at[7 + s, sem], sum_recv.at[7 + s, sem]))
            sum_ops["store", k].append(pltpu.make_async_copy(source, part[6], store_sems.at[s, sem]))
            start += part[5]

    def begin(stage, k):
        for op in sum_ops[stage, k]:
            op.start()

    def came(stage, k):
        for op in sum_ops[stage, k]:
            op.wait_recv()

    def left_here(stage, k):
        for op in sum_ops[stage, k]:
            op.wait_send()

    def make(k):
        @pl.loop(0, 2)
        def _(j):
            of = j * x + (1 - j) * (1 - x)
            slot = j * (k % 6) + (1 - j) * (6 + k % 3)
            start = 0
            for left, stride, left_at, right, right_at, width_now, _ in pieces[k]:
                lanes = right_at if isinstance(right_at, int) else pl.multiple_of(right_at, 128)
                product = lax.dot_general(
                    left[:, cols(of * stride + left_at, EDGE)],
                    right[:, pl.ds(lanes, width_now)],
                    tn,
                    preferred_element_type=f32,
                )
                blocks[slot, :, start : start + width_now] = product.astype(bf16)
                start += width_now

        begin("x", k)

    def add(k, start, size, other, goal, goal_slot):
        @pl.loop(0, size // 80)
        def _(i):
            here = rows_at(start + i * 80, 80)
            there = rows_at(i * 80, 80)
            total = blocks[k % 6, here, :].astype(f32) + other[there, :].astype(f32)
            goal[goal_slot, here, :] = total.astype(bf16)

    def tick(t):
        k = t
        if 0 <= k < total_count:
            came("x", k)
            add(k, 0, EDGE, from_x.at[k % 4], blocks, k % 6)
            begin("y", k)
            if k >= 1:
                left_here("x", k - 1)
            if k + 2 < total_count:
                make(k + 2)
        k = t - 1
        if 0 <= k < total_count:
            came("y", k)
            add(k, y0, half, from_y.at[k % 4], blocks, k % 6)
            begin("low", k)
        k = t - 2
        if 0 <= k < total_count:
            came("low", k)
            add(k, l0, quarter, from_low.at[k % 4], blocks, k % 6)
            begin("high", k)
        k = t - 3
        if 0 <= k < total_count:
            came("high", k)
            add(k, h0, eighth, from_high.at[k % 4], res, k % 7)
            begin("all_high", k)
            for stage in ("y", "low", "high"):
                left_here(stage, k)
        for before, stage, after in ((4, "all_high", "all_low"), (5, "all_low", "all_y"), (6, "all_y", "core")):
            k = t - before
            if 0 <= k < total_count:
                came(stage, k)
                begin(after, k)
                if after == "core":
                    begin("store", k)
        k = t - 7
        if 0 <= k < total_count:
            came("core", k)
            for stage in ("all_high", "all_low", "all_y", "core"):
                left_here(stage, k)
            for op in sum_ops["store", k]:
                op.wait()

    two_copy = core_copy(11, given.at[0], taken.at[0])
    result_copy = core_copy(12, given.at[1], taken.at[1])
    attn_copy = core_copy(13, ffn.at[top], ffn.at[bottom])
    one_copy = core_copy(14, given.at[0], taken.at[0])
    swaps = []
    for i, target in enumerate((result_ref, input_ref)):
        source = taken.at[1 - i]
        swaps.append(
            (
                at.send("diagonal", source, target, swap_send.at[i], swap_recv.at[i]),
                pltpu.make_async_copy(source, target, swap_local.at[i]),
            )
        )

    def swap_back(i, act):
        @pl.when(x != core)
        def _():
            act(swaps[i][0])

        @pl.when(x == core)
        def _():
            act(swaps[i][1])

    def add_vector(i, value):
        total = jnp.sum(value, axis=0, keepdims=True)
        sums[0, 2 * i : 2 * i + 1, :] += total[:, :EDGE]
        sums[0, 2 * i + 1 : 2 * i + 2, :] += total[:, EDGE:]

    def norm_back(values, grad_normed, gain):
        average = jnp.mean(values, axis=-1, keepdims=True)
        centred = values - average
        inverse = lax.rsqrt(jnp.mean(centred * centred, axis=-1, keepdims=True) + 1e-05)
        standard = centred * inverse
        scaled = grad_normed * gain
        back = inverse * (
            scaled
            - jnp.mean(scaled, axis=-1, keepdims=True)
            - standard * jnp.mean(scaled * standard, axis=-1, keepdims=True)
        )
        return standard, back

    make(0)
    make(1)
    for t in (23, 24, 25):
        bring(t)
    owns[5].wait()
    for op in direct:
        op.wait()
    normed_two_core.wait_send()
    loads = {}

    def load(name, source, target):
        loads[name] = pltpu.make_async_copy(source, target, load_sems.at[len(loads)])
        loads[name].start()

    for i in range(4):
        lanes = pl.ds(i * EDGE, EDGE)
        row = pl.ds(16 + 2 * (core * 2 + i % 2) + i // 2, 1)

        @pl.loop(0, both // 256)
        def _(r):
            here = rows_at(r * 256, 256)
            value = lax.dot_general(ffn[here, :], down_w[lanes, :], nt, preferred_element_type=f32)
            value = (value * grad_up[here, lanes].astype(f32)).astype(bf16)
            grad_up[here, lanes] = value
            sums[0, row, :] += jnp.sum(value.astype(f32), axis=0, keepdims=True)

        tick(i)

    @pl.loop(0, rows // 256)
    def _(r):
        value = lax.dot_general(grad_up[rows_at(rows + r * 256, 256), :], up_w[...], nt, preferred_element_type=f32)
        given[0, rows_at(r * 256, 256), :] = value.astype(bf16)

    two_copy.start()
    tick(4)

    @pl.loop(0, rows // 256)
    def _(r):
        value = lax.dot_general(grad_up[rows_at(r * 256, 256), :], up_w[...], nt, preferred_element_type=f32)
        partial_sum[rows_at(r * 256, 256), :] = value

    tick(5)

    @pl.loop(0, rows // 256)
    def _(r):
        value = jnp.dot(wide[rows_at(rows + r * 256, 256), :], down_w[...], preferred_element_type=f32)
        given[1, rows_at(r * 256, 256), :] = value.astype(bf16)

    tick(6)
    tick(7)
    result_copy.start()
    two_copy.wait_recv()
    result_copy.wait_recv()
    down_bias = vector(7)

    @pl.loop(0, rows // 128)
    def _(r):
        here = rows_at(r * 128, 128)
        value = jnp.dot(wide[here, :], down_w[...], preferred_element_type=f32)
        value = mid[here, :] + value + taken[1, here, :].astype(f32) + down_bias
        taken[1, here, :] = value.astype(bf16)

    swap_back(0, lambda copy: copy.start())
    for k in range(count):
        for name in stages:
            for op in ops[name, k]:
                op.wait_send()
    for op in (ffn_core, out_x, out_core, vec_x):
        op.wait_send()
    load("qkv", qkv_spill, wide.at[:, pl.ds(0, 3 * EDGE)])
    load("mixed", mixed_spill, down_w.at[mixed_rows])
    weight = scale[0:1, 0:1]
    tick(8)

    @pl.loop(0, rows // 32)
    def _(r):
        here = rows_at(r * 32, 32)
        add_vector(7, ffn[here, :].astype(f32))
        grad_normed = partial_sum[here, :] + taken[0, here, :].astype(f32)
        standard, back = norm_back(mid[here, :], grad_normed, gain_two)
        add_vector(5, grad_normed * standard)
        add_vector(6, grad_normed)
        value = pair[here, :].astype(f32) * weight + back
        mid[here, :] = value
        value = value.astype(bf16)
        ffn[here, :] = value
        add_vector(4, value.astype(f32))

    attn_copy.start()
    two_copy.wait_send()
    tick(9)
    attn_copy.wait_recv()

    @pl.loop(0, both // 256)
    def _(r):
        here = rows_at(r * 256, 256)
        value = lax.dot_general(ffn[here, :], out_w[rows_at(core * EDGE, EDGE), :], nt, preferred_element_type=f32)
        wide[here, pl.ds(3 * EDGE, EDGE)] = value.astype(bf16)

    loads["qkv"].wait()
    tick(10)

    @pl.loop(0, EDGE // 128)
    def _(two):
        attend_back_pair(wide, tot, keys_acc, values_acc, two)
        for i in range(5):

            @pl.when(two == i)
            def _():
                tick(11 + i)

    weights = pl.ds(0, 3 * EDGE)

    @pl.loop(0, rows // 256)
    def _(r):
        value = lax.dot_general(
            wide[rows_at(rows + r * 256, 256), weights], qkv_w[...], nt, preferred_element_type=f32
        )
        given[0, rows_at(r * 256, 256), :] = value.astype(bf16)

    one_copy.start()
    tick(16)
    tick(17)
    load("normed_one", normed_spill, normed)
    loads["mixed"].wait()

    @pl.loop(0, rows // 256)
    def _(r):
        value = lax.dot_general(wide[rows_at(r * 256, 256), weights], qkv_w[...], nt, preferred_element_type=f32)
        partial_sum[rows_at(r * 256, 256), :] = value

    tick(18)
    one_copy.wait_recv()

    @pl.loop(0, rows // 32)
    def _(r):
        here = rows_at(r * 32, 32)
        tok = pair[rows_at(rows + r * 32, 32), :].astype(f32)
        grad_normed = partial_sum[here, :] + taken[0, here, :].astype(f32)
        standard, back = norm_back(tok, grad_normed, gain_one)
        add_vector(0, grad_normed * standard)
        add_vector(1, grad_normed)
        taken[0, here, :] = (mid[here, :] + back).astype(bf16)

    swap_back(1, lambda copy: copy.start())
    tick(19)
    loads["normed_one"].wait()

    @pl.loop(0, both // 128)
    def _(r):
        here = rows_at(r * 128, 128)
        for i in (0, 2):
            row = pl.ds(4 + i + core, 1)
            value = wide[here, pl.ds(i * EDGE, EDGE)].astype(f32)
            sums[0, row, :] += jnp.sum(value, axis=0, keepdims=True)

    names = ("x", "core", "y", "low", "high")
    vec_ops = [at.send(name, sums.at[i], sums.at[6 + i], vec_send.at[i], vec_recv.at[i]) for i, name in enumerate(names)]
    vec_ops[0].start()
    for t in range(20, total_count + 7):
        tick(t)
        if t < 25:
            i = t - 20
            vec_ops[i].wait_recv()
            sums[i + 1] = sums[i] + sums[6 + i]
            if i < 4:
                vec_ops[i + 1].start()
    vec_store = pltpu.make_async_copy(sums.at[5], vec_ref, vec_store_sem.at[0])
    vec_store.start()
    vec_store.wait()
    for op in (result_copy, attn_copy, one_copy, *vec_ops):
        op.wait_send()
    swap_back(0, lambda copy: copy.wait())
    swap_back(1, lambda copy: copy.wait())
    left_here("x", total_count - 1)


def layer(*args):
    bf16, f32 = jnp.bfloat16, jnp.float32
    rows, width = args[0].shape
    both = 2 * rows
    outs = [
        ((rows, width), bf16),
        ((rows, width), bf16),
        ((4 * EDGE, width), bf16),
        ((EDGE, 8 * EDGE), bf16),
        ((EDGE, width), bf16),
        ((EDGE, width), bf16),
        ((EDGE, width), bf16),
        ((EDGE, width), bf16),
        ((24, EDGE), f32),
        ((both, width), bf16),
        ((both, 3 * EDGE), bf16),
        ((both, width), bf16),
    ]
    scratch = [
        ((both, width), bf16),
        ((8, 128), f32),
        ((2, 16, EDGE), f32),
        ((width, 3 * EDGE), bf16),
        ((width, width), bf16),
        ((width, 4 * EDGE), bf16),
        ((4 * EDGE, width), bf16),
        ((both, width), bf16),
        ((both, 4 * EDGE), bf16),
        ((both, 4 * EDGE), bf16),
        ((both, width), bf16),
        ((rows, width), f32),
        ((rows, width), f32),
        ((2, rows, width), bf16),
        ((2, rows, width), bf16),
        ((EDGE // HDIM, 1, both), f32),
        ((both, 128), f32),
        ((both, 128), f32),
        ((9, EDGE, WIDE), bf16),
        ((4, EDGE, WIDE), bf16),
        ((4, EDGE // 2, WIDE), bf16),
        ((4, EDGE // 4, WIDE), bf16),
        ((4, EDGE // 8, WIDE), bf16),
        ((7, EDGE, WIDE), bf16),
        ((11, 24, EDGE), f32),
        ((8, 128), f32),
        ((16, EDGE), f32),
    ]
    dma = pltpu.SemaphoreType.DMA
    sizes = [(6, 23), (6, 23), (6,), (15,), (15,), (5,), (3,), (9, RING), (9, RING), (2, RING), (3,)]
    sizes += [(2,), (2,), (2,), (5,), (5,), (1,)]
    return pl.pallas_call(
        layer_kernel,
        in_specs=[ANY] * 2 + [pl.BlockSpec(memory_space=pltpu.SMEM)] + [ANY] * 6 + [pl.BlockSpec(memory_space=pltpu.VMEM)] * 9,
        out_specs=[ANY] * len(outs),
        out_shape=[jax.ShapeDtypeStruct(*out) for out in outs],
        scratch_shapes=[pltpu.VMEM(*array) for array in scratch] + [dma(size) for size in sizes],
        compiler_params=pltpu.CompilerParams(
            collective_id=0, has_side_effects=True, vmem_limit_bytes=64 * 1024 * 1024
        ),
        name="layer",
    )(*args)


def widen_kernel(*refs):
    half = len(refs) // 2
    for source, target in zip(refs[:half], refs[half:]):
        target[...] = source[...].astype(target.dtype)


def widen(*arrays):
    steps = 8
    specs = [pl.BlockSpec((a.shape[0] // steps, a.shape[1]), lambda i: (i, 0)) for a in arrays]
    types = [jnp.float32] * (len(arrays) - 2) + [jnp.bfloat16] * 2
    return pl.pallas_call(
        widen_kernel,
        grid=(steps,),
        in_specs=specs,
        out_specs=specs,
        out_shape=[jax.ShapeDtypeStruct(a.shape, kind) for a, kind in zip(arrays, types)],
        compiler_params=pltpu.CompilerParams(vmem_limit_bytes=64 * 1024 * 1024),
        name="widen",
    )(*arrays)


def tuned(
    tokens,
    out_grad,
    query_counts,
    first_gain,
    first_bias,
    query_weight,
    query_bias,
    key_weight,
    value_weight,
    value_bias,
    output_weight,
    output_bias,
    second_gain,
    second_bias,
    up_weight,
    up_bias,
    down_weight,
    down_bias,
):
    f32, bf16 = jnp.float32, jnp.bfloat16
    x = lax.axis_index("seq")
    head_width = tokens.shape[2] // 2

    result, input_grad, down, up, out, query, key, value, sums, *_ = layer(
        tokens[0],
        out_grad[0],
        query_counts,
        query_weight,
        key_weight,
        value_weight,
        output_weight,
        up_weight,
        down_weight,
        first_gain,
        first_bias,
        query_bias,
        value_bias,
        output_bias,
        second_gain,
        second_bias,
        down_bias,
        up_bias,
    )
    out, query, key, value, up, down, result, input_grad = widen(out, query, key, value, up, down, result, input_grad)
    sums = lax.dynamic_index_in_dim(sums.reshape(12, 2, head_width), x, 1, keepdims=False)
    up_sum = sums[8:].reshape(-1)
    return (
        result[None],
        input_grad[None],
        sums[0],
        sums[1],
        query,
        sums[2],
        key,
        value,
        sums[3],
        out,
        sums[4],
        sums[5],
        sums[6],
        up,
        up_sum,
        down,
        sums[7],
    )


def chosen(mesh):
    cells, blocks = mesh.shape["cell"], mesh.shape["seq"]

    def per_device(tokens, *rest):
        if blocks == 2 and cells == 16 and tokens.shape == (1, 512, 1280):
            return tuned(tokens, *rest)
        return general(tokens, *rest)

    return per_device


def solution(mesh):
    placed = (
        P("cell", "seq", None),
        P("cell", "seq", None),
        P("cell"),
        P("seq"),
        P("seq"),
        P("seq", None),
        P("seq"),
        P("seq", None),
        P("seq", None),
        P("seq"),
        P("seq", None),
        P("seq"),
        P("seq"),
        P("seq"),
        P("seq", None),
        P("seq"),
        P("seq", None),
        P("seq"),
    )
    return jax.shard_map(
        chosen(mesh),
        mesh=mesh,
        in_specs=placed,
        out_specs=(
            P("cell", "seq", None),
            P("cell", "seq", None),
            P("seq"),
            P("seq"),
            P("seq", None),
            P("seq"),
            P("seq", None),
            P("seq", None),
            P("seq"),
            P("seq", None),
            P("seq"),
            P("seq"),
            P("seq"),
            P("seq", None),
            P("seq"),
            P("seq", None),
            P("seq"),
        ),
        check_vma=False,
    )
```

```python
import jax
import jax.numpy as jnp
from jax import lax
from jax.experimental import pallas as pl
from jax.experimental.pallas import tpu as pltpu
from jax.sharding import PartitionSpec as P

HEADS = 20
HDIM = 64


def from_behind(value, axis, steps):
    count = lax.axis_size(axis)
    pairs = [(source, (source + steps) % count) for source in range(count)]
    return lax.ppermute(value, axis, pairs)


def for_sending(x):
    return jax.tree.map(lambda a: a.astype(jnp.bfloat16) if a.dtype == jnp.float32 else a, x)


def matmul(left, right):
    return jnp.dot(left, right, preferred_element_type=jnp.float32)


def matmul_right_t(left, right):
    return jnp.einsum("to,io->ti", left, right, preferred_element_type=jnp.float32)


def weight_grad(left, right):
    return jnp.einsum("ti,to->io", left, right, preferred_element_type=jnp.float32)


def standardize(values):
    average = jnp.mean(values, axis=-1, keepdims=True)
    centred = values - average
    inverse = lax.rsqrt(jnp.mean(centred * centred, axis=-1, keepdims=True) + 1e-05)
    return (centred * inverse, inverse)


def standardize_back(grad_normed, standard, inverse, gain_vec):
    scaled = grad_normed * gain_vec
    return inverse * (
        scaled
        - jnp.mean(scaled, axis=-1, keepdims=True)
        - standard * jnp.mean(scaled * standard, axis=-1, keepdims=True)
    )


def gelu_value(up_proj):
    return 0.5 * up_proj * (1.0 + lax.erf(up_proj * 0.7071067811865476))


def gelu_slope(up_proj):
    return (
        0.5 * (1.0 + lax.erf(up_proj * 0.7071067811865476))
        + up_proj * jnp.exp(-0.5 * up_proj * up_proj) * 0.3989422804014327
    )


def score_block(queries, key_rows):
    return (
        jnp.einsum("cqhd,ckhd->chqk", queries, key_rows, preferred_element_type=jnp.float32) * 0.125
    )


def column_sum(values):
    return jnp.sum(values.astype(jnp.float32), axis=0)


def general(
    tokens,
    out_grad,
    query_counts,
    first_gain,
    first_bias,
    query_weight,
    query_bias,
    key_weight,
    value_weight,
    value_bias,
    output_weight,
    output_bias,
    second_gain,
    second_bias,
    up_weight,
    up_bias,
    down_weight,
    down_bias,
):
    (
        first_gain,
        first_bias,
        query_weight,
        query_bias,
        key_weight,
        value_weight,
        value_bias,
        output_weight,
        output_bias,
        second_gain,
        second_bias,
        up_weight,
        up_bias,
        down_weight,
        down_bias,
    ) = (
        lax.all_gather(first_gain, "seq", axis=0, tiled=True),
        lax.all_gather(first_bias, "seq", axis=0, tiled=True),
        lax.all_gather(query_weight, "seq", axis=0, tiled=True),
        lax.all_gather(query_bias, "seq", axis=0, tiled=True),
        lax.all_gather(key_weight, "seq", axis=0, tiled=True),
        lax.all_gather(value_weight, "seq", axis=0, tiled=True),
        lax.all_gather(value_bias, "seq", axis=0, tiled=True),
        lax.all_gather(output_weight, "seq", axis=0, tiled=True),
        lax.all_gather(output_bias, "seq", axis=0, tiled=True),
        lax.all_gather(second_gain, "seq", axis=0, tiled=True),
        lax.all_gather(second_bias, "seq", axis=0, tiled=True),
        lax.all_gather(up_weight, "seq", axis=0, tiled=True),
        lax.all_gather(up_bias, "seq", axis=0, tiled=True),
        lax.all_gather(down_weight, "seq", axis=0, tiled=True),
        lax.all_gather(down_bias, "seq", axis=0, tiled=True),
    )
    f32 = jnp.float32
    bf16 = jnp.bfloat16
    gain_first = first_gain.astype(f32)
    gain_second = second_gain.astype(f32)
    cell_count, seg_len, model_width = tokens.shape
    row_count = cell_count * seg_len
    head_shape = (cell_count, seg_len, HEADS, HDIM)
    cycle_size = lax.axis_size("seq")
    flat_input = tokens.reshape(row_count, model_width).astype(f32)
    standard_one, inverse_one = standardize(flat_input)
    normed_one = (standard_one * gain_first + first_bias.astype(f32)).astype(bf16)
    query_heads = (
        (matmul(normed_one, query_weight) + query_bias.astype(f32)).astype(bf16).reshape(head_shape)
    )
    key_heads = matmul(normed_one, key_weight).astype(bf16).reshape(head_shape)
    value_heads = (
        (matmul(normed_one, value_weight) + value_bias.astype(f32)).astype(bf16).reshape(head_shape)
    )
    running_max = jnp.full((cell_count, HEADS, seg_len), -1e30, f32)
    running_sum = jnp.zeros((cell_count, HEADS, seg_len), f32)
    weighted = jnp.zeros((cell_count, HEADS, seg_len, HDIM), f32)
    travel = (key_heads, value_heads)
    for step in range(cycle_size):
        if step > 0:
            travel = from_behind((travel[0], travel[1]), "seq", 1)
        scores = score_block(query_heads, travel[0])
        new_max = jnp.maximum(running_max, jnp.max(scores, axis=-1))
        rescale = jnp.exp(running_max - new_max)
        exp_scores = jnp.exp(scores - new_max[..., None])
        running_sum = running_sum * rescale + jnp.sum(exp_scores, axis=-1)
        weighted = weighted * rescale[..., None] + jnp.einsum(
            "chqk,ckhd->chqd", exp_scores.astype(bf16), travel[1], preferred_element_type=f32
        )
        running_max = new_max
    attended = weighted / running_sum[..., None]
    log_total = running_max + jnp.log(running_sum)
    mixed = attended.transpose(0, 2, 1, 3).reshape(row_count, model_width).astype(bf16)
    middle = flat_input + matmul(mixed, output_weight) + output_bias.astype(f32)
    standard_two, inverse_two = standardize(middle)
    normed_two = (standard_two * gain_second + second_bias.astype(f32)).astype(bf16)
    up_proj = matmul(normed_two, up_weight) + up_bias.astype(f32)
    hidden = gelu_value(up_proj).astype(bf16)
    result = middle + matmul(hidden, down_weight) + down_bias.astype(f32)
    result_out = result.astype(bf16).reshape(cell_count, seg_len, model_width)
    weight_cell = jnp.sqrt(query_counts.astype(f32) / 1000.0)
    grad_result = (out_grad.astype(f32) * weight_cell[:, None, None]).reshape(
        row_count, model_width
    )
    grad_ffn_out = grad_result.astype(bf16)
    grad_down_weight = weight_grad(hidden, grad_ffn_out)
    grad_down_bias = column_sum(grad_ffn_out)
    grad_up = (matmul_right_t(grad_ffn_out, down_weight) * gelu_slope(up_proj)).astype(bf16)
    grad_up_weight = weight_grad(normed_two, grad_up)
    grad_up_bias = column_sum(grad_up)
    grad_normed_two = matmul_right_t(grad_up, up_weight)
    grad_second_gain = jnp.sum(grad_normed_two * standard_two, axis=0)
    grad_second_bias = jnp.sum(grad_normed_two, axis=0)
    grad_middle = grad_result + standardize_back(
        grad_normed_two, standard_two, inverse_two, gain_second
    )
    grad_attn_out = grad_middle.astype(bf16)
    grad_output_weight = weight_grad(mixed, grad_attn_out)
    grad_output_bias = column_sum(grad_attn_out)
    grad_mixed = matmul_right_t(grad_attn_out, output_weight).astype(bf16).reshape(head_shape)
    row_delta = jnp.sum(grad_mixed.astype(f32).transpose(0, 2, 1, 3) * attended, axis=-1)
    grad_query_acc = jnp.zeros(head_shape, f32)
    moving = (jnp.zeros(head_shape, f32), jnp.zeros(head_shape, f32))
    travel = (key_heads, value_heads)
    for step in range(cycle_size):
        if step > 0:
            travel = from_behind((travel[0], travel[1]), "seq", 1)
        block_keys, block_values = travel
        scores = score_block(query_heads, block_keys)
        prob_block = jnp.exp(scores - log_total[..., None])
        part_values = jnp.einsum(
            "chqk,cqhd->ckhd", prob_block.astype(bf16), grad_mixed, preferred_element_type=f32
        )
        grad_probs = jnp.einsum(
            "cqhd,ckhd->chqk", grad_mixed, block_values, preferred_element_type=f32
        )
        grad_scores = (prob_block * (grad_probs - row_delta[..., None])).astype(bf16)
        grad_query_acc = (
            grad_query_acc
            + jnp.einsum("chqk,ckhd->cqhd", grad_scores, block_keys, preferred_element_type=f32)
            * 0.125
        )
        part_keys = (
            jnp.einsum("chqk,cqhd->ckhd", grad_scores, query_heads, preferred_element_type=f32)
            * 0.125
        )
        moving = from_behind(
            (for_sending(moving[0] + part_keys), for_sending(moving[1] + part_values)), "seq", 1
        )
    grad_queries = grad_query_acc.astype(bf16).reshape(row_count, model_width)
    grad_keys = moving[0].astype(bf16).reshape(row_count, model_width)
    grad_values = moving[1].astype(bf16).reshape(row_count, model_width)
    grad_query_weight = weight_grad(normed_one, grad_queries)
    grad_query_bias = column_sum(grad_queries)
    grad_key_weight = weight_grad(normed_one, grad_keys)
    grad_value_weight = weight_grad(normed_one, grad_values)
    grad_value_bias = column_sum(grad_values)
    grad_normed_one = (
        matmul_right_t(grad_queries, query_weight)
        + matmul_right_t(grad_keys, key_weight)
        + matmul_right_t(grad_values, value_weight)
    )
    grad_first_gain = jnp.sum(grad_normed_one * standard_one, axis=0)
    grad_first_bias = jnp.sum(grad_normed_one, axis=0)
    grad_input = grad_middle + standardize_back(
        grad_normed_one, standard_one, inverse_one, gain_first
    )
    input_grad = grad_input.astype(bf16).reshape(cell_count, seg_len, model_width)
    shared_all = (
        lax.psum_scatter(
            grad_first_gain.astype(jnp.bfloat16), "seq", scatter_dimension=0, tiled=True
        ).astype(jnp.float32),
        lax.psum_scatter(
            grad_first_bias.astype(jnp.bfloat16), "seq", scatter_dimension=0, tiled=True
        ).astype(jnp.float32),
        lax.psum_scatter(
            grad_query_weight.astype(jnp.bfloat16), "seq", scatter_dimension=0, tiled=True
        ).astype(jnp.float32),
        lax.psum_scatter(
            grad_query_bias.astype(jnp.bfloat16), "seq", scatter_dimension=0, tiled=True
        ).astype(jnp.float32),
        lax.psum_scatter(
            grad_key_weight.astype(jnp.bfloat16), "seq", scatter_dimension=0, tiled=True
        ).astype(jnp.float32),
        lax.psum_scatter(
            grad_value_weight.astype(jnp.bfloat16), "seq", scatter_dimension=0, tiled=True
        ).astype(jnp.float32),
        lax.psum_scatter(
            grad_value_bias.astype(jnp.bfloat16), "seq", scatter_dimension=0, tiled=True
        ).astype(jnp.float32),
        lax.psum_scatter(
            grad_output_weight.astype(jnp.bfloat16), "seq", scatter_dimension=0, tiled=True
        ).astype(jnp.float32),
        lax.psum_scatter(
            grad_output_bias.astype(jnp.bfloat16), "seq", scatter_dimension=0, tiled=True
        ).astype(jnp.float32),
        lax.psum_scatter(
            grad_second_gain.astype(jnp.bfloat16), "seq", scatter_dimension=0, tiled=True
        ).astype(jnp.float32),
        lax.psum_scatter(
            grad_second_bias.astype(jnp.bfloat16), "seq", scatter_dimension=0, tiled=True
        ).astype(jnp.float32),
        lax.psum_scatter(
            grad_up_weight.astype(jnp.bfloat16), "seq", scatter_dimension=0, tiled=True
        ).astype(jnp.float32),
        lax.psum_scatter(
            grad_up_bias.astype(jnp.bfloat16), "seq", scatter_dimension=0, tiled=True
        ).astype(jnp.float32),
        lax.psum_scatter(
            grad_down_weight.astype(jnp.bfloat16), "seq", scatter_dimension=0, tiled=True
        ).astype(jnp.float32),
        lax.psum_scatter(
            grad_down_bias.astype(jnp.bfloat16), "seq", scatter_dimension=0, tiled=True
        ).astype(jnp.float32),
    )
    (
        grad_first_gain,
        grad_first_bias,
        grad_query_weight,
        grad_query_bias,
        grad_key_weight,
        grad_value_weight,
        grad_value_bias,
        grad_output_weight,
        grad_output_bias,
        grad_second_gain,
        grad_second_bias,
        grad_up_weight,
        grad_up_bias,
        grad_down_weight,
        grad_down_bias,
    ) = shared_all
    (
        grad_first_gain,
        grad_first_bias,
        grad_query_weight,
        grad_query_bias,
        grad_key_weight,
        grad_value_weight,
        grad_value_bias,
        grad_output_weight,
        grad_output_bias,
        grad_second_gain,
        grad_second_bias,
        grad_up_weight,
        grad_up_bias,
        grad_down_weight,
        grad_down_bias,
    ) = (
        lax.psum(grad_first_gain.astype(jnp.bfloat16), "cell").astype(jnp.float32),
        lax.psum(grad_first_bias.astype(jnp.bfloat16), "cell").astype(jnp.float32),
        lax.psum(grad_query_weight.astype(jnp.bfloat16), "cell").astype(jnp.float32),
        lax.psum(grad_query_bias.astype(jnp.bfloat16), "cell").astype(jnp.float32),
        lax.psum(grad_key_weight.astype(jnp.bfloat16), "cell").astype(jnp.float32),
        lax.psum(grad_value_weight.astype(jnp.bfloat16), "cell").astype(jnp.float32),
        lax.psum(grad_value_bias.astype(jnp.bfloat16), "cell").astype(jnp.float32),
        lax.psum(grad_output_weight.astype(jnp.bfloat16), "cell").astype(jnp.float32),
        lax.psum(grad_output_bias.astype(jnp.bfloat16), "cell").astype(jnp.float32),
        lax.psum(grad_second_gain.astype(jnp.bfloat16), "cell").astype(jnp.float32),
        lax.psum(grad_second_bias.astype(jnp.bfloat16), "cell").astype(jnp.float32),
        lax.psum(grad_up_weight.astype(jnp.bfloat16), "cell").astype(jnp.float32),
        lax.psum(grad_up_bias.astype(jnp.bfloat16), "cell").astype(jnp.float32),
        lax.psum(grad_down_weight.astype(jnp.bfloat16), "cell").astype(jnp.float32),
        lax.psum(grad_down_bias.astype(jnp.bfloat16), "cell").astype(jnp.float32),
    )
    return (
        result_out,
        input_grad,
        grad_first_gain,
        grad_first_bias,
        grad_query_weight,
        grad_query_bias,
        grad_key_weight,
        grad_value_weight,
        grad_value_bias,
        grad_output_weight,
        grad_output_bias,
        grad_second_gain,
        grad_second_bias,
        grad_up_weight,
        grad_up_bias,
        grad_down_weight,
        grad_down_bias,
    )


Q_BLOCK = 256


MESH = pl.DeviceIdType.MESH
ANY = pl.BlockSpec(memory_space=pl.ANY)
EDGE = 640
WIDE = 256
RING = 10


class Spot:
    def __init__(self):
        self.x = lax.axis_index("seq")
        self.cell = lax.axis_index("cell")
        self.core = lax.rem(self.cell, 2)
        self.y = lax.rem(self.cell // 2, 2)
        self.low = lax.rem(self.cell // 4, 2)
        self.high = lax.rem(self.cell // 8, 2)

    def flip(self, index, bit):
        return {"cell": self.cell + bit - 2 * bit * index}

    def over(self, name):
        if name == "x":
            return {"seq": 1 - self.x}
        if name == "core":
            return self.flip(self.core, 1)
        if name == "diagonal":
            return {"seq": 1 - self.x, **self.flip(self.core, 1)}
        return self.flip(*{"y": (self.y, 2), "low": (self.low, 4), "high": (self.high, 8)}[name])

    def meet(self, names):
        barrier = pltpu.get_barrier_semaphore()
        for name in names:
            pl.semaphore_signal(barrier, inc=1, device_id=self.over(name), device_id_type=MESH)
        pl.semaphore_wait(barrier, len(names))

    def send(self, name, source, target, send_sem, recv_sem):
        return pltpu.make_async_remote_copy(
            source, target, send_sem, recv_sem, device_id=self.over(name), device_id_type=MESH
        )


def rows_at(start, size):
    return pl.ds(pl.multiple_of(start, 16), size)


def cols(start, size):
    return pl.ds(pl.multiple_of(start, 128), size)


def attend_pair(qkv, mixed, total_ref, pair, base):
    f32, bf16 = jnp.float32, jnp.bfloat16
    rows = qkv.shape[0]
    lane = lax.broadcasted_iota(jnp.int32, (1, 128), 1)
    here = pair * 128
    keys = qkv[:, cols(EDGE + here, 128)]
    values_t = qkv[:, cols(2 * EDGE + here, 128)].T
    for block in range(rows // Q_BLOCK):
        part = pl.ds(block * Q_BLOCK, Q_BLOCK)
        queries = qkv[part, cols(here, 128)] * jnp.asarray(0.125, bf16)
        outs = []
        for head in range(2):
            own = (lane // HDIM) == head
            scores = lax.dot_general(
                keys,
                jnp.where(own, queries, jnp.zeros_like(queries)),
                (((1,), (1,)), ((), ())),
                preferred_element_type=f32,
            )
            largest = jnp.max(scores, axis=0, keepdims=True)
            weights = jnp.exp(scores - largest)
            total = jnp.sum(weights, axis=0, keepdims=True)
            out = jnp.dot(
                values_t[head * HDIM : (head + 1) * HDIM, :],
                weights.astype(bf16),
                preferred_element_type=f32,
            )
            outs.append(out / total)
            total_ref[2 * pair + head, :, part] = largest + jnp.log(total)
        mixed[part, cols(base + here, 128)] = jnp.concatenate(outs, axis=0).T.astype(bf16)


def attend_back_pair(qkv, totals, keys_acc, values_acc, pair):
    f32, bf16 = jnp.float32, jnp.bfloat16
    rows = qkv.shape[0]
    size = Q_BLOCK
    lane = lax.broadcasted_iota(jnp.int32, (1, 128), 1)
    here, key_lanes, value_lanes, grad_lanes = (cols(i * EDGE + pair * 128, 128) for i in range(4))
    keys = qkv[:, key_lanes]
    keys_t = keys.T
    nt = (((1,), (1,)), ((), ()))
    keys_acc[...] = jnp.zeros_like(keys_acc)
    values_acc[...] = jnp.zeros_like(values_acc)

    @pl.loop(0, rows // size)
    def _(block):
        part = rows_at(block * size, size)
        queries = qkv[part, here] * jnp.asarray(0.125, bf16)
        grads = qkv[part, grad_lanes]
        values = qkv[:, value_lanes]
        outs = []
        key_part = value_part = 0.0
        for head in range(2):
            own = (lane // HDIM) == head
            q_own = jnp.where(own, queries, jnp.zeros_like(queries))
            g_own = jnp.where(own, grads, jnp.zeros_like(grads))
            scores = lax.dot_general(keys, q_own, nt, preferred_element_type=f32)
            probs = jnp.exp(scores - totals[2 * pair + head, :, cols(block * size, size)])
            grad_probs = lax.dot_general(values, g_own, nt, preferred_element_type=f32)
            delta = jnp.sum(probs * grad_probs, axis=0, keepdims=True)
            grad_scores = (probs * (grad_probs - delta)).astype(bf16)
            value_part += jnp.dot(probs.astype(bf16), g_own, preferred_element_type=f32)
            key_part += jnp.dot(grad_scores, q_own, preferred_element_type=f32)
            outs.append(jnp.dot(keys_t[head * HDIM : (head + 1) * HDIM, :], grad_scores, preferred_element_type=f32))
        qkv[part, here] = (jnp.concatenate(outs, axis=0) * 0.125).T.astype(bf16)
        keys_acc[...] += key_part
        values_acc[...] += value_part

    qkv[:, key_lanes] = keys_acc[...].astype(bf16)
    qkv[:, value_lanes] = values_acc[...].astype(bf16)


def layer_kernel(
    tokens, out_grad, counts, wq, wk, wv, wo, wup, wdown, v0, v1, v2, v3, v4, v5, v6, v7, v8,
    result_ref, input_ref, down_ref, up_ref, out_ref, q_ref, k_ref, v_ref, vec_ref, normed_spill, qkv_spill, mixed_spill,
    pair, scale, vec, qkv_w, out_w, up_w, down_w, normed, wide, grad_up, ffn, mid, partial_sum, taken, given, tot,
    keys_acc, values_acc, blocks, from_x, from_y, from_low, from_high, res, sums,
    cell_weight, vectors, send_sems, recv_sems, local_sems, side_send, side_recv, side_local, out_sems,
    sum_send, sum_recv, store_sems, load_sems, swap_send, swap_recv, swap_local, vec_send, vec_recv, vec_store_sem,
):
    f32, bf16 = jnp.float32, jnp.bfloat16
    at = Spot()
    x, core = at.x, at.core
    rows, width = tokens.shape
    both = 2 * rows
    top, bottom = pl.ds(0, rows), pl.ds(rows, rows)
    grad, tok = pair.at[top], pair.at[bottom]
    nt = (((1,), (1,)), ((), ()))
    tn = (((0,), (0,)), ((), ()))
    sums[0] = jnp.zeros(sums.shape[1:], f32)
    for i, ref in enumerate((v0, v1, v2, v3, v4, v5, v6, v7)):
        vectors[i : i + 1, :] = ref[...].astype(f32).reshape(1, EDGE)
    for i in range(4):
        vectors[8 + i : 9 + i, :] = v8[i * EDGE : (i + 1) * EDGE].astype(f32).reshape(1, EDGE)
    vectors[12:16, :] = jnp.zeros((4, EDGE), f32)
    cell_weight[...] = jnp.sqrt(jnp.full(cell_weight.shape, counts[0], jnp.int32).astype(f32) / 1000.0)
    at.meet(("x", "core", "diagonal", "y", "low", "high"))

    side = [(tokens, tok), (cell_weight, scale), (out_grad, grad)]
    diagonal = [at.send("diagonal", s, t, side_send.at[i], side_recv.at[i]) for i, (s, t) in enumerate(side)]
    straight = [pltpu.make_async_copy(s, t, side_local.at[i]) for i, (s, t) in enumerate(side)]

    def swap(i, remote, local):
        @pl.when(x != core)
        def _():
            remote(diagonal[i])

        @pl.when(x == core)
        def _():
            local(straight[i])

    def swap_start(i):
        swap(i, lambda c: c.start(), lambda c: c.start())

    def swap_wait(i):
        swap(i, lambda c: c.wait(), lambda c: c.wait())

    chunks = []
    for start in range(0, 3 * EDGE, WIDE):
        width_now = min(WIDE, 3 * EDGE - start)
        parts = []
        for i, ref in enumerate((wq, wk, wv)):
            low, high = max(start, i * EDGE), min(start + width_now, (i + 1) * EDGE)
            if low < high:
                parts.append((ref.at[:, cols(core * EDGE + low - i * EDGE, high - low)], low))
        chunks.append((parts, qkv_w, EDGE, 0, start, width_now))
    for start in range(0, 4 * EDGE, WIDE):
        part = start // (2 * EDGE) * 2 * EDGE + start + core * 2 * EDGE
        chunks.append(([(wup.at[:, cols(part, WIDE)], start)], up_w, EDGE, 0, start, WIDE))
    for start in range(0, 2 * EDGE, WIDE):
        source = wdown.at[rows_at(core * 2 * EDGE, EDGE), pl.ds(start, WIDE)]
        chunks.append(([(source, start)], down_w, 2 * EDGE, 0, start, WIDE))
    count = len(chunks)
    eighth = EDGE // 8
    place = at.y * 4 + at.low * 2 + at.high

    def region(k, half, start, size, column=None, width=None):
        _, ref, stride, row, first, most = chunks[k]
        column, width = (first, most) if column is None else (column, width)
        return ref.at[rows_at(half * stride + row + start * eighth, size * eighth), pl.ds(column, width)]

    ops = {}
    for k, chunk in enumerate(chunks):
        ops["x", k] = [
            at.send(
                "x",
                source.at[rows_at(place * eighth, eighth)],
                region(k, x, place, 1, column, source.shape[1]),
                send_sems.at[4 * j, k],
                recv_sems.at[4 * j, k],
            )
            for j, (source, column) in enumerate(chunk[0])
        ]
        for s, (name, start, size) in enumerate(
            (("high", place, 1), ("low", at.y * 4 + at.low * 2, 2), ("y", at.y * 4, 4))
        ):
            part = region(k, 1 - x, start, size)
            ops[name, k] = [at.send(name, part, part, send_sems.at[s + 1, k], recv_sems.at[s + 1, k])]
    direct = []
    for i, start in enumerate(range(0, 2 * EDGE, WIDE)):
        source = wdown.at[rows_at(core * 2 * EDGE + EDGE, EDGE), pl.ds(start, WIDE)]
        target = down_w.at[rows_at(x * 2 * EDGE + EDGE, EDGE), pl.ds(start, WIDE)]
        direct.append(at.send("x", source, target, send_sems.at[5, i], recv_sems.at[5, i]))
    owns = []
    mine = rows_at(x * EDGE, EDGE)
    for i, ref in enumerate((wq, wk, wv)):
        owns.append((ref.at[:, cols(core * EDGE, EDGE)], qkv_w.at[mine, pl.ds(i * EDGE, EDGE)]))
    for i in range(2):
        owns.append((wup.at[:, cols((2 * i + core) * 2 * EDGE, 2 * EDGE)], up_w.at[mine, pl.ds(i * 2 * EDGE, 2 * EDGE)]))
    owns.append((wdown.at[rows_at(core * 2 * EDGE, 2 * EDGE)], down_w.at[rows_at(x * 2 * EDGE, 2 * EDGE)]))
    owns = [pltpu.make_async_copy(source, target, local_sems.at[i]) for i, (source, target) in enumerate(owns)]
    half = EDGE // 2
    out_x = at.send(
        "x", wo.at[rows_at(core * half, half)], out_w.at[rows_at(x * EDGE + core * half, half)], side_send.at[4], side_recv.at[4]
    )
    part = out_w.at[rows_at((1 - x) * EDGE + core * half, half)]
    out_core = at.send("core", part, part, side_send.at[5], side_recv.at[5])
    out_local = pltpu.make_async_copy(wo, out_w.at[rows_at(x * EDGE, EDGE)], side_local.at[4])
    vec_x = at.send("x", vectors, vec.at[x], side_send.at[3], side_recv.at[3])
    vec_local = pltpu.make_async_copy(vectors, vec.at[x], side_local.at[3])
    def core_copy(i, source, target):
        return at.send("core", source, target, side_send.at[i], side_recv.at[i])

    normed_one_core = core_copy(6, normed.at[top], normed.at[bottom])
    heads = cols(core * EDGE, EDGE)
    mixed_core = [
        core_copy(7, ffn.at[top, heads], ffn.at[bottom, heads]),
        core_copy(8, ffn.at[bottom, heads], ffn.at[top, heads]),
    ]
    normed_two_core = core_copy(9, normed.at[top], normed.at[bottom])
    ffn_core = core_copy(10, ffn.at[top], ffn.at[bottom])

    spills = {}

    def put(name, source, target):
        spills[name] = pltpu.make_async_copy(source, target, out_sems.at[len(spills)])
        spills[name].start()

    stages = ("x", "high", "low", "y")

    def fetch(name, k):
        for op in ops[name, k]:
            op.start()

    def bring(t):
        for s, name in enumerate(stages):
            k = t - s
            if 0 <= k < count:
                for op in ops[name, k]:
                    op.wait_recv()
                if s < 3:
                    fetch(stages[s + 1], k)
        if t + 3 < count:
            fetch("x", t + 3)
        if t == 3:
            out_x.start()
        if t == 8:
            out_x.wait_recv()
            out_core.start()
        if t % 2 and 5 <= t < 5 + 2 * len(direct):
            direct[(t - 5) // 2].start()
        if t == 14:
            swap_start(2)
        if t in (1, 2, 4):
            for op in {1: (out_local,), 2: owns[3:5], 4: owns[5:]}[t]:
                op.start()

    fetch("x", 0)
    fetch("x", 1)
    fetch("x", 2)
    vec_x.start()
    swap_start(0)
    swap_start(1)
    vec_local.start()
    for op in owns[:3]:
        op.start()
    bring(0)
    bring(1)
    vec_x.wait_recv()
    vec_local.wait()

    def vector(i):
        return jnp.concatenate([vec[0, i : i + 1, :], vec[1, i : i + 1, :]], axis=1)

    def norm(values, gain, bias):
        average = jnp.mean(values, axis=-1, keepdims=True)
        centred = values - average
        inverse = lax.rsqrt(jnp.mean(centred * centred, axis=-1, keepdims=True) + 1e-05)
        return (centred * inverse * gain + bias).astype(bf16)

    swap_wait(0)
    gain_one, bias_one = vector(0), vector(1)

    @pl.loop(0, rows // 64)
    def _(i):
        here = rows_at(i * 64, 64)
        normed[here, :] = norm(tok[here, :].astype(f32), gain_one, bias_one)

    normed_one_core.start()
    bring(2)
    bring(3)
    normed_one_core.wait_recv()
    put("normed_one", normed, normed_spill)

    for i in range(3):
        for t in ((4, 5), (6, 7), (8, 9, 10))[i]:
            bring(t)
        owns[i].wait()
        lanes = pl.ds(i * EDGE, EDGE)
        bias = 0.0 if i == 1 else vec[core, 2 + i // 2 : 3 + i // 2, :]

        @pl.loop(0, 2 * rows // 256)
        def _(r):
            here = rows_at(r * 256, 256)
            value = jnp.dot(normed[here, :], qkv_w[:, lanes], preferred_element_type=f32)
            wide[here, lanes] = (value + bias).astype(bf16)

    put("qkv", wide.at[:, pl.ds(0, 3 * EDGE)], qkv_spill)

    @pl.loop(0, EDGE // 128)
    def _(two):
        attend_pair(wide, ffn, tot, two, core * EDGE)

        for i in range(5):

            @pl.when(two == i)
            def _():
                bring(11 + i)

    spills["normed_one"].wait()
    normed_one_core.wait_send()
    mixed_core[0].start()
    mixed_core[1].start()
    bring(16)
    out_local.wait()
    out_core.wait_recv()
    mixed_core[1].wait_recv()
    mixed_core[0].wait_recv()
    put("mixed", ffn, mixed_spill)
    gain_two, bias_two, out_bias = vector(5), vector(6), vector(4)

    @pl.loop(0, rows // 128)
    def _(r):
        here = rows_at(r * 128, 128)
        value = jnp.dot(ffn[here, :], out_w[...], preferred_element_type=f32)
        value = tok[here, :].astype(f32) + value + out_bias
        mid[here, :] = value
        normed[here, :] = norm(value, gain_two, bias_two)

    spills["mixed"].wait()
    spills["qkv"].wait()
    for op in mixed_core:
        op.wait_send()
    normed_two_core.start()
    bring(17)
    normed_two_core.wait_recv()
    up_bias = jnp.concatenate([vec[h, pl.ds(8 + core * 2 + i, 1), :] for h in range(2) for i in range(2)], axis=1)
    for i in range(4):
        if i % 2 == 0:
            owns[3 + i // 2].wait()
        lanes = pl.ds(i * EDGE, EDGE)
        bias = up_bias[:, i * EDGE : (i + 1) * EDGE]

        @pl.loop(0, both // 128)
        def _(r):
            here = rows_at(r * 128, 128)
            up = jnp.dot(normed[here, :], up_w[:, lanes], preferred_element_type=f32) + bias
            cdf = 0.5 * (1.0 + lax.erf(up * 0.7071067811865476))
            wide[here, lanes] = (up * cdf).astype(bf16)
            grad_up[here, lanes] = (cdf + up * jnp.exp(-0.5 * up * up) * 0.3989422804014327).astype(bf16)

        if i == 0:
            swap_wait(1)
            swap_wait(2)
            weight = scale[0:1, 0:1]

            @pl.loop(0, rows // 64)
            def _(r):
                here = rows_at(r * 64, 64)
                ffn[here, :] = (grad[here, :].astype(f32) * weight).astype(bf16)

            ffn_core.start()
        for t in ((18,), (19, 20), (21,), (22,))[i]:
            bring(t)
    ffn_core.wait_recv()

    pieces = []
    for i in range(2):
        for start in range(0, 2 * EDGE, WIDE):
            target = down_ref.at[rows_at(core * 2 * EDGE + i * EDGE, EDGE), pl.ds(start, WIDE)]
            pieces.append([(wide, 2 * EDGE, i * EDGE, ffn, start, WIDE, target)])
    for start in range(0, 4 * EDGE, WIDE):
        target = up_ref.at[:, cols(start // (2 * EDGE) * 2 * EDGE + start + core * 2 * EDGE, WIDE)]
        pieces.append([(normed, EDGE, 0, grad_up, start, WIDE, target)])
    mixed_rows = pl.ds(EDGE, both)

    def out_part(start, width):
        target = out_ref.at[:, cols(core * EDGE + start, width)]
        return (down_w.at[mixed_rows], EDGE, 0, ffn, core * EDGE + start, width, target)

    last = EDGE % WIDE
    pieces += [[out_part(start, WIDE)] for start in range(0, EDGE - last, WIDE)]
    for start in range(0, 3 * EDGE, WIDE):
        parts = []
        for i, ref in enumerate((q_ref, k_ref, v_ref)):
            first, end = max(start, i * EDGE), min(start + WIDE, (i + 1) * EDGE)
            if first < end:
                target = ref.at[:, cols(core * EDGE + first - i * EDGE, end - first)]
                parts.append((normed, EDGE, 0, wide, first, end - first, target))
        pieces.append(parts)
    pieces[-1].append(out_part(EDGE - last, last))
    total_count = len(pieces)

    half, quarter, eighth = EDGE // 2, EDGE // 4, EDGE // 8
    y0 = at.y * half
    l0 = y0 + at.low * quarter
    h0 = l0 + at.high * eighth
    sum_ops = {}
    for k, parts in enumerate(pieces):
        acc, four, slot, sem = k % 6, k % 4, k % 7, k % RING
        hops = (
            ("x", "x", blocks.at[6 + k % 3], from_x.at[four]),
            ("y", "y", blocks.at[acc, rows_at((1 - at.y) * half, half)], from_y.at[four]),
            ("low", "low", blocks.at[acc, rows_at(y0 + (1 - at.low) * quarter, quarter)], from_low.at[four]),
            ("high", "high", blocks.at[acc, rows_at(l0 + (1 - at.high) * eighth, eighth)], from_high.at[four]),
            ("all_high", "high", res.at[slot, rows_at(h0, eighth)], res.at[slot, rows_at(h0, eighth)]),
            ("all_low", "low", res.at[slot, rows_at(l0, quarter)], res.at[slot, rows_at(l0, quarter)]),
            ("all_y", "y", res.at[slot, rows_at(y0, half)], res.at[slot, rows_at(y0, half)]),
        )
        for s, (stage, name, source, goal) in enumerate(hops):
            sum_ops[stage, k] = [at.send(name, source, goal, sum_send.at[s, sem], sum_recv.at[s, sem])]
        sum_ops["core", k] = []
        sum_ops["store", k] = []
        start = 0
        for s, part in enumerate(parts):
            source = res.at[slot, :, pl.ds(start, part[5])]
            sum_ops["core", k].append(at.send("core", source, part[6], sum_send.at[7 + s, sem], sum_recv.at[7 + s, sem]))
            sum_ops["store", k].append(pltpu.make_async_copy(source, part[6], store_sems.at[s, sem]))
            start += part[5]

    def begin(stage, k):
        for op in sum_ops[stage, k]:
            op.start()

    def came(stage, k):
        for op in sum_ops[stage, k]:
            op.wait_recv()

    def left_here(stage, k):
        for op in sum_ops[stage, k]:
            op.wait_send()

    def make(k):
        @pl.loop(0, 2)
        def _(j):
            of = j * x + (1 - j) * (1 - x)
            slot = j * (k % 6) + (1 - j) * (6 + k % 3)
            start = 0
            for left, stride, left_at, right, right_at, width_now, _ in pieces[k]:
                lanes = right_at if isinstance(right_at, int) else pl.multiple_of(right_at, 128)
                product = lax.dot_general(
                    left[:, cols(of * stride + left_at, EDGE)],
                    right[:, pl.ds(lanes, width_now)],
                    tn,
                    preferred_element_type=f32,
                )
                blocks[slot, :, start : start + width_now] = product.astype(bf16)
                start += width_now

        begin("x", k)

    def add(k, start, size, other, goal, goal_slot):
        @pl.loop(0, size // 80)
        def _(i):
            here = rows_at(start + i * 80, 80)
            there = rows_at(i * 80, 80)
            total = blocks[k % 6, here, :].astype(f32) + other[there, :].astype(f32)
            goal[goal_slot, here, :] = total.astype(bf16)

    def tick(t):
        k = t
        if 0 <= k < total_count:
            came("x", k)
            add(k, 0, EDGE, from_x.at[k % 4], blocks, k % 6)
            begin("y", k)
            if k >= 1:
                left_here("x", k - 1)
            if k + 2 < total_count:
                make(k + 2)
        k = t - 1
        if 0 <= k < total_count:
            came("y", k)
            add(k, y0, half, from_y.at[k % 4], blocks, k % 6)
            begin("low", k)
        k = t - 2
        if 0 <= k < total_count:
            came("low", k)
            add(k, l0, quarter, from_low.at[k % 4], blocks, k % 6)
            begin("high", k)
        k = t - 3
        if 0 <= k < total_count:
            came("high", k)
            add(k, h0, eighth, from_high.at[k % 4], res, k % 7)
            begin("all_high", k)
            for stage in ("y", "low", "high"):
                left_here(stage, k)
        for before, stage, after in ((4, "all_high", "all_low"), (5, "all_low", "all_y"), (6, "all_y", "core")):
            k = t - before
            if 0 <= k < total_count:
                came(stage, k)
                begin(after, k)
                if after == "core":
                    begin("store", k)
        k = t - 7
        if 0 <= k < total_count:
            came("core", k)
            for stage in ("all_high", "all_low", "all_y", "core"):
                left_here(stage, k)
            for op in sum_ops["store", k]:
                op.wait()

    two_copy = core_copy(11, given.at[0], taken.at[0])
    result_copy = core_copy(12, given.at[1], taken.at[1])
    attn_copy = core_copy(13, ffn.at[top], ffn.at[bottom])
    one_copy = core_copy(14, given.at[0], taken.at[0])
    swaps = []
    for i, target in enumerate((result_ref, input_ref)):
        source = taken.at[1 - i]
        swaps.append(
            (
                at.send("diagonal", source, target, swap_send.at[i], swap_recv.at[i]),
                pltpu.make_async_copy(source, target, swap_local.at[i]),
            )
        )

    def swap_back(i, act):
        @pl.when(x != core)
        def _():
            act(swaps[i][0])

        @pl.when(x == core)
        def _():
            act(swaps[i][1])

    def add_vector(i, value):
        total = jnp.sum(value, axis=0, keepdims=True)
        sums[0, 2 * i : 2 * i + 1, :] += total[:, :EDGE]
        sums[0, 2 * i + 1 : 2 * i + 2, :] += total[:, EDGE:]

    def norm_back(values, grad_normed, gain):
        average = jnp.mean(values, axis=-1, keepdims=True)
        centred = values - average
        inverse = lax.rsqrt(jnp.mean(centred * centred, axis=-1, keepdims=True) + 1e-05)
        standard = centred * inverse
        scaled = grad_normed * gain
        back = inverse * (
            scaled
            - jnp.mean(scaled, axis=-1, keepdims=True)
            - standard * jnp.mean(scaled * standard, axis=-1, keepdims=True)
        )
        return standard, back

    make(0)
    make(1)
    for t in (23, 24, 25):
        bring(t)
    owns[5].wait()
    for op in direct:
        op.wait()
    normed_two_core.wait_send()
    loads = {}

    def load(name, source, target):
        loads[name] = pltpu.make_async_copy(source, target, load_sems.at[len(loads)])
        loads[name].start()

    for i in range(4):
        lanes = pl.ds(i * EDGE, EDGE)
        row = pl.ds(16 + 2 * (core * 2 + i % 2) + i // 2, 1)

        @pl.loop(0, both // 256)
        def _(r):
            here = rows_at(r * 256, 256)
            value = lax.dot_general(ffn[here, :], down_w[lanes, :], nt, preferred_element_type=f32)
            value = (value * grad_up[here, lanes].astype(f32)).astype(bf16)
            grad_up[here, lanes] = value
            sums[0, row, :] += jnp.sum(value.astype(f32), axis=0, keepdims=True)

        tick(i)

    @pl.loop(0, rows // 256)
    def _(r):
        value = lax.dot_general(grad_up[rows_at(rows + r * 256, 256), :], up_w[...], nt, preferred_element_type=f32)
        given[0, rows_at(r * 256, 256), :] = value.astype(bf16)

    two_copy.start()
    tick(4)

    @pl.loop(0, rows // 256)
    def _(r):
        value = lax.dot_general(grad_up[rows_at(r * 256, 256), :], up_w[...], nt, preferred_element_type=f32)
        partial_sum[rows_at(r * 256, 256), :] = value

    tick(5)

    @pl.loop(0, rows // 256)
    def _(r):
        value = jnp.dot(wide[rows_at(rows + r * 256, 256), :], down_w[...], preferred_element_type=f32)
        given[1, rows_at(r * 256, 256), :] = value.astype(bf16)

    tick(6)
    tick(7)
    result_copy.start()
    two_copy.wait_recv()
    result_copy.wait_recv()
    down_bias = vector(7)

    @pl.loop(0, rows // 128)
    def _(r):
        here = rows_at(r * 128, 128)
        value = jnp.dot(wide[here, :], down_w[...], preferred_element_type=f32)
        value = mid[here, :] + value + taken[1, here, :].astype(f32) + down_bias
        taken[1, here, :] = value.astype(bf16)

    swap_back(0, lambda copy: copy.start())
    for k in range(count):
        for name in stages:
            for op in ops[name, k]:
                op.wait_send()
    for op in (ffn_core, out_x, out_core, vec_x):
        op.wait_send()
    load("qkv", qkv_spill, wide.at[:, pl.ds(0, 3 * EDGE)])
    load("mixed", mixed_spill, down_w.at[mixed_rows])
    weight = scale[0:1, 0:1]
    tick(8)

    @pl.loop(0, rows // 32)
    def _(r):
        here = rows_at(r * 32, 32)
        add_vector(7, ffn[here, :].astype(f32))
        grad_normed = partial_sum[here, :] + taken[0, here, :].astype(f32)
        standard, back = norm_back(mid[here, :], grad_normed, gain_two)
        add_vector(5, grad_normed * standard)
        add_vector(6, grad_normed)
        value = pair[here, :].astype(f32) * weight + back
        mid[here, :] = value
        value = value.astype(bf16)
        ffn[here, :] = value
        add_vector(4, value.astype(f32))

    attn_copy.start()
    two_copy.wait_send()
    tick(9)
    attn_copy.wait_recv()

    @pl.loop(0, both // 256)
    def _(r):
        here = rows_at(r * 256, 256)
        value = lax.dot_general(ffn[here, :], out_w[rows_at(core * EDGE, EDGE), :], nt, preferred_element_type=f32)
        wide[here, pl.ds(3 * EDGE, EDGE)] = value.astype(bf16)

    loads["qkv"].wait()
    tick(10)

    @pl.loop(0, EDGE // 128)
    def _(two):
        attend_back_pair(wide, tot, keys_acc, values_acc, two)
        for i in range(5):

            @pl.when(two == i)
            def _():
                tick(11 + i)

    weights = pl.ds(0, 3 * EDGE)

    @pl.loop(0, rows // 256)
    def _(r):
        value = lax.dot_general(
            wide[rows_at(rows + r * 256, 256), weights], qkv_w[...], nt, preferred_element_type=f32
        )
        given[0, rows_at(r * 256, 256), :] = value.astype(bf16)

    one_copy.start()
    tick(16)
    tick(17)
    load("normed_one", normed_spill, normed)
    loads["mixed"].wait()

    @pl.loop(0, rows // 256)
    def _(r):
        value = lax.dot_general(wide[rows_at(r * 256, 256), weights], qkv_w[...], nt, preferred_element_type=f32)
        partial_sum[rows_at(r * 256, 256), :] = value

    tick(18)
    one_copy.wait_recv()

    @pl.loop(0, rows // 32)
    def _(r):
        here = rows_at(r * 32, 32)
        tok = pair[rows_at(rows + r * 32, 32), :].astype(f32)
        grad_normed = partial_sum[here, :] + taken[0, here, :].astype(f32)
        standard, back = norm_back(tok, grad_normed, gain_one)
        add_vector(0, grad_normed * standard)
        add_vector(1, grad_normed)
        taken[0, here, :] = (mid[here, :] + back).astype(bf16)

    swap_back(1, lambda copy: copy.start())
    tick(19)
    loads["normed_one"].wait()

    @pl.loop(0, both // 128)
    def _(r):
        here = rows_at(r * 128, 128)
        for i in (0, 2):
            row = pl.ds(4 + i + core, 1)
            value = wide[here, pl.ds(i * EDGE, EDGE)].astype(f32)
            sums[0, row, :] += jnp.sum(value, axis=0, keepdims=True)

    names = ("x", "core", "y", "low", "high")
    vec_ops = [at.send(name, sums.at[i], sums.at[6 + i], vec_send.at[i], vec_recv.at[i]) for i, name in enumerate(names)]
    vec_ops[0].start()
    for t in range(20, total_count + 7):
        tick(t)
        if t < 25:
            i = t - 20
            vec_ops[i].wait_recv()
            sums[i + 1] = sums[i] + sums[6 + i]
            if i < 4:
                vec_ops[i + 1].start()
    vec_store = pltpu.make_async_copy(sums.at[5], vec_ref, vec_store_sem.at[0])
    vec_store.start()
    vec_store.wait()
    for op in (result_copy, attn_copy, one_copy, *vec_ops):
        op.wait_send()
    swap_back(0, lambda copy: copy.wait())
    swap_back(1, lambda copy: copy.wait())
    left_here("x", total_count - 1)


def layer(*args):
    bf16, f32 = jnp.bfloat16, jnp.float32
    rows, width = args[0].shape
    both = 2 * rows
    outs = [
        ((rows, width), bf16),
        ((rows, width), bf16),
        ((4 * EDGE, width), bf16),
        ((EDGE, 8 * EDGE), bf16),
        ((EDGE, width), bf16),
        ((EDGE, width), bf16),
        ((EDGE, width), bf16),
        ((EDGE, width), bf16),
        ((24, EDGE), f32),
        ((both, width), bf16),
        ((both, 3 * EDGE), bf16),
        ((both, width), bf16),
    ]
    scratch = [
        ((both, width), bf16),
        ((8, 128), f32),
        ((2, 16, EDGE), f32),
        ((width, 3 * EDGE), bf16),
        ((width, width), bf16),
        ((width, 4 * EDGE), bf16),
        ((4 * EDGE, width), bf16),
        ((both, width), bf16),
        ((both, 4 * EDGE), bf16),
        ((both, 4 * EDGE), bf16),
        ((both, width), bf16),
        ((rows, width), f32),
        ((rows, width), f32),
        ((2, rows, width), bf16),
        ((2, rows, width), bf16),
        ((EDGE // HDIM, 1, both), f32),
        ((both, 128), f32),
        ((both, 128), f32),
        ((9, EDGE, WIDE), bf16),
        ((4, EDGE, WIDE), bf16),
        ((4, EDGE // 2, WIDE), bf16),
        ((4, EDGE // 4, WIDE), bf16),
        ((4, EDGE // 8, WIDE), bf16),
        ((7, EDGE, WIDE), bf16),
        ((11, 24, EDGE), f32),
        ((8, 128), f32),
        ((16, EDGE), f32),
    ]
    dma = pltpu.SemaphoreType.DMA
    sizes = [(6, 23), (6, 23), (6,), (15,), (15,), (5,), (3,), (9, RING), (9, RING), (2, RING), (3,)]
    sizes += [(2,), (2,), (2,), (5,), (5,), (1,)]
    return pl.pallas_call(
        layer_kernel,
        in_specs=[ANY] * 2 + [pl.BlockSpec(memory_space=pltpu.SMEM)] + [ANY] * 6 + [pl.BlockSpec(memory_space=pltpu.VMEM)] * 9,
        out_specs=[ANY] * len(outs),
        out_shape=[jax.ShapeDtypeStruct(*out) for out in outs],
        scratch_shapes=[pltpu.VMEM(*array) for array in scratch] + [dma(size) for size in sizes],
        compiler_params=pltpu.CompilerParams(
            collective_id=0, has_side_effects=True, vmem_limit_bytes=64 * 1024 * 1024
        ),
        name="layer",
    )(*args)


def widen_kernel(*refs):
    half = len(refs) // 2
    for source, target in zip(refs[:half], refs[half:]):
        target[...] = source[...].astype(target.dtype)


def widen(*arrays):
    steps = 4
    specs = [pl.BlockSpec((a.shape[0] // steps, a.shape[1]), lambda i: (i, 0)) for a in arrays]
    types = [jnp.float32] * (len(arrays) - 2) + [jnp.bfloat16] * 2
    return pl.pallas_call(
        widen_kernel,
        grid=(steps,),
        in_specs=specs,
        out_specs=specs,
        out_shape=[jax.ShapeDtypeStruct(a.shape, kind) for a, kind in zip(arrays, types)],
        compiler_params=pltpu.CompilerParams(vmem_limit_bytes=64 * 1024 * 1024),
        name="widen",
    )(*arrays)


def tuned(
    tokens,
    out_grad,
    query_counts,
    first_gain,
    first_bias,
    query_weight,
    query_bias,
    key_weight,
    value_weight,
    value_bias,
    output_weight,
    output_bias,
    second_gain,
    second_bias,
    up_weight,
    up_bias,
    down_weight,
    down_bias,
):
    f32, bf16 = jnp.float32, jnp.bfloat16
    x = lax.axis_index("seq")
    head_width = tokens.shape[2] // 2

    result, input_grad, down, up, out, query, key, value, sums, *_ = layer(
        tokens[0],
        out_grad[0],
        query_counts,
        query_weight,
        key_weight,
        value_weight,
        output_weight,
        up_weight,
        down_weight,
        first_gain,
        first_bias,
        query_bias,
        value_bias,
        output_bias,
        second_gain,
        second_bias,
        down_bias,
        up_bias,
    )
    out, query, key, value, up, down, result, input_grad = widen(out, query, key, value, up, down, result, input_grad)
    sums = lax.dynamic_index_in_dim(sums.reshape(12, 2, head_width), x, 1, keepdims=False)
    up_sum = sums[8:].reshape(-1)
    return (
        result[None],
        input_grad[None],
        sums[0],
        sums[1],
        query,
        sums[2],
        key,
        value,
        sums[3],
        out,
        sums[4],
        sums[5],
        sums[6],
        up,
        up_sum,
        down,
        sums[7],
    )


def chosen(mesh):
    cells, blocks = mesh.shape["cell"], mesh.shape["seq"]

    def per_device(tokens, *rest):
        if blocks == 2 and cells == 16 and tokens.shape == (1, 512, 1280):
            return tuned(tokens, *rest)
        return general(tokens, *rest)

    return per_device


def solution(mesh):
    placed = (
        P("cell", "seq", None),
        P("cell", "seq", None),
        P("cell"),
        P("seq"),
        P("seq"),
        P("seq", None),
        P("seq"),
        P("seq", None),
        P("seq", None),
        P("seq"),
        P("seq", None),
        P("seq"),
        P("seq"),
        P("seq"),
        P("seq", None),
        P("seq"),
        P("seq", None),
        P("seq"),
    )
    return jax.shard_map(
        chosen(mesh),
        mesh=mesh,
        in_specs=placed,
        out_specs=(
            P("cell", "seq", None),
            P("cell", "seq", None),
            P("seq"),
            P("seq"),
            P("seq", None),
            P("seq"),
            P("seq", None),
            P("seq", None),
            P("seq"),
            P("seq", None),
            P("seq"),
            P("seq"),
            P("seq"),
            P("seq", None),
            P("seq"),
            P("seq", None),
            P("seq"),
        ),
        check_vma=False,
    )
```

```python
import jax
import jax.numpy as jnp
from jax import lax
from jax.experimental import pallas as pl
from jax.experimental.pallas import tpu as pltpu
from jax.sharding import PartitionSpec as P

HEADS = 20
HDIM = 64


def from_behind(value, axis, steps):
    count = lax.axis_size(axis)
    pairs = [(source, (source + steps) % count) for source in range(count)]
    return lax.ppermute(value, axis, pairs)


def for_sending(x):
    return jax.tree.map(lambda a: a.astype(jnp.bfloat16) if a.dtype == jnp.float32 else a, x)


def matmul(left, right):
    return jnp.dot(left, right, preferred_element_type=jnp.float32)


def matmul_right_t(left, right):
    return jnp.einsum("to,io->ti", left, right, preferred_element_type=jnp.float32)


def weight_grad(left, right):
    return jnp.einsum("ti,to->io", left, right, preferred_element_type=jnp.float32)


def standardize(values):
    average = jnp.mean(values, axis=-1, keepdims=True)
    centred = values - average
    inverse = lax.rsqrt(jnp.mean(centred * centred, axis=-1, keepdims=True) + 1e-05)
    return (centred * inverse, inverse)


def standardize_back(grad_normed, standard, inverse, gain_vec):
    scaled = grad_normed * gain_vec
    return inverse * (
        scaled
        - jnp.mean(scaled, axis=-1, keepdims=True)
        - standard * jnp.mean(scaled * standard, axis=-1, keepdims=True)
    )


def gelu_value(up_proj):
    return 0.5 * up_proj * (1.0 + lax.erf(up_proj * 0.7071067811865476))


def gelu_slope(up_proj):
    return (
        0.5 * (1.0 + lax.erf(up_proj * 0.7071067811865476))
        + up_proj * jnp.exp(-0.5 * up_proj * up_proj) * 0.3989422804014327
    )


def score_block(queries, key_rows):
    return (
        jnp.einsum("cqhd,ckhd->chqk", queries, key_rows, preferred_element_type=jnp.float32) * 0.125
    )


def column_sum(values):
    return jnp.sum(values.astype(jnp.float32), axis=0)


def general(
    tokens,
    out_grad,
    query_counts,
    first_gain,
    first_bias,
    query_weight,
    query_bias,
    key_weight,
    value_weight,
    value_bias,
    output_weight,
    output_bias,
    second_gain,
    second_bias,
    up_weight,
    up_bias,
    down_weight,
    down_bias,
):
    (
        first_gain,
        first_bias,
        query_weight,
        query_bias,
        key_weight,
        value_weight,
        value_bias,
        output_weight,
        output_bias,
        second_gain,
        second_bias,
        up_weight,
        up_bias,
        down_weight,
        down_bias,
    ) = (
        lax.all_gather(first_gain, "seq", axis=0, tiled=True),
        lax.all_gather(first_bias, "seq", axis=0, tiled=True),
        lax.all_gather(query_weight, "seq", axis=0, tiled=True),
        lax.all_gather(query_bias, "seq", axis=0, tiled=True),
        lax.all_gather(key_weight, "seq", axis=0, tiled=True),
        lax.all_gather(value_weight, "seq", axis=0, tiled=True),
        lax.all_gather(value_bias, "seq", axis=0, tiled=True),
        lax.all_gather(output_weight, "seq", axis=0, tiled=True),
        lax.all_gather(output_bias, "seq", axis=0, tiled=True),
        lax.all_gather(second_gain, "seq", axis=0, tiled=True),
        lax.all_gather(second_bias, "seq", axis=0, tiled=True),
        lax.all_gather(up_weight, "seq", axis=0, tiled=True),
        lax.all_gather(up_bias, "seq", axis=0, tiled=True),
        lax.all_gather(down_weight, "seq", axis=0, tiled=True),
        lax.all_gather(down_bias, "seq", axis=0, tiled=True),
    )
    f32 = jnp.float32
    bf16 = jnp.bfloat16
    gain_first = first_gain.astype(f32)
    gain_second = second_gain.astype(f32)
    cell_count, seg_len, model_width = tokens.shape
    row_count = cell_count * seg_len
    head_shape = (cell_count, seg_len, HEADS, HDIM)
    cycle_size = lax.axis_size("seq")
    flat_input = tokens.reshape(row_count, model_width).astype(f32)
    standard_one, inverse_one = standardize(flat_input)
    normed_one = (standard_one * gain_first + first_bias.astype(f32)).astype(bf16)
    query_heads = (
        (matmul(normed_one, query_weight) + query_bias.astype(f32)).astype(bf16).reshape(head_shape)
    )
    key_heads = matmul(normed_one, key_weight).astype(bf16).reshape(head_shape)
    value_heads = (
        (matmul(normed_one, value_weight) + value_bias.astype(f32)).astype(bf16).reshape(head_shape)
    )
    running_max = jnp.full((cell_count, HEADS, seg_len), -1e30, f32)
    running_sum = jnp.zeros((cell_count, HEADS, seg_len), f32)
    weighted = jnp.zeros((cell_count, HEADS, seg_len, HDIM), f32)
    travel = (key_heads, value_heads)
    for step in range(cycle_size):
        if step > 0:
            travel = from_behind((travel[0], travel[1]), "seq", 1)
        scores = score_block(query_heads, travel[0])
        new_max = jnp.maximum(running_max, jnp.max(scores, axis=-1))
        rescale = jnp.exp(running_max - new_max)
        exp_scores = jnp.exp(scores - new_max[..., None])
        running_sum = running_sum * rescale + jnp.sum(exp_scores, axis=-1)
        weighted = weighted * rescale[..., None] + jnp.einsum(
            "chqk,ckhd->chqd", exp_scores.astype(bf16), travel[1], preferred_element_type=f32
        )
        running_max = new_max
    attended = weighted / running_sum[..., None]
    log_total = running_max + jnp.log(running_sum)
    mixed = attended.transpose(0, 2, 1, 3).reshape(row_count, model_width).astype(bf16)
    middle = flat_input + matmul(mixed, output_weight) + output_bias.astype(f32)
    standard_two, inverse_two = standardize(middle)
    normed_two = (standard_two * gain_second + second_bias.astype(f32)).astype(bf16)
    up_proj = matmul(normed_two, up_weight) + up_bias.astype(f32)
    hidden = gelu_value(up_proj).astype(bf16)
    result = middle + matmul(hidden, down_weight) + down_bias.astype(f32)
    result_out = result.astype(bf16).reshape(cell_count, seg_len, model_width)
    weight_cell = jnp.sqrt(query_counts.astype(f32) / 1000.0)
    grad_result = (out_grad.astype(f32) * weight_cell[:, None, None]).reshape(
        row_count, model_width
    )
    grad_ffn_out = grad_result.astype(bf16)
    grad_down_weight = weight_grad(hidden, grad_ffn_out)
    grad_down_bias = column_sum(grad_ffn_out)
    grad_up = (matmul_right_t(grad_ffn_out, down_weight) * gelu_slope(up_proj)).astype(bf16)
    grad_up_weight = weight_grad(normed_two, grad_up)
    grad_up_bias = column_sum(grad_up)
    grad_normed_two = matmul_right_t(grad_up, up_weight)
    grad_second_gain = jnp.sum(grad_normed_two * standard_two, axis=0)
    grad_second_bias = jnp.sum(grad_normed_two, axis=0)
    grad_middle = grad_result + standardize_back(
        grad_normed_two, standard_two, inverse_two, gain_second
    )
    grad_attn_out = grad_middle.astype(bf16)
    grad_output_weight = weight_grad(mixed, grad_attn_out)
    grad_output_bias = column_sum(grad_attn_out)
    grad_mixed = matmul_right_t(grad_attn_out, output_weight).astype(bf16).reshape(head_shape)
    row_delta = jnp.sum(grad_mixed.astype(f32).transpose(0, 2, 1, 3) * attended, axis=-1)
    grad_query_acc = jnp.zeros(head_shape, f32)
    moving = (jnp.zeros(head_shape, f32), jnp.zeros(head_shape, f32))
    travel = (key_heads, value_heads)
    for step in range(cycle_size):
        if step > 0:
            travel = from_behind((travel[0], travel[1]), "seq", 1)
        block_keys, block_values = travel
        scores = score_block(query_heads, block_keys)
        prob_block = jnp.exp(scores - log_total[..., None])
        part_values = jnp.einsum(
            "chqk,cqhd->ckhd", prob_block.astype(bf16), grad_mixed, preferred_element_type=f32
        )
        grad_probs = jnp.einsum(
            "cqhd,ckhd->chqk", grad_mixed, block_values, preferred_element_type=f32
        )
        grad_scores = (prob_block * (grad_probs - row_delta[..., None])).astype(bf16)
        grad_query_acc = (
            grad_query_acc
            + jnp.einsum("chqk,ckhd->cqhd", grad_scores, block_keys, preferred_element_type=f32)
            * 0.125
        )
        part_keys = (
            jnp.einsum("chqk,cqhd->ckhd", grad_scores, query_heads, preferred_element_type=f32)
            * 0.125
        )
        moving = from_behind(
            (for_sending(moving[0] + part_keys), for_sending(moving[1] + part_values)), "seq", 1
        )
    grad_queries = grad_query_acc.astype(bf16).reshape(row_count, model_width)
    grad_keys = moving[0].astype(bf16).reshape(row_count, model_width)
    grad_values = moving[1].astype(bf16).reshape(row_count, model_width)
    grad_query_weight = weight_grad(normed_one, grad_queries)
    grad_query_bias = column_sum(grad_queries)
    grad_key_weight = weight_grad(normed_one, grad_keys)
    grad_value_weight = weight_grad(normed_one, grad_values)
    grad_value_bias = column_sum(grad_values)
    grad_normed_one = (
        matmul_right_t(grad_queries, query_weight)
        + matmul_right_t(grad_keys, key_weight)
        + matmul_right_t(grad_values, value_weight)
    )
    grad_first_gain = jnp.sum(grad_normed_one * standard_one, axis=0)
    grad_first_bias = jnp.sum(grad_normed_one, axis=0)
    grad_input = grad_middle + standardize_back(
        grad_normed_one, standard_one, inverse_one, gain_first
    )
    input_grad = grad_input.astype(bf16).reshape(cell_count, seg_len, model_width)
    shared_all = (
        lax.psum_scatter(
            grad_first_gain.astype(jnp.bfloat16), "seq", scatter_dimension=0, tiled=True
        ).astype(jnp.float32),
        lax.psum_scatter(
            grad_first_bias.astype(jnp.bfloat16), "seq", scatter_dimension=0, tiled=True
        ).astype(jnp.float32),
        lax.psum_scatter(
            grad_query_weight.astype(jnp.bfloat16), "seq", scatter_dimension=0, tiled=True
        ).astype(jnp.float32),
        lax.psum_scatter(
            grad_query_bias.astype(jnp.bfloat16), "seq", scatter_dimension=0, tiled=True
        ).astype(jnp.float32),
        lax.psum_scatter(
            grad_key_weight.astype(jnp.bfloat16), "seq", scatter_dimension=0, tiled=True
        ).astype(jnp.float32),
        lax.psum_scatter(
            grad_value_weight.astype(jnp.bfloat16), "seq", scatter_dimension=0, tiled=True
        ).astype(jnp.float32),
        lax.psum_scatter(
            grad_value_bias.astype(jnp.bfloat16), "seq", scatter_dimension=0, tiled=True
        ).astype(jnp.float32),
        lax.psum_scatter(
            grad_output_weight.astype(jnp.bfloat16), "seq", scatter_dimension=0, tiled=True
        ).astype(jnp.float32),
        lax.psum_scatter(
            grad_output_bias.astype(jnp.bfloat16), "seq", scatter_dimension=0, tiled=True
        ).astype(jnp.float32),
        lax.psum_scatter(
            grad_second_gain.astype(jnp.bfloat16), "seq", scatter_dimension=0, tiled=True
        ).astype(jnp.float32),
        lax.psum_scatter(
            grad_second_bias.astype(jnp.bfloat16), "seq", scatter_dimension=0, tiled=True
        ).astype(jnp.float32),
        lax.psum_scatter(
            grad_up_weight.astype(jnp.bfloat16), "seq", scatter_dimension=0, tiled=True
        ).astype(jnp.float32),
        lax.psum_scatter(
            grad_up_bias.astype(jnp.bfloat16), "seq", scatter_dimension=0, tiled=True
        ).astype(jnp.float32),
        lax.psum_scatter(
            grad_down_weight.astype(jnp.bfloat16), "seq", scatter_dimension=0, tiled=True
        ).astype(jnp.float32),
        lax.psum_scatter(
            grad_down_bias.astype(jnp.bfloat16), "seq", scatter_dimension=0, tiled=True
        ).astype(jnp.float32),
    )
    (
        grad_first_gain,
        grad_first_bias,
        grad_query_weight,
        grad_query_bias,
        grad_key_weight,
        grad_value_weight,
        grad_value_bias,
        grad_output_weight,
        grad_output_bias,
        grad_second_gain,
        grad_second_bias,
        grad_up_weight,
        grad_up_bias,
        grad_down_weight,
        grad_down_bias,
    ) = shared_all
    (
        grad_first_gain,
        grad_first_bias,
        grad_query_weight,
        grad_query_bias,
        grad_key_weight,
        grad_value_weight,
        grad_value_bias,
        grad_output_weight,
        grad_output_bias,
        grad_second_gain,
        grad_second_bias,
        grad_up_weight,
        grad_up_bias,
        grad_down_weight,
        grad_down_bias,
    ) = (
        lax.psum(grad_first_gain.astype(jnp.bfloat16), "cell").astype(jnp.float32),
        lax.psum(grad_first_bias.astype(jnp.bfloat16), "cell").astype(jnp.float32),
        lax.psum(grad_query_weight.astype(jnp.bfloat16), "cell").astype(jnp.float32),
        lax.psum(grad_query_bias.astype(jnp.bfloat16), "cell").astype(jnp.float32),
        lax.psum(grad_key_weight.astype(jnp.bfloat16), "cell").astype(jnp.float32),
        lax.psum(grad_value_weight.astype(jnp.bfloat16), "cell").astype(jnp.float32),
        lax.psum(grad_value_bias.astype(jnp.bfloat16), "cell").astype(jnp.float32),
        lax.psum(grad_output_weight.astype(jnp.bfloat16), "cell").astype(jnp.float32),
        lax.psum(grad_output_bias.astype(jnp.bfloat16), "cell").astype(jnp.float32),
        lax.psum(grad_second_gain.astype(jnp.bfloat16), "cell").astype(jnp.float32),
        lax.psum(grad_second_bias.astype(jnp.bfloat16), "cell").astype(jnp.float32),
        lax.psum(grad_up_weight.astype(jnp.bfloat16), "cell").astype(jnp.float32),
        lax.psum(grad_up_bias.astype(jnp.bfloat16), "cell").astype(jnp.float32),
        lax.psum(grad_down_weight.astype(jnp.bfloat16), "cell").astype(jnp.float32),
        lax.psum(grad_down_bias.astype(jnp.bfloat16), "cell").astype(jnp.float32),
    )
    return (
        result_out,
        input_grad,
        grad_first_gain,
        grad_first_bias,
        grad_query_weight,
        grad_query_bias,
        grad_key_weight,
        grad_value_weight,
        grad_value_bias,
        grad_output_weight,
        grad_output_bias,
        grad_second_gain,
        grad_second_bias,
        grad_up_weight,
        grad_up_bias,
        grad_down_weight,
        grad_down_bias,
    )


Q_BLOCK = 256


MESH = pl.DeviceIdType.MESH
ANY = pl.BlockSpec(memory_space=pl.ANY)
EDGE = 640
WIDE = 256
RING = 10


class Spot:
    def __init__(self):
        self.x = lax.axis_index("seq")
        self.cell = lax.axis_index("cell")
        self.core = lax.rem(self.cell, 2)
        self.y = lax.rem(self.cell // 2, 2)
        self.low = lax.rem(self.cell // 4, 2)
        self.high = lax.rem(self.cell // 8, 2)

    def flip(self, index, bit):
        return {"cell": self.cell + bit - 2 * bit * index}

    def over(self, name):
        if name == "x":
            return {"seq": 1 - self.x}
        if name == "core":
            return self.flip(self.core, 1)
        if name == "diagonal":
            return {"seq": 1 - self.x, **self.flip(self.core, 1)}
        return self.flip(*{"y": (self.y, 2), "low": (self.low, 4), "high": (self.high, 8)}[name])

    def meet(self, names):
        barrier = pltpu.get_barrier_semaphore()
        for name in names:
            pl.semaphore_signal(barrier, inc=1, device_id=self.over(name), device_id_type=MESH)
        pl.semaphore_wait(barrier, len(names))

    def send(self, name, source, target, send_sem, recv_sem):
        return pltpu.make_async_remote_copy(
            source, target, send_sem, recv_sem, device_id=self.over(name), device_id_type=MESH
        )


def rows_at(start, size):
    return pl.ds(pl.multiple_of(start, 16), size)


def cols(start, size):
    return pl.ds(pl.multiple_of(start, 128), size)


def attend_pair(qkv, mixed, total_ref, pair, base):
    f32, bf16 = jnp.float32, jnp.bfloat16
    rows = qkv.shape[0]
    lane = lax.broadcasted_iota(jnp.int32, (1, 128), 1)
    here = pair * 128
    keys = qkv[:, cols(EDGE + here, 128)]
    values_t = qkv[:, cols(2 * EDGE + here, 128)].T
    for block in range(rows // Q_BLOCK):
        part = pl.ds(block * Q_BLOCK, Q_BLOCK)
        queries = qkv[part, cols(here, 128)] * jnp.asarray(0.125, bf16)
        outs = []
        for head in range(2):
            own = (lane // HDIM) == head
            scores = lax.dot_general(
                keys,
                jnp.where(own, queries, jnp.zeros_like(queries)),
                (((1,), (1,)), ((), ())),
                preferred_element_type=f32,
            )
            largest = jnp.max(scores, axis=0, keepdims=True)
            weights = jnp.exp(scores - largest)
            total = jnp.sum(weights, axis=0, keepdims=True)
            out = jnp.dot(
                values_t[head * HDIM : (head + 1) * HDIM, :],
                weights.astype(bf16),
                preferred_element_type=f32,
            )
            outs.append(out / total)
            total_ref[2 * pair + head, :, part] = largest + jnp.log(total)
        mixed[part, cols(base + here, 128)] = jnp.concatenate(outs, axis=0).T.astype(bf16)


def attend_back_pair(qkv, totals, keys_acc, values_acc, pair):
    f32, bf16 = jnp.float32, jnp.bfloat16
    rows = qkv.shape[0]
    size = Q_BLOCK
    lane = lax.broadcasted_iota(jnp.int32, (1, 128), 1)
    here, key_lanes, value_lanes, grad_lanes = (cols(i * EDGE + pair * 128, 128) for i in range(4))
    keys = qkv[:, key_lanes]
    keys_t = keys.T
    nt = (((1,), (1,)), ((), ()))
    keys_acc[...] = jnp.zeros_like(keys_acc)
    values_acc[...] = jnp.zeros_like(values_acc)

    @pl.loop(0, rows // size)
    def _(block):
        part = rows_at(block * size, size)
        queries = qkv[part, here] * jnp.asarray(0.125, bf16)
        grads = qkv[part, grad_lanes]
        values = qkv[:, value_lanes]
        outs = []
        key_part = value_part = 0.0
        for head in range(2):
            own = (lane // HDIM) == head
            q_own = jnp.where(own, queries, jnp.zeros_like(queries))
            g_own = jnp.where(own, grads, jnp.zeros_like(grads))
            scores = lax.dot_general(keys, q_own, nt, preferred_element_type=f32)
            probs = jnp.exp(scores - totals[2 * pair + head, :, cols(block * size, size)])
            grad_probs = lax.dot_general(values, g_own, nt, preferred_element_type=f32)
            delta = jnp.sum(probs * grad_probs, axis=0, keepdims=True)
            grad_scores = (probs * (grad_probs - delta)).astype(bf16)
            value_part += jnp.dot(probs.astype(bf16), g_own, preferred_element_type=f32)
            key_part += jnp.dot(grad_scores, q_own, preferred_element_type=f32)
            outs.append(jnp.dot(keys_t[head * HDIM : (head + 1) * HDIM, :], grad_scores, preferred_element_type=f32))
        qkv[part, here] = (jnp.concatenate(outs, axis=0) * 0.125).T.astype(bf16)
        keys_acc[...] += key_part
        values_acc[...] += value_part

    qkv[:, key_lanes] = keys_acc[...].astype(bf16)
    qkv[:, value_lanes] = values_acc[...].astype(bf16)


def layer_kernel(
    tokens, out_grad, counts, wq, wk, wv, wo, wup, wdown, v0, v1, v2, v3, v4, v5, v6, v7, v8,
    result_ref, input_ref, down_ref, up_ref, out_ref, q_ref, k_ref, v_ref, vec_ref, normed_spill, qkv_spill, mixed_spill,
    pair, scale, vec, qkv_w, out_w, up_w, down_w, normed, wide, grad_up, ffn, mid, partial_sum, taken, given, tot,
    keys_acc, values_acc, blocks, from_x, from_y, from_low, from_high, res, sums,
    cell_weight, vectors, send_sems, recv_sems, local_sems, side_send, side_recv, side_local, out_sems,
    sum_send, sum_recv, store_sems, load_sems, swap_send, swap_recv, swap_local, vec_send, vec_recv, vec_store_sem,
):
    f32, bf16 = jnp.float32, jnp.bfloat16
    at = Spot()
    x, core = at.x, at.core
    rows, width = tokens.shape
    both = 2 * rows
    top, bottom = pl.ds(0, rows), pl.ds(rows, rows)
    grad, tok = pair.at[top], pair.at[bottom]
    nt = (((1,), (1,)), ((), ()))
    tn = (((0,), (0,)), ((), ()))
    sums[0] = jnp.zeros(sums.shape[1:], f32)
    for i, ref in enumerate((v0, v1, v2, v3, v4, v5, v6, v7)):
        vectors[i : i + 1, :] = ref[...].astype(f32).reshape(1, EDGE)
    for i in range(4):
        vectors[8 + i : 9 + i, :] = v8[i * EDGE : (i + 1) * EDGE].astype(f32).reshape(1, EDGE)
    vectors[12:16, :] = jnp.zeros((4, EDGE), f32)
    cell_weight[...] = jnp.sqrt(jnp.full(cell_weight.shape, counts[0], jnp.int32).astype(f32) / 1000.0)
    at.meet(("x", "core", "diagonal", "y", "low", "high"))

    side = [(tokens, tok), (cell_weight, scale), (out_grad, grad)]
    diagonal = [at.send("diagonal", s, t, side_send.at[i], side_recv.at[i]) for i, (s, t) in enumerate(side)]
    straight = [pltpu.make_async_copy(s, t, side_local.at[i]) for i, (s, t) in enumerate(side)]

    def swap(i, remote, local):
        @pl.when(x != core)
        def _():
            remote(diagonal[i])

        @pl.when(x == core)
        def _():
            local(straight[i])

    def swap_start(i):
        swap(i, lambda c: c.start(), lambda c: c.start())

    def swap_wait(i):
        swap(i, lambda c: c.wait(), lambda c: c.wait())

    chunks = []
    for start in range(0, 3 * EDGE, WIDE):
        width_now = min(WIDE, 3 * EDGE - start)
        parts = []
        for i, ref in enumerate((wq, wk, wv)):
            low, high = max(start, i * EDGE), min(start + width_now, (i + 1) * EDGE)
            if low < high:
                parts.append((ref.at[:, cols(core * EDGE + low - i * EDGE, high - low)], low))
        chunks.append((parts, qkv_w, EDGE, 0, start, width_now))
    for start in range(0, 4 * EDGE, WIDE):
        part = start // (2 * EDGE) * 2 * EDGE + start + core * 2 * EDGE
        chunks.append(([(wup.at[:, cols(part, WIDE)], start)], up_w, EDGE, 0, start, WIDE))
    for start in range(0, 2 * EDGE, WIDE):
        source = wdown.at[rows_at(core * 2 * EDGE, EDGE), pl.ds(start, WIDE)]
        chunks.append(([(source, start)], down_w, 2 * EDGE, 0, start, WIDE))
    count = len(chunks)
    eighth = EDGE // 8
    place = at.y * 4 + at.low * 2 + at.high

    def region(k, half, start, size, column=None, width=None):
        _, ref, stride, row, first, most = chunks[k]
        column, width = (first, most) if column is None else (column, width)
        return ref.at[rows_at(half * stride + row + start * eighth, size * eighth), pl.ds(column, width)]

    ops = {}
    for k, chunk in enumerate(chunks):
        ops["x", k] = [
            at.send(
                "x",
                source.at[rows_at(place * eighth, eighth)],
                region(k, x, place, 1, column, source.shape[1]),
                send_sems.at[4 * j, k],
                recv_sems.at[4 * j, k],
            )
            for j, (source, column) in enumerate(chunk[0])
        ]
        for s, (name, start, size) in enumerate(
            (("high", place, 1), ("low", at.y * 4 + at.low * 2, 2), ("y", at.y * 4, 4))
        ):
            part = region(k, 1 - x, start, size)
            ops[name, k] = [at.send(name, part, part, send_sems.at[s + 1, k], recv_sems.at[s + 1, k])]
    direct = []
    for i, start in enumerate(range(0, 2 * EDGE, WIDE)):
        source = wdown.at[rows_at(core * 2 * EDGE + EDGE, EDGE), pl.ds(start, WIDE)]
        target = down_w.at[rows_at(x * 2 * EDGE + EDGE, EDGE), pl.ds(start, WIDE)]
        direct.append(at.send("x", source, target, send_sems.at[5, i], recv_sems.at[5, i]))
    owns = []
    mine = rows_at(x * EDGE, EDGE)
    for i, ref in enumerate((wq, wk, wv)):
        owns.append((ref.at[:, cols(core * EDGE, EDGE)], qkv_w.at[mine, pl.ds(i * EDGE, EDGE)]))
    for i in range(2):
        owns.append((wup.at[:, cols((2 * i + core) * 2 * EDGE, 2 * EDGE)], up_w.at[mine, pl.ds(i * 2 * EDGE, 2 * EDGE)]))
    owns.append((wdown.at[rows_at(core * 2 * EDGE, 2 * EDGE)], down_w.at[rows_at(x * 2 * EDGE, 2 * EDGE)]))
    owns = [pltpu.make_async_copy(source, target, local_sems.at[i]) for i, (source, target) in enumerate(owns)]
    half = EDGE // 2
    out_x = at.send(
        "x", wo.at[rows_at(core * half, half)], out_w.at[rows_at(x * EDGE + core * half, half)], side_send.at[4], side_recv.at[4]
    )
    part = out_w.at[rows_at((1 - x) * EDGE + core * half, half)]
    out_core = at.send("core", part, part, side_send.at[5], side_recv.at[5])
    out_local = pltpu.make_async_copy(wo, out_w.at[rows_at(x * EDGE, EDGE)], side_local.at[4])
    vec_x = at.send("x", vectors, vec.at[x], side_send.at[3], side_recv.at[3])
    vec_local = pltpu.make_async_copy(vectors, vec.at[x], side_local.at[3])
    def core_copy(i, source, target):
        return at.send("core", source, target, side_send.at[i], side_recv.at[i])

    normed_one_core = core_copy(6, normed.at[top], normed.at[bottom])
    heads = cols(core * EDGE, EDGE)
    mixed_core = [
        core_copy(7, ffn.at[top, heads], ffn.at[bottom, heads]),
        core_copy(8, ffn.at[bottom, heads], ffn.at[top, heads]),
    ]
    normed_two_core = core_copy(9, normed.at[top], normed.at[bottom])
    ffn_core = core_copy(10, ffn.at[top], ffn.at[bottom])

    spills = {}

    def put(name, source, target):
        spills[name] = pltpu.make_async_copy(source, target, out_sems.at[len(spills)])
        spills[name].start()

    stages = ("x", "high", "low", "y")

    def fetch(name, k):
        for op in ops[name, k]:
            op.start()

    def bring(t):
        for s, name in enumerate(stages):
            k = t - s
            if 0 <= k < count:
                for op in ops[name, k]:
                    op.wait_recv()
                if s < 3:
                    fetch(stages[s + 1], k)
        for k in range(8 + 5 * t, min(count, 13 + 5 * t)):
            fetch("x", k)
        if t == 3:
            out_x.start()
        if t == 8:
            out_x.wait_recv()
            out_core.start()
        if t % 2 and 5 <= t < 5 + 2 * len(direct):
            direct[(t - 5) // 2].start()
        if t == 14:
            swap_start(2)
        if t in (1, 2, 4):
            for op in {1: (out_local,), 2: owns[3:5], 4: owns[5:]}[t]:
                op.start()

    for k in range(8):
        fetch("x", k)
    vec_x.start()
    swap_start(0)
    swap_start(1)
    vec_local.start()
    for op in owns[:3]:
        op.start()
    bring(0)
    bring(1)
    vec_x.wait_recv()
    vec_local.wait()

    def vector(i):
        return jnp.concatenate([vec[0, i : i + 1, :], vec[1, i : i + 1, :]], axis=1)

    def norm(values, gain, bias):
        average = jnp.mean(values, axis=-1, keepdims=True)
        centred = values - average
        inverse = lax.rsqrt(jnp.mean(centred * centred, axis=-1, keepdims=True) + 1e-05)
        return (centred * inverse * gain + bias).astype(bf16)

    swap_wait(0)
    gain_one, bias_one = vector(0), vector(1)

    @pl.loop(0, rows // 64)
    def _(i):
        here = rows_at(i * 64, 64)
        normed[here, :] = norm(tok[here, :].astype(f32), gain_one, bias_one)

    normed_one_core.start()
    bring(2)
    bring(3)
    normed_one_core.wait_recv()
    put("normed_one", normed, normed_spill)

    for i in range(3):
        for t in ((4, 5), (6, 7), (8, 9, 10))[i]:
            bring(t)
        owns[i].wait()
        lanes = pl.ds(i * EDGE, EDGE)
        bias = 0.0 if i == 1 else vec[core, 2 + i // 2 : 3 + i // 2, :]

        @pl.loop(0, 2 * rows // 256)
        def _(r):
            here = rows_at(r * 256, 256)
            value = jnp.dot(normed[here, :], qkv_w[:, lanes], preferred_element_type=f32)
            wide[here, lanes] = (value + bias).astype(bf16)

    put("qkv", wide.at[:, pl.ds(0, 3 * EDGE)], qkv_spill)

    @pl.loop(0, EDGE // 128)
    def _(two):
        attend_pair(wide, ffn, tot, two, core * EDGE)

        for i in range(5):

            @pl.when(two == i)
            def _():
                bring(11 + i)

    spills["normed_one"].wait()
    normed_one_core.wait_send()
    mixed_core[0].start()
    mixed_core[1].start()
    bring(16)
    out_local.wait()
    out_core.wait_recv()
    mixed_core[1].wait_recv()
    mixed_core[0].wait_recv()
    put("mixed", ffn, mixed_spill)
    gain_two, bias_two, out_bias = vector(5), vector(6), vector(4)

    @pl.loop(0, rows // 128)
    def _(r):
        here = rows_at(r * 128, 128)
        value = jnp.dot(ffn[here, :], out_w[...], preferred_element_type=f32)
        value = tok[here, :].astype(f32) + value + out_bias
        mid[here, :] = value
        normed[here, :] = norm(value, gain_two, bias_two)

    spills["mixed"].wait()
    spills["qkv"].wait()
    for op in mixed_core:
        op.wait_send()
    normed_two_core.start()
    bring(17)
    normed_two_core.wait_recv()
    up_bias = jnp.concatenate([vec[h, pl.ds(8 + core * 2 + i, 1), :] for h in range(2) for i in range(2)], axis=1)
    for i in range(4):
        if i % 2 == 0:
            owns[3 + i // 2].wait()
        lanes = pl.ds(i * EDGE, EDGE)
        bias = up_bias[:, i * EDGE : (i + 1) * EDGE]

        @pl.loop(0, both // 128)
        def _(r):
            here = rows_at(r * 128, 128)
            up = jnp.dot(normed[here, :], up_w[:, lanes], preferred_element_type=f32) + bias
            cdf = 0.5 * (1.0 + lax.erf(up * 0.7071067811865476))
            wide[here, lanes] = (up * cdf).astype(bf16)
            grad_up[here, lanes] = (cdf + up * jnp.exp(-0.5 * up * up) * 0.3989422804014327).astype(bf16)

        if i == 0:
            swap_wait(1)
            swap_wait(2)
            weight = scale[0:1, 0:1]

            @pl.loop(0, rows // 64)
            def _(r):
                here = rows_at(r * 64, 64)
                ffn[here, :] = (grad[here, :].astype(f32) * weight).astype(bf16)

            ffn_core.start()
        for t in ((18,), (19, 20), (21,), (22,))[i]:
            bring(t)
    ffn_core.wait_recv()

    pieces = []
    for i in range(2):
        for start in range(0, 2 * EDGE, WIDE):
            target = down_ref.at[rows_at(core * 2 * EDGE + i * EDGE, EDGE), pl.ds(start, WIDE)]
            pieces.append([(wide, 2 * EDGE, i * EDGE, ffn, start, WIDE, target)])
    for start in range(0, 4 * EDGE, WIDE):
        target = up_ref.at[:, cols(start // (2 * EDGE) * 2 * EDGE + start + core * 2 * EDGE, WIDE)]
        pieces.append([(normed, EDGE, 0, grad_up, start, WIDE, target)])
    mixed_rows = pl.ds(EDGE, both)

    def out_part(start, width):
        target = out_ref.at[:, cols(core * EDGE + start, width)]
        return (down_w.at[mixed_rows], EDGE, 0, ffn, core * EDGE + start, width, target)

    last = EDGE % WIDE
    pieces += [[out_part(start, WIDE)] for start in range(0, EDGE - last, WIDE)]
    for start in range(0, 3 * EDGE, WIDE):
        parts = []
        for i, ref in enumerate((q_ref, k_ref, v_ref)):
            first, end = max(start, i * EDGE), min(start + WIDE, (i + 1) * EDGE)
            if first < end:
                target = ref.at[:, cols(core * EDGE + first - i * EDGE, end - first)]
                parts.append((normed, EDGE, 0, wide, first, end - first, target))
        pieces.append(parts)
    pieces[-1].append(out_part(EDGE - last, last))
    total_count = len(pieces)

    half, quarter, eighth = EDGE // 2, EDGE // 4, EDGE // 8
    y0 = at.y * half
    l0 = y0 + at.low * quarter
    h0 = l0 + at.high * eighth
    sum_ops = {}
    for k, parts in enumerate(pieces):
        acc, four, slot, sem = k % 6, k % 4, k % 7, k % RING
        hops = (
            ("x", "x", blocks.at[6 + k % 3], from_x.at[four]),
            ("y", "y", blocks.at[acc, rows_at((1 - at.y) * half, half)], from_y.at[four]),
            ("low", "low", blocks.at[acc, rows_at(y0 + (1 - at.low) * quarter, quarter)], from_low.at[four]),
            ("high", "high", blocks.at[acc, rows_at(l0 + (1 - at.high) * eighth, eighth)], from_high.at[four]),
            ("all_high", "high", res.at[slot, rows_at(h0, eighth)], res.at[slot, rows_at(h0, eighth)]),
            ("all_low", "low", res.at[slot, rows_at(l0, quarter)], res.at[slot, rows_at(l0, quarter)]),
            ("all_y", "y", res.at[slot, rows_at(y0, half)], res.at[slot, rows_at(y0, half)]),
        )
        for s, (stage, name, source, goal) in enumerate(hops):
            sum_ops[stage, k] = [at.send(name, source, goal, sum_send.at[s, sem], sum_recv.at[s, sem])]
        sum_ops["core", k] = []
        sum_ops["store", k] = []
        start = 0
        for s, part in enumerate(parts):
            source = res.at[slot, :, pl.ds(start, part[5])]
            sum_ops["core", k].append(at.send("core", source, part[6], sum_send.at[7 + s, sem], sum_recv.at[7 + s, sem]))
            sum_ops["store", k].append(pltpu.make_async_copy(source, part[6], store_sems.at[s, sem]))
            start += part[5]

    def begin(stage, k):
        for op in sum_ops[stage, k]:
            op.start()

    def came(stage, k):
        for op in sum_ops[stage, k]:
            op.wait_recv()

    def left_here(stage, k):
        for op in sum_ops[stage, k]:
            op.wait_send()

    def make(k):
        @pl.loop(0, 2)
        def _(j):
            of = j * x + (1 - j) * (1 - x)
            slot = j * (k % 6) + (1 - j) * (6 + k % 3)
            start = 0
            for left, stride, left_at, right, right_at, width_now, _ in pieces[k]:
                lanes = right_at if isinstance(right_at, int) else pl.multiple_of(right_at, 128)
                product = lax.dot_general(
                    left[:, cols(of * stride + left_at, EDGE)],
                    right[:, pl.ds(lanes, width_now)],
                    tn,
                    preferred_element_type=f32,
                )
                blocks[slot, :, start : start + width_now] = product.astype(bf16)
                start += width_now

        begin("x", k)

    def add(k, start, size, other, goal, goal_slot):
        @pl.loop(0, size // 80)
        def _(i):
            here = rows_at(start + i * 80, 80)
            there = rows_at(i * 80, 80)
            total = blocks[k % 6, here, :].astype(f32) + other[there, :].astype(f32)
            goal[goal_slot, here, :] = total.astype(bf16)

    def tick(t):
        k = t
        if 0 <= k < total_count:
            came("x", k)
            add(k, 0, EDGE, from_x.at[k % 4], blocks, k % 6)
            begin("y", k)
            if k >= 1:
                left_here("x", k - 1)
            if k + 2 < total_count:
                make(k + 2)
        k = t - 1
        if 0 <= k < total_count:
            came("y", k)
            add(k, y0, half, from_y.at[k % 4], blocks, k % 6)
            begin("low", k)
        k = t - 2
        if 0 <= k < total_count:
            came("low", k)
            add(k, l0, quarter, from_low.at[k % 4], blocks, k % 6)
            begin("high", k)
        k = t - 3
        if 0 <= k < total_count:
            came("high", k)
            add(k, h0, eighth, from_high.at[k % 4], res, k % 7)
            begin("all_high", k)
            for stage in ("y", "low", "high"):
                left_here(stage, k)
        for before, stage, after in ((4, "all_high", "all_low"), (5, "all_low", "all_y"), (6, "all_y", "core")):
            k = t - before
            if 0 <= k < total_count:
                came(stage, k)
                begin(after, k)
                if after == "core":
                    begin("store", k)
        k = t - 7
        if 0 <= k < total_count:
            came("core", k)
            for stage in ("all_high", "all_low", "all_y", "core"):
                left_here(stage, k)
            for op in sum_ops["store", k]:
                op.wait()

    two_copy = core_copy(11, given.at[0], taken.at[0])
    result_copy = core_copy(12, given.at[1], taken.at[1])
    attn_copy = core_copy(13, ffn.at[top], ffn.at[bottom])
    one_copy = core_copy(14, given.at[0], taken.at[0])
    swaps = []
    for i, target in enumerate((result_ref, input_ref)):
        source = taken.at[1 - i]
        swaps.append(
            (
                at.send("diagonal", source, target, swap_send.at[i], swap_recv.at[i]),
                pltpu.make_async_copy(source, target, swap_local.at[i]),
            )
        )

    def swap_back(i, act):
        @pl.when(x != core)
        def _():
            act(swaps[i][0])

        @pl.when(x == core)
        def _():
            act(swaps[i][1])

    def add_vector(i, value):
        total = jnp.sum(value, axis=0, keepdims=True)
        sums[0, 2 * i : 2 * i + 1, :] += total[:, :EDGE]
        sums[0, 2 * i + 1 : 2 * i + 2, :] += total[:, EDGE:]

    def norm_back(values, grad_normed, gain):
        average = jnp.mean(values, axis=-1, keepdims=True)
        centred = values - average
        inverse = lax.rsqrt(jnp.mean(centred * centred, axis=-1, keepdims=True) + 1e-05)
        standard = centred * inverse
        scaled = grad_normed * gain
        back = inverse * (
            scaled
            - jnp.mean(scaled, axis=-1, keepdims=True)
            - standard * jnp.mean(scaled * standard, axis=-1, keepdims=True)
        )
        return standard, back

    make(0)
    make(1)
    for t in (23, 24, 25):
        bring(t)
    owns[5].wait()
    for op in direct:
        op.wait()
    normed_two_core.wait_send()
    loads = {}

    def load(name, source, target):
        loads[name] = pltpu.make_async_copy(source, target, load_sems.at[len(loads)])
        loads[name].start()

    for i in range(4):
        lanes = pl.ds(i * EDGE, EDGE)
        row = pl.ds(16 + 2 * (core * 2 + i % 2) + i // 2, 1)

        @pl.loop(0, both // 256)
        def _(r):
            here = rows_at(r * 256, 256)
            value = lax.dot_general(ffn[here, :], down_w[lanes, :], nt, preferred_element_type=f32)
            value = (value * grad_up[here, lanes].astype(f32)).astype(bf16)
            grad_up[here, lanes] = value
            sums[0, row, :] += jnp.sum(value.astype(f32), axis=0, keepdims=True)

        tick(i)

    @pl.loop(0, rows // 256)
    def _(r):
        value = lax.dot_general(grad_up[rows_at(rows + r * 256, 256), :], up_w[...], nt, preferred_element_type=f32)
        given[0, rows_at(r * 256, 256), :] = value.astype(bf16)

    two_copy.start()
    tick(4)

    @pl.loop(0, rows // 256)
    def _(r):
        value = lax.dot_general(grad_up[rows_at(r * 256, 256), :], up_w[...], nt, preferred_element_type=f32)
        partial_sum[rows_at(r * 256, 256), :] = value

    tick(5)

    @pl.loop(0, rows // 256)
    def _(r):
        value = jnp.dot(wide[rows_at(rows + r * 256, 256), :], down_w[...], preferred_element_type=f32)
        given[1, rows_at(r * 256, 256), :] = value.astype(bf16)

    tick(6)
    tick(7)
    result_copy.start()
    two_copy.wait_recv()
    result_copy.wait_recv()
    down_bias = vector(7)

    @pl.loop(0, rows // 128)
    def _(r):
        here = rows_at(r * 128, 128)
        value = jnp.dot(wide[here, :], down_w[...], preferred_element_type=f32)
        value = mid[here, :] + value + taken[1, here, :].astype(f32) + down_bias
        taken[1, here, :] = value.astype(bf16)

    swap_back(0, lambda copy: copy.start())
    for k in range(count):
        for name in stages:
            for op in ops[name, k]:
                op.wait_send()
    for op in (ffn_core, out_x, out_core, vec_x):
        op.wait_send()
    load("qkv", qkv_spill, wide.at[:, pl.ds(0, 3 * EDGE)])
    load("mixed", mixed_spill, down_w.at[mixed_rows])
    weight = scale[0:1, 0:1]
    tick(8)

    @pl.loop(0, rows // 32)
    def _(r):
        here = rows_at(r * 32, 32)
        add_vector(7, ffn[here, :].astype(f32))
        grad_normed = partial_sum[here, :] + taken[0, here, :].astype(f32)
        standard, back = norm_back(mid[here, :], grad_normed, gain_two)
        add_vector(5, grad_normed * standard)
        add_vector(6, grad_normed)
        value = pair[here, :].astype(f32) * weight + back
        mid[here, :] = value
        value = value.astype(bf16)
        ffn[here, :] = value
        add_vector(4, value.astype(f32))

    attn_copy.start()
    two_copy.wait_send()
    tick(9)
    attn_copy.wait_recv()

    @pl.loop(0, both // 256)
    def _(r):
        here = rows_at(r * 256, 256)
        value = lax.dot_general(ffn[here, :], out_w[rows_at(core * EDGE, EDGE), :], nt, preferred_element_type=f32)
        wide[here, pl.ds(3 * EDGE, EDGE)] = value.astype(bf16)

    loads["qkv"].wait()
    tick(10)

    @pl.loop(0, EDGE // 128)
    def _(two):
        attend_back_pair(wide, tot, keys_acc, values_acc, two)
        for i in range(5):

            @pl.when(two == i)
            def _():
                tick(11 + i)

    weights = pl.ds(0, 3 * EDGE)

    @pl.loop(0, rows // 256)
    def _(r):
        value = lax.dot_general(
            wide[rows_at(rows + r * 256, 256), weights], qkv_w[...], nt, preferred_element_type=f32
        )
        given[0, rows_at(r * 256, 256), :] = value.astype(bf16)

    one_copy.start()
    tick(16)
    tick(17)
    load("normed_one", normed_spill, normed)
    loads["mixed"].wait()

    @pl.loop(0, rows // 256)
    def _(r):
        value = lax.dot_general(wide[rows_at(r * 256, 256), weights], qkv_w[...], nt, preferred_element_type=f32)
        partial_sum[rows_at(r * 256, 256), :] = value

    tick(18)
    one_copy.wait_recv()

    @pl.loop(0, rows // 32)
    def _(r):
        here = rows_at(r * 32, 32)
        tok = pair[rows_at(rows + r * 32, 32), :].astype(f32)
        grad_normed = partial_sum[here, :] + taken[0, here, :].astype(f32)
        standard, back = norm_back(tok, grad_normed, gain_one)
        add_vector(0, grad_normed * standard)
        add_vector(1, grad_normed)
        taken[0, here, :] = (mid[here, :] + back).astype(bf16)

    swap_back(1, lambda copy: copy.start())
    tick(19)
    loads["normed_one"].wait()

    @pl.loop(0, both // 128)
    def _(r):
        here = rows_at(r * 128, 128)
        for i in (0, 2):
            row = pl.ds(4 + i + core, 1)
            value = wide[here, pl.ds(i * EDGE, EDGE)].astype(f32)
            sums[0, row, :] += jnp.sum(value, axis=0, keepdims=True)

    names = ("x", "core", "y", "low", "high")
    vec_ops = [at.send(name, sums.at[i], sums.at[6 + i], vec_send.at[i], vec_recv.at[i]) for i, name in enumerate(names)]
    vec_ops[0].start()
    for t in range(20, total_count + 7):
        tick(t)
        if t < 25:
            i = t - 20
            vec_ops[i].wait_recv()
            sums[i + 1] = sums[i] + sums[6 + i]
            if i < 4:
                vec_ops[i + 1].start()
    vec_store = pltpu.make_async_copy(sums.at[5], vec_ref, vec_store_sem.at[0])
    vec_store.start()
    vec_store.wait()
    for op in (result_copy, attn_copy, one_copy, *vec_ops):
        op.wait_send()
    swap_back(0, lambda copy: copy.wait())
    swap_back(1, lambda copy: copy.wait())
    left_here("x", total_count - 1)


def layer(*args):
    bf16, f32 = jnp.bfloat16, jnp.float32
    rows, width = args[0].shape
    both = 2 * rows
    outs = [
        ((rows, width), bf16),
        ((rows, width), bf16),
        ((4 * EDGE, width), bf16),
        ((EDGE, 8 * EDGE), bf16),
        ((EDGE, width), bf16),
        ((EDGE, width), bf16),
        ((EDGE, width), bf16),
        ((EDGE, width), bf16),
        ((24, EDGE), f32),
        ((both, width), bf16),
        ((both, 3 * EDGE), bf16),
        ((both, width), bf16),
    ]
    scratch = [
        ((both, width), bf16),
        ((8, 128), f32),
        ((2, 16, EDGE), f32),
        ((width, 3 * EDGE), bf16),
        ((width, width), bf16),
        ((width, 4 * EDGE), bf16),
        ((4 * EDGE, width), bf16),
        ((both, width), bf16),
        ((both, 4 * EDGE), bf16),
        ((both, 4 * EDGE), bf16),
        ((both, width), bf16),
        ((rows, width), f32),
        ((rows, width), f32),
        ((2, rows, width), bf16),
        ((2, rows, width), bf16),
        ((EDGE // HDIM, 1, both), f32),
        ((both, 128), f32),
        ((both, 128), f32),
        ((9, EDGE, WIDE), bf16),
        ((4, EDGE, WIDE), bf16),
        ((4, EDGE // 2, WIDE), bf16),
        ((4, EDGE // 4, WIDE), bf16),
        ((4, EDGE // 8, WIDE), bf16),
        ((7, EDGE, WIDE), bf16),
        ((11, 24, EDGE), f32),
        ((8, 128), f32),
        ((16, EDGE), f32),
    ]
    dma = pltpu.SemaphoreType.DMA
    sizes = [(6, 23), (6, 23), (6,), (15,), (15,), (5,), (3,), (9, RING), (9, RING), (2, RING), (3,)]
    sizes += [(2,), (2,), (2,), (5,), (5,), (1,)]
    return pl.pallas_call(
        layer_kernel,
        in_specs=[ANY] * 2 + [pl.BlockSpec(memory_space=pltpu.SMEM)] + [ANY] * 6 + [pl.BlockSpec(memory_space=pltpu.VMEM)] * 9,
        out_specs=[ANY] * len(outs),
        out_shape=[jax.ShapeDtypeStruct(*out) for out in outs],
        scratch_shapes=[pltpu.VMEM(*array) for array in scratch] + [dma(size) for size in sizes],
        compiler_params=pltpu.CompilerParams(
            collective_id=0, has_side_effects=True, vmem_limit_bytes=64 * 1024 * 1024
        ),
        name="layer",
    )(*args)


def widen_kernel(*refs):
    half = len(refs) // 2
    for source, target in zip(refs[:half], refs[half:]):
        target[...] = source[...].astype(target.dtype)


def widen(*arrays):
    steps = 4
    specs = [pl.BlockSpec((a.shape[0] // steps, a.shape[1]), lambda i: (i, 0)) for a in arrays]
    types = [jnp.float32] * (len(arrays) - 2) + [jnp.bfloat16] * 2
    return pl.pallas_call(
        widen_kernel,
        grid=(steps,),
        in_specs=specs,
        out_specs=specs,
        out_shape=[jax.ShapeDtypeStruct(a.shape, kind) for a, kind in zip(arrays, types)],
        compiler_params=pltpu.CompilerParams(vmem_limit_bytes=64 * 1024 * 1024),
        name="widen",
    )(*arrays)


def tuned(
    tokens,
    out_grad,
    query_counts,
    first_gain,
    first_bias,
    query_weight,
    query_bias,
    key_weight,
    value_weight,
    value_bias,
    output_weight,
    output_bias,
    second_gain,
    second_bias,
    up_weight,
    up_bias,
    down_weight,
    down_bias,
):
    f32, bf16 = jnp.float32, jnp.bfloat16
    x = lax.axis_index("seq")
    head_width = tokens.shape[2] // 2

    result, input_grad, down, up, out, query, key, value, sums, *_ = layer(
        tokens[0],
        out_grad[0],
        query_counts,
        query_weight,
        key_weight,
        value_weight,
        output_weight,
        up_weight,
        down_weight,
        first_gain,
        first_bias,
        query_bias,
        value_bias,
        output_bias,
        second_gain,
        second_bias,
        down_bias,
        up_bias,
    )
    out, query, key, value, up, down, result, input_grad = widen(out, query, key, value, up, down, result, input_grad)
    sums = lax.dynamic_index_in_dim(sums.reshape(12, 2, head_width), x, 1, keepdims=False)
    up_sum = sums[8:].reshape(-1)
    return (
        result[None],
        input_grad[None],
        sums[0],
        sums[1],
        query,
        sums[2],
        key,
        value,
        sums[3],
        out,
        sums[4],
        sums[5],
        sums[6],
        up,
        up_sum,
        down,
        sums[7],
    )


def chosen(mesh):
    cells, blocks = mesh.shape["cell"], mesh.shape["seq"]

    def per_device(tokens, *rest):
        if blocks == 2 and cells == 16 and tokens.shape == (1, 512, 1280):
            return tuned(tokens, *rest)
        return general(tokens, *rest)

    return per_device


def solution(mesh):
    placed = (
        P("cell", "seq", None),
        P("cell", "seq", None),
        P("cell"),
        P("seq"),
        P("seq"),
        P("seq", None),
        P("seq"),
        P("seq", None),
        P("seq", None),
        P("seq"),
        P("seq", None),
        P("seq"),
        P("seq"),
        P("seq"),
        P("seq", None),
        P("seq"),
        P("seq", None),
        P("seq"),
    )
    return jax.shard_map(
        chosen(mesh),
        mesh=mesh,
        in_specs=placed,
        out_specs=(
            P("cell", "seq", None),
            P("cell", "seq", None),
            P("seq"),
            P("seq"),
            P("seq", None),
            P("seq"),
            P("seq", None),
            P("seq", None),
            P("seq"),
            P("seq", None),
            P("seq"),
            P("seq"),
            P("seq"),
            P("seq", None),
            P("seq"),
            P("seq", None),
            P("seq"),
        ),
        check_vma=False,
    )
```
